32 devices in a mesh: groups: 2 (over y), dom: 4 (over z), sub: 2 (over x), chip: 2 (over core).
Axes of the slice: x: 2, y: 2, z: 4, core: 2. Of those that a mesh axis runs over, the one named last changes fastest.
Arguments:
- fine_nodes: bfloat16 [65536, 128], P(('groups', 'dom', 'sub', 'chip')), parts along dimension 0, may hold values from -6 to 6
- fine_src: int32 [512, 768], P(('groups', 'dom', 'sub', 'chip')), parts along dimension 0, may hold values from 0 to 3071, as said below
- fine_dst: int32 [512, 768], P(('groups', 'dom', 'sub', 'chip')), parts along dimension 0, may hold values from -1 to 127
- halo_send: int32 [32, 4, 256], P(('groups', 'dom', 'sub', 'chip')), parts along dimension 0, may hold values from 0 to 2048, as said below
- pool_send: int32 [32, 4, 64], P(('groups', 'dom', 'sub', 'chip')), parts along dimension 0, may hold values from 0 to 2048, as said below
- coarse_src: int32 [64, 768], P(('groups', 'dom', 'sub', 'chip')), parts along dimension 0, may hold values from 0 to 767, as said below
- coarse_dst: int32 [64, 768], P(('groups', 'dom', 'sub', 'chip')), parts along dimension 0, may hold values from -1 to 127, as said below
- coarse_send: int32 [32, 4, 128], P(('groups', 'dom', 'sub', 'chip')), parts along dimension 0, may hold values from 0 to 256, as said below
- prolong_idx: int32 [65536], P(('groups', 'dom', 'sub', 'chip')), parts along dimension 0, may hold values from 0 to 63, as said below
- fine_weights: bfloat16 [2, 4, 128, 128], replicated, may hold values from -0.5 to 0.5
- coarse_weights: bfloat16 [4, 128, 128], replicated, may hold values from -0.5 to 0.5
- prolong_weight: bfloat16 [128, 128], replicated, may hold values from -0.5 to 0.5
Outputs:
- fine_out: bfloat16 [65536, 128], P(('groups', 'dom', 'sub', 'chip')), parts along dimension 0
The draws below stay inside these ranges and needn't reach their ends.
There are 2 independent parts, one for each index of `groups`. The reference program is written for one: setup_inputs(seed, part) draws one part's arguments, and reference() takes and returns one part's arrays. A program takes and returns all parts, laid end to end along the dimension named above; an argument that names none is the same for every part. Nothing has to cross between parts.
Inputs may be any that keep to these rules, and one draw needn't show every extreme that they name: `halo_send`: rows of a device (d, q) go only to partitions d + 1, d - 1 and d + 2 (cyclic over 4); each list names at most 256 live rows in front, the rest is 2048; some receiver gets 256 live rows from each of its three senders. `fine_src`: in block b the first 576 slots name own rows from s to s + w - 1, with w = min(384, 2048) and s = min(max(128 * b - 128, 0), 2048 - w); the other slots name live halo rows. `pool_send`: only devices whose q is a multiple of 4 are coarse owners; live rows stand in front, at most 64 to one owner, distinct rows of a device; in partition 0 the first owner is full from every source. `coarse_src`: only owners have coarse edges and send lists; senders name live coarse slots or live coarse halo rows. `coarse_dst`: empty slots hold -1; all slots of non-owners are empty. `coarse_send`: same partner pattern as the fine lists among owners, live coarse slots in front, at most 128; the rest is 256. `prolong_idx`: each entry names a row that the device sent to an owner.
All inputs are finite; a program needn't handle non-finite values.
Results may differ from the reference program's by a relative error of at most 0.0075.
Values may be sent and summed in bfloat16 or wider, within the bound.
No kernel may reach another device: no remote copies, remote signals or barrier semaphores. Data moves between devices by JAX's collectives and lax.ppermute only.
A program may use at most 64 MiB of HBM per device.

```python
import jax
import jax.numpy as jnp
from jax import lax

LATENT = 128
NODE_DEV = 2048
EDGE_BLK = 768
HALO_CAP = 256
POOL_CAP = 64
CHALO_CAP = 128
PEERS = 4
DEVS = 16
NODES = 32768
COARSE_DEV = 256
FINE_BLOCKS = 16
COARSE_BLOCKS = 2
N_DOM = 4


OFFSETS = (1, -1, 2)


def device_grid():
    device_ids = jnp.arange(DEVS, dtype=jnp.int32)
    return (device_ids, device_ids // PEERS, device_ids % PEERS)


def neighbour_counts(key, salt, capacity):
    key = jax.random.fold_in(key, salt)
    counts = jax.random.randint(key, (DEVS, 3), capacity // 4, capacity + 1, dtype=jnp.int32)
    counts = counts.at[(N_DOM - 1) * PEERS, 0].set(capacity)
    counts = counts.at[PEERS, 1].set(capacity)
    counts = counts.at[(N_DOM - 2) * PEERS, 2].set(capacity)
    return counts


def pool_counts(key):
    key = jax.random.fold_in(key, 202)
    counts = jax.random.randint(key, (DEVS, PEERS // 4), POOL_CAP // 4, POOL_CAP + 1, dtype=jnp.int32)
    device_ids, dom_ids, place_ids = device_grid()
    first_owner = jnp.arange(PEERS // 4, dtype=jnp.int32)[None, :] == 0
    return jnp.where((dom_ids[:, None] == 0) & first_owner, POOL_CAP, counts)


def offset_value(choice_ids):
    return jnp.where(choice_ids == 0, 1, jnp.where(choice_ids == 1, -1, 2))


def live_coarse_slot(key, shape, dom_ids, place_ids, pooled):
    key_place, key_rest = jax.random.split(key)
    source_place = jax.random.randint(key_place, shape, 0, PEERS, dtype=jnp.int32)
    spread = jax.random.randint(key_rest, shape, 0, 2 ** 20, dtype=jnp.int32)
    live = pooled[dom_ids * PEERS + source_place, place_ids // 4]
    return source_place * POOL_CAP + spread % live


def send_lists(key, counts, capacity, fill_value, values):
    device_ids, dom_ids, place_ids = device_grid()
    slots = jnp.arange(N_DOM, dtype=jnp.int32)[None, :, None]
    places = jnp.arange(capacity, dtype=jnp.int32)[None, None, :]
    result = jnp.full((DEVS, N_DOM, capacity), fill_value, jnp.int32)
    for index, offset in enumerate(OFFSETS):
        hit = (slots == ((dom_ids + offset) % N_DOM)[:, None, None]) & (places < counts[:, index][:, None, None])
        result = jnp.where(hit, values, result)
    return result


def halo_reference(key, counts, dom_ids, place_ids, shape, base, capacity):
    key_choice, key_rest = jax.random.split(key)
    choice_ids = jax.random.randint(key_choice, shape, 0, 3, dtype=jnp.int32)
    spread = jax.random.randint(key_rest, shape, 0, 2 ** 20, dtype=jnp.int32)
    source_dom = (dom_ids - offset_value(choice_ids)) % N_DOM
    live = counts[source_dom * PEERS + place_ids, choice_ids]
    return base + source_dom * capacity + spread % live


def draw_halo_send(key, part):
    counts = neighbour_counts(key, 101, HALO_CAP)
    key = jax.random.fold_in(key, 1)
    values = jax.random.randint(key, (DEVS, N_DOM, HALO_CAP), 0, NODE_DEV, dtype=jnp.int32)
    return send_lists(key, counts, HALO_CAP, NODE_DEV, values)


def draw_fine_src(key, part):
    counts = neighbour_counts(key, 101, HALO_CAP)
    key = jax.random.fold_in(key, 2)
    key_local, key_halo = jax.random.split(key)
    local_count = EDGE_BLK * 3 // 4
    window = min(384, NODE_DEV)
    block_ids = jnp.arange(FINE_BLOCKS, dtype=jnp.int32)
    starts = jnp.clip(block_ids * 128 - 128, 0, NODE_DEV - window)
    local_rows = starts[None, :, None] + jax.random.randint(key_local, (DEVS, FINE_BLOCKS, local_count), 0, window, dtype=jnp.int32)
    device_ids, dom_ids, place_ids = device_grid()
    halo_shape = (DEVS, FINE_BLOCKS, EDGE_BLK - local_count)
    halo_rows = halo_reference(key_halo, counts, dom_ids[:, None, None], place_ids[:, None, None], halo_shape, NODE_DEV, HALO_CAP)
    return jnp.concatenate([local_rows, halo_rows], axis=2).reshape(DEVS * FINE_BLOCKS, EDGE_BLK)


def draw_fine_dst(key, part):
    key = jax.random.fold_in(key, 3)
    key_rows, key_empty = jax.random.split(key)
    shape = (DEVS * FINE_BLOCKS, EDGE_BLK)
    targets = jax.random.randint(key_rows, shape, 0, 128, dtype=jnp.int32)
    empty = jax.random.randint(key_empty, shape, 0, 4, dtype=jnp.int32) == 0
    return jnp.where(empty, -1, targets)


def draw_pool_send(key, part):
    pooled = pool_counts(key)
    key = jax.random.fold_in(key, 4)
    orders = jax.vmap(lambda one_key: jax.random.permutation(one_key, NODE_DEV))(jax.random.split(key, DEVS))
    owners = PEERS // 4
    rows = orders[:, :owners * POOL_CAP].reshape(DEVS, owners, POOL_CAP).astype(jnp.int32)
    places = jnp.arange(POOL_CAP, dtype=jnp.int32)[None, None, :]
    live_rows = jnp.where(places < pooled[:, :, None], rows, NODE_DEV)
    result = jnp.full((DEVS, PEERS, POOL_CAP), NODE_DEV, jnp.int32)
    return result.at[:, ::4, :].set(live_rows)


def draw_coarse_send(key, part):
    pooled = pool_counts(key)
    counts = neighbour_counts(key, 303, CHALO_CAP)
    key = jax.random.fold_in(key, 5)
    device_ids, dom_ids, place_ids = device_grid()
    shape = (DEVS, N_DOM, CHALO_CAP)
    values = live_coarse_slot(key, shape, dom_ids[:, None, None], place_ids[:, None, None], pooled)
    result = send_lists(key, counts, CHALO_CAP, COARSE_DEV, values)
    owner = (place_ids % 4 == 0)[:, None, None]
    return jnp.where(owner, result, COARSE_DEV)


def draw_coarse_src(key, part):
    pooled = pool_counts(key)
    counts = neighbour_counts(key, 303, CHALO_CAP)
    key = jax.random.fold_in(key, 6)
    key_local, key_halo, key_pick = jax.random.split(key, 3)
    shape = (DEVS, COARSE_BLOCKS * EDGE_BLK)
    device_ids, dom_ids, place_ids = device_grid()
    local_rows = live_coarse_slot(key_local, shape, dom_ids[:, None], place_ids[:, None], pooled)
    halo_rows = halo_reference(key_halo, counts, dom_ids[:, None], place_ids[:, None], shape, COARSE_DEV, CHALO_CAP)
    use_halo = jax.random.randint(key_pick, shape, 0, 4, dtype=jnp.int32) == 0
    result = jnp.where(use_halo, halo_rows, local_rows)
    result = jnp.where((place_ids % 4 == 0)[:, None], result, 0)
    return result.reshape(DEVS * COARSE_BLOCKS, EDGE_BLK)


def draw_coarse_dst(key, part):
    key = jax.random.fold_in(key, 7)
    key_rows, key_empty = jax.random.split(key)
    shape = (DEVS, COARSE_BLOCKS * EDGE_BLK)
    device_ids, dom_ids, place_ids = device_grid()
    targets = jax.random.randint(key_rows, shape, 0, 128, dtype=jnp.int32)
    empty = jax.random.randint(key_empty, shape, 0, 4, dtype=jnp.int32) == 0
    empty = empty | (place_ids % 4 != 0)[:, None]
    return jnp.where(empty, -1, targets).reshape(DEVS * COARSE_BLOCKS, EDGE_BLK)


def draw_prolong_idx(key, part):
    pooled = pool_counts(key)
    key = jax.random.fold_in(key, 8)
    key_owner, key_rest = jax.random.split(key)
    shape = (DEVS, NODE_DEV)
    owner_ids = jax.random.randint(key_owner, shape, 0, PEERS // 4, dtype=jnp.int32)
    spread = jax.random.randint(key_rest, shape, 0, 2 ** 20, dtype=jnp.int32)
    device_ids, dom_ids, place_ids = device_grid()
    live = pooled[device_ids[:, None], owner_ids]
    return (owner_ids * 4 * POOL_CAP + spread % live).reshape(DEVS * NODE_DEV)


def steps_of(own_key, shape, cuts, smallest, largest):
    def one(axis_at, parts):
        steps = jax.random.uniform(jax.random.fold_in(jax.random.fold_in(own_key, 6), axis_at), (parts,), jnp.float32, smallest / len(cuts), largest / len(cuts))
        return jnp.repeat(jnp.exp(steps), shape[axis_at] // parts).reshape((-1,) + (1,) * (len(shape) - axis_at - 1))

    factor_of = one(*cuts[0])
    for cut in cuts[1:]:
        factor_of = factor_of * one(*cut)
    return factor_of


def gaussian(stream_key, extent, scale, bound, shards=(), kind=jnp.bfloat16):
    values = scale * jax.random.normal(stream_key, extent, jnp.float32)
    if shards:
        values = values * steps_of(stream_key, extent, shards, -0.22, 0.18)
    return jnp.clip(values, -bound, bound).astype(kind)


def setup_inputs(seed: int = 0, part: int = 0) -> dict:
    seeds = jax.random.split(jax.random.key(seed), 13)
    part_splits = jax.random.split(jax.random.fold_in(seeds[12], part), 13)
    fine_nodes = gaussian(part_splits[0], (NODES, LATENT), 1.0, 6.0, ((0, 16),))
    fine_src = draw_fine_src(jax.random.fold_in(jax.random.fold_in(seeds[12], part), 71), part)
    fine_dst = draw_fine_dst(jax.random.fold_in(jax.random.fold_in(seeds[12], part), 71), part)
    halo_send = draw_halo_send(jax.random.fold_in(jax.random.fold_in(seeds[12], part), 71), part)
    pool_send = draw_pool_send(jax.random.fold_in(jax.random.fold_in(seeds[12], part), 71), part)
    coarse_src = draw_coarse_src(jax.random.fold_in(jax.random.fold_in(seeds[12], part), 71), part)
    coarse_dst = draw_coarse_dst(jax.random.fold_in(jax.random.fold_in(seeds[12], part), 71), part)
    coarse_send = draw_coarse_send(jax.random.fold_in(jax.random.fold_in(seeds[12], part), 71), part)
    prolong_idx = draw_prolong_idx(jax.random.fold_in(jax.random.fold_in(seeds[12], part), 71), part)
    fine_weights = gaussian(seeds[9], (2, 4, LATENT, LATENT), LATENT ** -0.5, 0.5)
    coarse_weights = gaussian(seeds[10], (4, LATENT, LATENT), LATENT ** -0.5, 0.5)
    prolong_weight = gaussian(seeds[11], (LATENT, LATENT), LATENT ** -0.5, 0.5)
    return dict(fine_nodes=fine_nodes, fine_src=fine_src, fine_dst=fine_dst, halo_send=halo_send, pool_send=pool_send, coarse_src=coarse_src, coarse_dst=coarse_dst, coarse_send=coarse_send, prolong_idx=prolong_idx, fine_weights=fine_weights, coarse_weights=coarse_weights, prolong_weight=prolong_weight)


def layer_apply(latent, extended, source_ids, target_ids, weights):
    node_count = latent.shape[0]
    sender_terms = jnp.dot(extended, weights[0], preferred_element_type=jnp.float32).astype(jnp.bfloat16)
    target_terms = jnp.dot(latent, weights[1], preferred_element_type=jnp.float32).astype(jnp.bfloat16)
    block_base = jnp.arange(source_ids.shape[0], dtype=jnp.int32)[:, None] * 128
    target_rows = (block_base + jnp.clip(target_ids, 0, 127)).reshape(-1)
    message = jax.nn.silu(sender_terms[source_ids.reshape(-1)].astype(jnp.float32)
                          + target_terms[target_rows].astype(jnp.float32)).astype(jnp.bfloat16)
    segment = jnp.where(target_ids.reshape(-1) >= 0, target_rows, node_count)
    summed = jax.ops.segment_sum(message.astype(jnp.float32), segment, num_segments=node_count + 1)[:node_count]
    summed = summed.astype(jnp.bfloat16)
    update = (jnp.dot(summed, weights[2], preferred_element_type=jnp.float32)
              + jnp.dot(latent, weights[3], preferred_element_type=jnp.float32))
    return (latent.astype(jnp.float32) + jax.nn.silu(update)).astype(jnp.bfloat16)


def halo_tables(table, send_lists):
    width = table.shape[2]
    padded = jnp.concatenate([table, jnp.zeros((table.shape[0], 1, width), table.dtype)], axis=1)
    sent_rows = jax.vmap(lambda rows, lists: rows[lists])(padded, send_lists)
    capacity = send_lists.shape[2]
    sent_rows = sent_rows.reshape(N_DOM, PEERS, N_DOM, capacity, width).transpose(2, 1, 0, 3, 4)
    return sent_rows.reshape(DEVS, N_DOM * capacity, width)


def run_level(table, send_lists, source_ids, target_ids, weights):
    halos = halo_tables(table, send_lists)

    def one_device(operands):
        latent, halo_rows, sources, targets = operands
        extended = jnp.concatenate([latent, halo_rows], axis=0)
        return layer_apply(latent, extended, sources, targets, weights)

    return lax.map(one_device, (table, halos, source_ids, target_ids))


def reference(fine_nodes, fine_src, fine_dst, halo_send, pool_send, coarse_src, coarse_dst, coarse_send, prolong_idx, fine_weights, coarse_weights, prolong_weight):
    width = fine_nodes.shape[1]
    start = fine_nodes.reshape(DEVS, NODE_DEV, width)
    fine_sources = fine_src.reshape(DEVS, FINE_BLOCKS, EDGE_BLK)
    fine_targets = fine_dst.reshape(DEVS, FINE_BLOCKS, EDGE_BLK)
    first = run_level(start, halo_send, fine_sources, fine_targets, fine_weights[0])
    padded = jnp.concatenate([first, jnp.zeros((DEVS, 1, width), jnp.bfloat16)], axis=1)
    sent_rows = jax.vmap(lambda rows, lists: rows[lists])(padded, pool_send)
    pooled = sent_rows.reshape(N_DOM, PEERS, PEERS, POOL_CAP, width).transpose(0, 2, 1, 3, 4)
    pooled = pooled.reshape(DEVS, COARSE_DEV, width)
    coarse = run_level(pooled, coarse_send,
                       coarse_src.reshape(DEVS, COARSE_BLOCKS, EDGE_BLK),
                       coarse_dst.reshape(DEVS, COARSE_BLOCKS, EDGE_BLK), coarse_weights)
    returned = coarse.reshape(N_DOM, PEERS, PEERS, POOL_CAP, width).transpose(0, 2, 1, 3, 4)
    returned = returned.reshape(DEVS, COARSE_DEV, width)
    picked = jax.vmap(lambda rows, lists: rows[lists])(returned, prolong_idx.reshape(DEVS, NODE_DEV))
    lifted_terms = jnp.dot(picked.reshape(NODES, width), prolong_weight, preferred_element_type=jnp.float32)
    lifted = (first.reshape(NODES, width).astype(jnp.float32) + jax.nn.silu(lifted_terms)).astype(jnp.bfloat16)
    final = run_level(lifted.reshape(DEVS, NODE_DEV, width), halo_send, fine_sources, fine_targets, fine_weights[1])
    return final.reshape(NODES, width)
```

```python
import functools

import jax
import jax.numpy as jnp
from jax import lax
from jax.experimental import pallas as pl
from jax.experimental.pallas import tpu as pltpu
from jax.sharding import PartitionSpec as P

BF16 = jnp.bfloat16
F32 = jnp.float32
I32 = jnp.int32
BLOCK = 128
VMEM_BYTES = 32 << 20


def dot(left, right):
    return jnp.dot(left, right, preferred_element_type=F32)


def dot_last(left, right):
    return lax.dot_general(left, right, (((1,), (1,)), ((), ())), preferred_element_type=F32)


def rows_hot(index_row, height):
    shape = (height, index_row.shape[1])
    index = jnp.broadcast_to(index_row, shape).astype(jnp.int16)
    return jnp.where(
        index == lax.broadcasted_iota(jnp.int16, shape, 0), jnp.ones((), BF16), jnp.zeros((), BF16)
    )


def columns_hot(index_column, width, wrap=None):
    shape = (index_column.shape[0], width)
    columns = lax.broadcasted_iota(I32, shape, 1)
    if wrap is not None:
        columns = lax.rem(columns, wrap)
    return jnp.where(index_column == columns, 1.0, 0.0).astype(BF16)


def silu_of_half(half):
    return half + half * jnp.tanh(half)


def halved(weight):
    return weight * jnp.asarray(0.5, BF16)


def partner_offsets(dom_count):
    offsets = []
    for offset in (1, dom_count - 1, 2 % dom_count):
        if offset not in offsets:
            offsets.append(offset)
    return tuple(offsets)


def partner_place(source_dom, own_dom, dom_count, offsets):
    step = own_dom - source_dom
    step = jnp.where(step < 0, step + dom_count, step)
    place = jnp.zeros_like(step)
    for index, offset in enumerate(offsets):
        place = jnp.where(step == offset, index, place)
    return place


def terms_of(latent, weights):
    features = latent.shape[1]
    both = jnp.concatenate([halved(weights[0]), halved(weights[1])], axis=1)
    terms = dot(latent, both).astype(BF16)
    return terms[:, :features].T, terms[:, features:].T


def emit_halo(sender_terms, lists_ref, out_refs, dom_count, offsets):
    own_dom = lax.axis_index("dom")
    for offset, out_ref in zip(offsets, out_refs):
        partner = lax.rem(own_dom + offset, dom_count)
        index_row = lists_ref[pl.ds(partner, 1), :]
        hot = rows_hot(index_row, sender_terms.shape[1])
        out_ref[...] = dot(sender_terms, hot).astype(BF16)


def terms_kernel(dom_count, offsets, latent_ref, lists_ref, weights_ref, sender_ref, target_ref, *sent_refs):
    sender, target = terms_of(latent_ref[...], weights_ref)
    sender_ref[...] = sender
    target_ref[...] = target
    emit_halo(sender, lists_ref, sent_refs, dom_count, offsets)


def near_kernel(sender_ref, target_ref, source_ref, place_ref, sums_ref):
    node_count = sender_ref.shape[1]
    block_count, slot_count = source_ref.shape
    local_count = slot_count * 3 // 4
    window = min(3 * BLOCK, node_count)

    def messages(block):
        start = min(max(block * BLOCK - BLOCK, 0), node_count - window)
        table = jnp.concatenate(
            [sender_ref[:, start : start + window], target_ref[:, block * BLOCK : (block + 1) * BLOCK]], axis=1
        )
        places = rows_hot(place_ref[block : block + 1, :local_count], BLOCK)
        sources = rows_hot(source_ref[block : block + 1, :local_count] - start, window)
        picked = dot(table, jnp.concatenate([sources, places], axis=0))
        return silu_of_half(picked).astype(BF16)

    def add_up(block, message):
        places = rows_hot(place_ref[block : block + 1, :local_count], BLOCK)
        sums_ref[block * BLOCK : (block + 1) * BLOCK, :] = dot_last(places, message)

    waiting = None
    for block in range(block_count):
        message = messages(block)
        if waiting is not None:
            add_up(*waiting)
        waiting = (block, message)
    add_up(*waiting)


def far_layer(dom_count, offsets, latent_ref, target_ref, source_ref, place_ref, sums_ref, weights_ref, halo_refs, out_ref):
    node_count, features = latent_ref.shape
    block_count, slot_count = source_ref.shape
    local_count = slot_count * 3 // 4
    capacity = halo_refs[0].shape[1]
    halo = jnp.concatenate([ref[...] for ref in halo_refs], axis=1)
    halo_rows = halo.shape[1]
    own_dom = lax.axis_index("dom")
    update_weights = jnp.concatenate([halved(weights_ref[2]), halved(weights_ref[3])], axis=0)
    shift = capacity.bit_length() - 1

    slots = source_ref[:, local_count:] - node_count
    source_dom = lax.shift_right_logical(slots, shift)
    far_sources = partner_place(source_dom, own_dom, dom_count, offsets) * capacity + (slots & (capacity - 1))

    def messages(block):
        table = jnp.concatenate([halo, target_ref[:, block * BLOCK : (block + 1) * BLOCK]], axis=1)
        places = rows_hot(place_ref[block : block + 1, local_count:], BLOCK)
        sources = rows_hot(far_sources[block : block + 1, :], halo_rows)
        picked = dot(table, jnp.concatenate([sources, places], axis=0))
        return silu_of_half(picked).astype(BF16)

    def add_up(block, message):
        rows = slice(block * BLOCK, (block + 1) * BLOCK)
        places = rows_hot(place_ref[block : block + 1, local_count:], BLOCK)
        summed = (sums_ref[rows, :] + dot_last(places, message)).astype(BF16)
        latent = latent_ref[rows, :]
        update = dot(jnp.concatenate([summed, latent], axis=1), update_weights)
        out_ref[rows, :] = (latent.astype(F32) + silu_of_half(update)).astype(BF16)

    waiting = None
    for block in range(block_count):
        message = messages(block)
        if waiting is not None:
            add_up(*waiting)
        waiting = (block, message)
    add_up(*waiting)


def lane_rows(ref):
    pieces = []
    for block in range(ref.shape[0]):
        for start in range(0, ref.shape[1], BLOCK):
            pieces.append(ref[block : block + 1, start : start + BLOCK])
    return pieces


def far_pool_kernel(
    dom_count,
    offsets,
    latent_ref,
    target_ref,
    source_ref,
    place_ref,
    sums_ref,
    weights_ref,
    pool_ref,
    coarse_source_ref,
    coarse_place_ref,
    coarse_send_ref,
    *rest,
):
    halo_refs, (out_ref, packet_ref) = rest[:-2], rest[-2:]
    far_layer(dom_count, offsets, latent_ref, target_ref, source_ref, place_ref, sums_ref, weights_ref, halo_refs, out_ref)
    owners = range(0, pool_ref.shape[0], 4)
    capacity = pool_ref.shape[1]
    first = out_ref[...]
    lists = jnp.concatenate([pool_ref[owner : owner + 1, :] for owner in owners], axis=1).T
    packet_ref[: len(owners) * capacity, :] = dot(columns_hot(lists, first.shape[0]), first).astype(BF16)
    pieces = lane_rows(coarse_source_ref) + [coarse_send_ref[...]] + lane_rows(coarse_place_ref)
    spare = -sum(piece.shape[0] for piece in pieces) % 16
    if spare:
        pieces.append(jnp.zeros((spare, BLOCK), I32))
    whole = jnp.concatenate(pieces, axis=0) + 1
    high = lax.shift_right_logical(whole, 8)
    packet_ref[len(owners) * capacity :, :] = jnp.concatenate(
        [high.astype(F32), (whole & 255).astype(F32)], axis=0
    ).astype(BF16)


def packet_rows(count):
    return -(-count // 16) * 16


def far_kernel(dom_count, offsets, latent_ref, target_ref, source_ref, place_ref, sums_ref, weights_ref, *rest):
    far_layer(
        dom_count, offsets, latent_ref, target_ref, source_ref, place_ref, sums_ref, weights_ref, rest[:-1], rest[-1]
    )


def own_place(grid):
    return lax.axis_index("sub") * grid.chip_count + lax.axis_index("chip")


class Grid:
    def __init__(self, mesh, pool_capacity, coarse_capacity, coarse_blocks, slot_count):
        self.dom_count = mesh.shape["dom"]
        self.sub_count = mesh.shape["sub"]
        self.chip_count = mesh.shape["chip"]
        self.places = self.sub_count * self.chip_count
        self.offsets = partner_offsets(self.dom_count)
        self.owners = len(range(0, self.places, 4))
        self.swapped = self.sub_count == 2 and self.chip_count == 2
        self.pool_capacity = pool_capacity
        self.coarse_capacity = coarse_capacity
        self.blocks = coarse_blocks
        self.pieces = slot_count // BLOCK
        self.slots = self.places * pool_capacity
        self.pooled_rows = self.owners * pool_capacity
        self.list_rows = 2 * coarse_blocks * self.pieces + self.dom_count
        self.packed_rows = packet_rows(self.list_rows)
        self.packet = self.pooled_rows + 2 * self.packed_rows


def owner_lists(grid, packets, owner, place):
    if grid.swapped:
        rows = packets[0][grid.pooled_rows :, :].astype(F32)
        for other in range(1, grid.places):
            rows = jnp.where(place == other, packets[other][grid.pooled_rows :, :].astype(F32), rows)
    else:
        rows = packets[4 * owner][grid.pooled_rows :, :].astype(F32)
    whole = rows[: grid.packed_rows] * 256.0 + rows[grid.packed_rows :]
    return whole.astype(I32) - 1


def owner_table(grid, packets, owner):
    start = owner * grid.pool_capacity
    return jnp.concatenate([packet[start : start + grid.pool_capacity, :] for packet in packets], axis=0)


def slot_order(grid, slots, place):
    return slots ^ (place * grid.pool_capacity) if grid.swapped else slots


def coarse_send_kernel(grid, weights_ref, *refs):
    packets = refs[: grid.places]
    outs = refs[grid.places : grid.places + len(grid.offsets)]
    lists_ref = refs[-1]
    place = own_place(grid)
    own_dom = lax.axis_index("dom")
    first_list = grid.blocks * grid.pieces
    for owner in range(grid.owners):
        lists_ref[...] = owner_lists(grid, packets, owner, place)
        table = owner_table(grid, packets, owner)
        terms = dot(table, halved(weights_ref[0])).astype(BF16).T
        for offset, out_ref in zip(grid.offsets, outs):
            partner = lax.rem(own_dom + offset, grid.dom_count)
            index_row = slot_order(grid, lists_ref[pl.ds(first_list + partner, 1), :], place)
            picked = dot(terms, rows_hot(index_row, grid.slots))
            out_ref[owner * BLOCK : (owner + 1) * BLOCK, :] = picked.astype(BF16)


def coarse_own_kernel(grid, weights_ref, *refs):
    packets = refs[: grid.places]
    picked_ref, source_out, place_out, rows_out, lists_ref = refs[grid.places :]
    place = own_place(grid)
    own_dom = lax.axis_index("dom")
    first_slot = place * grid.pool_capacity
    block = lax.shift_right_logical(first_slot, BLOCK.bit_length() - 1)
    within = first_slot & (BLOCK - 1)
    shift = grid.coarse_capacity.bit_length() - 1
    for owner in range(grid.owners):
        lists_ref[...] = owner_lists(grid, packets, owner, place)
        sources = jnp.concatenate(
            [lists_ref[pl.ds(block * grid.pieces + piece, 1), :] for piece in range(grid.pieces)], axis=1
        )
        offset = grid.blocks * grid.pieces + grid.dom_count
        places = jnp.concatenate(
            [lists_ref[pl.ds(offset + block * grid.pieces + piece, 1), :] for piece in range(grid.pieces)], axis=1
        )
        places = places - within
        places = jnp.where((places >= 0) & (places < grid.pool_capacity), places, -1)
        halo_slots = sources - grid.slots
        source_dom = lax.shift_right_arithmetic(halo_slots, shift)
        halo_sources = partner_place(source_dom, own_dom, grid.dom_count, grid.offsets) * grid.coarse_capacity + (
            halo_slots & (grid.coarse_capacity - 1)
        )
        is_halo = halo_slots >= 0
        source_out[owner : owner + 1, :] = jnp.where(is_halo, halo_sources, -1)
        place_out[owner : owner + 1, :] = places
        own_sources = jnp.where(is_halo, -1, slot_order(grid, sources, place))

        table = owner_table(grid, packets, owner)
        if grid.swapped:
            rows = table[: grid.pool_capacity]
        else:
            rows = table[: grid.pool_capacity]
            for other in range(1, grid.places):
                other_rows = table[other * grid.pool_capacity : (other + 1) * grid.pool_capacity]
                rows = jnp.where(place == other, other_rows, rows)
        rows_out[owner * grid.pool_capacity : (owner + 1) * grid.pool_capacity, :] = rows
        sender = dot(table, halved(weights_ref[0])).astype(BF16).T
        target = dot(rows, halved(weights_ref[1])).astype(BF16).T
        hot = jnp.concatenate([rows_hot(own_sources, grid.slots), rows_hot(places, grid.pool_capacity)], axis=0)
        picked_ref[owner] = dot(jnp.concatenate([sender, target], axis=1), hot)


def lift_kernel(
    grid,
    picked_ref,
    source_ref,
    place_ref,
    rows_ref,
    coarse_weights_ref,
    prolong_weight_ref,
    prolong_ref,
    first_ref,
    weights_ref,
    lists_ref,
    *rest,
):
    count = len(grid.offsets)
    halo_refs = rest[:count]
    lifted_ref, sender_ref, target_ref = rest[count : count + 3]
    sent_refs = rest[count + 3 :]
    update_weights = jnp.concatenate([halved(coarse_weights_ref[2]), halved(coarse_weights_ref[3])], axis=0)
    prolonged = []
    for owner in range(grid.owners):
        halo = jnp.concatenate([ref[owner * BLOCK : (owner + 1) * BLOCK, :] for ref in halo_refs], axis=1)
        picked = picked_ref[owner] + dot(halo, rows_hot(source_ref[owner : owner + 1, :], halo.shape[1]))
        message = silu_of_half(picked).astype(BF16)
        places = rows_hot(place_ref[owner : owner + 1, :], grid.pool_capacity)
        summed = dot_last(places, message).astype(BF16)
        rows = rows_ref[owner * grid.pool_capacity : (owner + 1) * grid.pool_capacity, :]
        update = dot(jnp.concatenate([summed, rows], axis=1), update_weights)
        coarse = (rows.astype(F32) + silu_of_half(update)).astype(BF16)
        prolonged.append(dot(coarse, halved(prolong_weight_ref[...])))
    prolonged = jnp.concatenate(prolonged, axis=0)
    high = prolonged.astype(BF16)
    low = (prolonged - high.astype(F32)).astype(BF16)
    table = jnp.concatenate([high, low], axis=0)
    indices = prolong_ref[...]
    shift = (4 * grid.pool_capacity).bit_length() - 1
    indices = lax.shift_right_logical(indices, shift) * grid.pool_capacity + (indices & (grid.pool_capacity - 1))
    columns = indices.T
    node_count = first_ref.shape[0]
    for block in range(node_count // BLOCK):
        rows = slice(block * BLOCK, (block + 1) * BLOCK)
        hot = columns_hot(columns[:, block : block + 1], table.shape[0], grid.pooled_rows)
        lifted_ref[rows, :] = (first_ref[rows, :].astype(F32) + silu_of_half(dot(hot, table))).astype(BF16)
    sender, target = terms_of(lifted_ref[...], weights_ref)
    sender_ref[...] = sender
    target_ref[...] = target
    emit_halo(sender, lists_ref, sent_refs, grid.dom_count, grid.offsets)


def call(kernel, outs, scratch=(), flops=0, name=None):
    return pl.pallas_call(
        kernel,
        out_shape=tuple(jax.ShapeDtypeStruct(shape, dtype) for shape, dtype in outs),
        scratch_shapes=list(scratch),
        compiler_params=pltpu.CompilerParams(vmem_limit_bytes=VMEM_BYTES),
        cost_estimate=pl.CostEstimate(flops=flops, bytes_accessed=4 << 20, transcendentals=0),
        name=name,
    )


def swap_dom(arrays, dom_count, offsets):
    return [
        lax.ppermute(array, "dom", [(place, (place + offset) % dom_count) for place in range(dom_count)])
        for array, offset in zip(arrays, offsets)
    ]


def trade_packets(grid, packet):
    if grid.swapped:
        pairs = [(0, 1), (1, 0)]
        across = lax.ppermute(packet, "chip", pairs)
        return [packet, across, lax.ppermute(packet, "sub", pairs), lax.ppermute(across, "sub", pairs)]
    gathered = lax.all_gather(packet, ("sub", "chip"), axis=0, tiled=False)
    return [gathered[place] for place in range(grid.places)]


def body(
    mesh,
    fine_nodes,
    fine_src,
    fine_dst,
    halo_send,
    pool_send,
    coarse_src,
    coarse_dst,
    coarse_send,
    prolong_idx,
    fine_weights,
    coarse_weights,
    prolong_weight,
):
    node_count, features = fine_nodes.shape
    slot_count = fine_src.shape[1]
    grid = Grid(mesh, pool_send.shape[2], coarse_send.shape[2], coarse_src.shape[0], coarse_src.shape[1])
    halo_capacity = halo_send.shape[2]
    dom_count, offsets = grid.dom_count, grid.offsets
    lists = halo_send[0]
    table = ((features, node_count), BF16)
    halo_outs = [((features, halo_capacity), BF16)] * len(offsets)
    nodes = ((node_count, features), BF16)
    big = 1 << 30

    sender, target, *sent = call(
        functools.partial(terms_kernel, dom_count, offsets), [table, table, *halo_outs], flops=big, name="terms"
    )(fine_nodes, lists, fine_weights[0])
    halo = swap_dom(sent, dom_count, offsets)
    (sums,) = call(near_kernel, [((node_count, features), F32)], flops=4 * big, name="near")(
        sender, target, fine_src, fine_dst
    )
    first, packet = call(
        functools.partial(far_pool_kernel, dom_count, offsets),
        [nodes, ((grid.packet, features), BF16)],
        flops=2 * big,
        name="far_pool",
    )(
        fine_nodes,
        target,
        fine_src,
        fine_dst,
        sums,
        fine_weights[0],
        pool_send[0],
        coarse_src,
        coarse_dst,
        coarse_send[0],
        *halo,
    )
    packets = trade_packets(grid, packet)
    lists_scratch = pltpu.VMEM((grid.packed_rows, BLOCK), I32)
    sent = call(
        functools.partial(coarse_send_kernel, grid),
        [((grid.owners * features, grid.coarse_capacity), BF16)] * len(offsets),
        [lists_scratch],
        flops=big // 2,
        name="coarse_send",
    )(coarse_weights, *packets)
    coarse_halo = swap_dom(sent, dom_count, offsets)
    coarse_slots = coarse_src.shape[1]
    picked, sources, places, rows = call(
        functools.partial(coarse_own_kernel, grid),
        [
            ((grid.owners, features, coarse_slots), F32),
            ((grid.owners, coarse_slots), I32),
            ((grid.owners, coarse_slots), I32),
            ((grid.pooled_rows, features), BF16),
        ],
        [lists_scratch],
        flops=4 * big,
        name="coarse_own",
    )(coarse_weights, *packets)
    lifted, sender, target, *sent = call(
        functools.partial(lift_kernel, grid), [nodes, table, table, *halo_outs], flops=2 * big, name="lift"
    )(
        picked,
        sources,
        places,
        rows,
        coarse_weights,
        prolong_weight,
        prolong_idx.reshape(node_count // BLOCK, BLOCK),
        first,
        fine_weights[1],
        lists,
        *coarse_halo,
    )
    halo = swap_dom(sent, dom_count, offsets)
    (sums,) = call(near_kernel, [((node_count, features), F32)], flops=4 * big, name="near")(
        sender, target, fine_src, fine_dst
    )
    (fine_out,) = call(functools.partial(far_kernel, dom_count, offsets), [nodes], flops=2 * big, name="far")(
        lifted, target, fine_src, fine_dst, sums, fine_weights[1], *halo
    )
    return fine_out


def solution(mesh):
    split = ("groups", "dom", "sub", "chip")
    return jax.shard_map(
        functools.partial(body, mesh),
        mesh=mesh,
        in_specs=(
            P(split, None),
            P(split, None),
            P(split, None),
            P(split, None, None),
            P(split, None, None),
            P(split, None),
            P(split, None),
            P(split, None, None),
            P(split),
            P(),
            P(),
            P(),
        ),
        out_specs=P(split, None),
        check_vma=False,
    )
```

```python
import functools

import jax
import jax.numpy as jnp
from jax import lax
from jax.experimental import pallas as pl
from jax.experimental.pallas import tpu as pltpu
from jax.sharding import PartitionSpec as P

BF16 = jnp.bfloat16
F32 = jnp.float32
I32 = jnp.int32
BLOCK = 128
VMEM_BYTES = 32 << 20
GROUP = 4
LAG = 2


def dot(left, right):
    return jnp.dot(left, right, preferred_element_type=F32)


def dot_last(left, right):
    return lax.dot_general(left, right, (((1,), (1,)), ((), ())), preferred_element_type=F32)


def rows_hot(index_row, height):
    shape = (height, index_row.shape[1])
    index = jnp.broadcast_to(index_row, shape).astype(jnp.int16)
    return jnp.where(
        index == lax.broadcasted_iota(jnp.int16, shape, 0), jnp.ones((), BF16), jnp.zeros((), BF16)
    )


def silu_of_half(half):
    return half + half * jnp.tanh(half)


def halved(weight):
    return weight * jnp.asarray(0.5, BF16)


class Grid:
    def __init__(self, mesh, pool_capacity, coarse_capacity, coarse_blocks, slot_count):
        self.dom_count = mesh.shape["dom"]
        self.sub_count = mesh.shape["sub"]
        self.chip_count = mesh.shape["chip"]
        self.places = self.sub_count * self.chip_count
        self.mirrored = self.dom_count == 4
        self.steps = (1, 2, 3) if self.mirrored else tuple(sorted({1, self.dom_count - 1, 2 % self.dom_count}))
        self.owners = len(range(0, self.places, 4))
        self.swapped = self.sub_count == 2 and self.chip_count == 2
        self.pool_capacity = pool_capacity
        self.coarse_capacity = coarse_capacity
        self.blocks = coarse_blocks
        self.pieces = slot_count // BLOCK
        self.slots = self.places * pool_capacity
        self.pooled_rows = self.owners * pool_capacity
        self.list_rows = 2 * coarse_blocks * self.pieces + self.dom_count
        self.packed_rows = -(-self.list_rows // 16) * 16
        self.packet = self.pooled_rows + 2 * self.packed_rows

    def partner(self, dom, step):
        return dom ^ step if self.mirrored else (dom + step) % self.dom_count

    def partner_here(self, step):
        own = lax.axis_index("dom")
        return own ^ step if self.mirrored else lax.rem(own + step, self.dom_count)

    def halo_place(self, source_dom):
        own = lax.axis_index("dom")
        if self.mirrored:
            step = source_dom ^ own
        else:
            step = own - source_dom
            step = jnp.where(step < 0, step + self.dom_count, step)
        place = jnp.zeros_like(step)
        for index, value in enumerate(self.steps):
            place = jnp.where(step == value, index, place)
        return place

    def own_place(self):
        return lax.axis_index("sub") * self.chip_count + lax.axis_index("chip")

    def slot_order(self, slots, place):
        return slots ^ (place * self.pool_capacity) if self.swapped else slots


def turned(weight):
    return halved(weight).T


def send_kernel(grid, latent_hbm, lists_hbm, weights_hbm, table_ref, *rest):
    sent_refs = rest[: len(grid.steps)]
    latent_ref, lists_ref, weight_ref, arrived = rest[len(grid.steps) :]
    copies = [
        pltpu.make_async_copy(lists_hbm.at[0], lists_ref, arrived.at[0]),
        pltpu.make_async_copy(weights_hbm.at[0, 0], weight_ref, arrived.at[1]),
        pltpu.make_async_copy(latent_hbm, latent_ref, arrived.at[2]),
    ]
    for copy in copies:
        copy.start()
    for copy in copies:
        copy.wait()
    table = latent_ref[...].T
    table_ref[...] = table
    weight = turned(weight_ref[...])
    for step, out_ref in zip(grid.steps, sent_refs):
        index_row = lists_ref[pl.ds(grid.partner_here(step), 1), :]
        picked = dot(table, rows_hot(index_row, table.shape[1])).astype(BF16)
        out_ref[...] = dot(weight, picked).astype(BF16)


def near_edges(table, source_ref, place_ref, weights_ref, layer, target_ref, sums_ref, terms_ref):
    features, node_count = table.shape
    block_count, slot_count = source_ref.shape
    local_count = slot_count * 3 // 4
    window = min(3 * BLOCK, node_count)
    both = jnp.concatenate([turned(weights_ref[layer, 0]), turned(weights_ref[layer, 1])], axis=0)
    terms_ref[...] = dot(both, table).astype(BF16)
    target_ref[...] = terms_ref[features:, :]

    def messages(block):
        start = min(max(block * BLOCK - BLOCK, 0), node_count - window)
        terms = jnp.concatenate(
            [
                terms_ref[:features, start : start + window],
                terms_ref[features:, block * BLOCK : (block + 1) * BLOCK],
            ],
            axis=1,
        )
        places = rows_hot(place_ref[block : block + 1, :local_count], BLOCK)
        sources = rows_hot(source_ref[block : block + 1, :local_count] - start, window)
        picked = dot(terms, jnp.concatenate([sources, places], axis=0))
        return silu_of_half(picked).astype(BF16)

    def add_up(block, message):
        places = rows_hot(place_ref[block : block + 1, :local_count], BLOCK)
        sums_ref[:, block * BLOCK : (block + 1) * BLOCK] = dot_last(message, places)

    waiting = None
    for block in range(block_count):
        message = messages(block)
        if waiting is not None:
            add_up(*waiting)
        waiting = (block, message)
    add_up(*waiting)


def near_kernel(layer, table_ref, source_ref, place_ref, weights_ref, target_ref, sums_ref, terms_ref):
    near_edges(table_ref[...], source_ref, place_ref, weights_ref, layer, target_ref, sums_ref, terms_ref)


def far_edges(grid, layer, table_ref, target_ref, source_ref, place_ref, sums_ref, weights_ref, halo_refs, both_ref, write):
    features, node_count = table_ref.shape
    block_count, slot_count = source_ref.shape
    local_count = slot_count * 3 // 4
    capacity = halo_refs[0].shape[1]
    halo = jnp.concatenate([ref[...] for ref in halo_refs], axis=1)
    halo_rows = halo.shape[1]
    update_weights = jnp.concatenate([turned(weights_ref[layer, 2]), turned(weights_ref[layer, 3])], axis=1)
    shift = capacity.bit_length() - 1
    slots = source_ref[:, local_count:] - node_count
    source_dom = lax.shift_right_logical(slots, shift)
    far_sources = grid.halo_place(source_dom) * capacity + (slots & (capacity - 1))
    both_ref[features:, :] = table_ref[...]

    def messages(block):
        terms = jnp.concatenate([halo, target_ref[:, block * BLOCK : (block + 1) * BLOCK]], axis=1)
        places = rows_hot(place_ref[block : block + 1, local_count:], BLOCK)
        sources = rows_hot(far_sources[block : block + 1, :], halo_rows)
        picked = dot(terms, jnp.concatenate([sources, places], axis=0))
        return silu_of_half(picked).astype(BF16)

    def add_up(block, message):
        columns = slice(block * BLOCK, (block + 1) * BLOCK)
        places = rows_hot(place_ref[block : block + 1, local_count:], BLOCK)
        both_ref[:features, columns] = (sums_ref[:, columns] + dot_last(message, places)).astype(BF16)

    def update(block):
        columns = slice((block - GROUP + 1) * BLOCK, (block + 1) * BLOCK)
        change = silu_of_half(dot(update_weights, both_ref[:, columns]))
        write(columns, (both_ref[features:, columns].astype(F32) + change).astype(BF16))

    waiting = []
    for block in range(block_count):
        waiting.append((block, messages(block)))
        if len(waiting) > LAG:
            done = waiting.pop(0)
            add_up(*done)
            if (done[0] + 1) % GROUP == 0 and done[0] >= 0:
                update(done[0])
    for done in waiting:
        add_up(*done)
        if (done[0] + 1) % GROUP == 0:
            update(done[0])


def lane_rows(ref):
    pieces = []
    for block in range(ref.shape[0]):
        for start in range(0, ref.shape[1], BLOCK):
            pieces.append(ref[block : block + 1, start : start + BLOCK])
    return pieces


def far_pool_kernel(
    grid,
    table_ref,
    target_ref,
    source_ref,
    place_ref,
    sums_ref,
    weights_ref,
    pool_ref,
    coarse_source_ref,
    coarse_place_ref,
    coarse_send_ref,
    *rest,
):
    halo_refs, (first_ref, packet_ref, both_ref) = rest[:-3], rest[-3:]

    def write(columns, value):
        first_ref[:, columns] = value

    pieces = lane_rows(coarse_source_ref) + [coarse_send_ref[0]] + lane_rows(coarse_place_ref)
    spare = grid.packed_rows - grid.list_rows
    if spare:
        pieces.append(jnp.zeros((spare, BLOCK), I32))
    whole = jnp.concatenate(pieces, axis=0) + 1
    high = lax.shift_right_logical(whole, 8)
    packet_ref[grid.pooled_rows :, :] = jnp.concatenate(
        [high.astype(F32), (whole & 255).astype(F32)], axis=0
    ).astype(BF16)
    far_edges(
        grid, 0, table_ref, target_ref, source_ref, place_ref, sums_ref, weights_ref, halo_refs, both_ref, write
    )
    for owner in range(grid.owners):
        hot = rows_hot(pool_ref[0, 4 * owner : 4 * owner + 1, :], first_ref.shape[1])
        pooled = dot(first_ref[...], hot).astype(BF16).T
        packet_ref[owner * grid.pool_capacity : (owner + 1) * grid.pool_capacity, :] = pooled


def far_kernel(grid, table_ref, target_ref, source_ref, place_ref, sums_ref, weights_ref, *rest):
    halo_refs, (out_ref, both_ref) = rest[:-2], rest[-2:]

    def write(columns, value):
        out_ref[columns, :] = value.T

    far_edges(
        grid, 1, table_ref, target_ref, source_ref, place_ref, sums_ref, weights_ref, halo_refs, both_ref, write
    )


def ahead_kernel(grid, first_ref, prolong_ref, lists_ref, out_ref):
    indices = prolong_ref[...]
    shift = (4 * grid.pool_capacity).bit_length() - 1
    indices = lax.shift_right_logical(indices, shift) * grid.pool_capacity + (indices & (grid.pool_capacity - 1))
    indices = indices.astype(F32)
    row = jnp.concatenate([indices[block : block + 1, :] for block in range(indices.shape[0])], axis=1)
    extra = jnp.concatenate([row, jnp.zeros((15, row.shape[1]), F32)], axis=0).astype(BF16)
    table = jnp.concatenate([first_ref[...], extra], axis=0)
    capacity = lists_ref.shape[2]
    for index, step in enumerate(grid.steps):
        index_row = lists_ref[0, pl.ds(grid.partner_here(step), 1), :]
        picked = dot(table, rows_hot(index_row, table.shape[1]))
        out_ref[:, index * capacity : (index + 1) * capacity] = picked.astype(BF16)


def owner_lists(grid, packets, owner, place):
    if grid.swapped:
        rows = packets[0][grid.pooled_rows :, :].astype(F32)
        for other in range(1, grid.places):
            rows = jnp.where(place == other, packets[other][grid.pooled_rows :, :].astype(F32), rows)
    else:
        rows = packets[4 * owner][grid.pooled_rows :, :].astype(F32)
    whole = rows[: grid.packed_rows] * 256.0 + rows[grid.packed_rows :]
    return whole.astype(I32) - 1


def owner_table(grid, packets, owner):
    start = owner * grid.pool_capacity
    return jnp.concatenate([packet[start : start + grid.pool_capacity, :] for packet in packets], axis=0)


def coarse_send_kernel(grid, weights_ref, *refs):
    packets = refs[: grid.places]
    outs = refs[grid.places : grid.places + len(grid.steps)]
    lists_ref = refs[-1]
    place = grid.own_place()
    first_list = grid.blocks * grid.pieces
    for owner in range(grid.owners):
        lists_ref[...] = owner_lists(grid, packets, owner, place)
        table = owner_table(grid, packets, owner)
        terms = dot(table, halved(weights_ref[0])).astype(BF16).T
        for step, out_ref in zip(grid.steps, outs):
            index_row = grid.slot_order(lists_ref[pl.ds(first_list + grid.partner_here(step), 1), :], place)
            picked = dot(terms, rows_hot(index_row, grid.slots))
            out_ref[owner * BLOCK : (owner + 1) * BLOCK, :] = picked.astype(BF16)


def coarse_own_kernel(grid, weights_ref, *refs):
    packets = refs[: grid.places]
    picked_ref, source_out, place_out, rows_out, lists_ref = refs[grid.places :]
    place = grid.own_place()
    first_slot = place * grid.pool_capacity
    block = lax.shift_right_logical(first_slot, BLOCK.bit_length() - 1)
    within = first_slot & (BLOCK - 1)
    shift = grid.coarse_capacity.bit_length() - 1
    for owner in range(grid.owners):
        lists_ref[...] = owner_lists(grid, packets, owner, place)
        sources = jnp.concatenate(
            [lists_ref[pl.ds(block * grid.pieces + piece, 1), :] for piece in range(grid.pieces)], axis=1
        )
        offset = grid.blocks * grid.pieces + grid.dom_count
        places = jnp.concatenate(
            [lists_ref[pl.ds(offset + block * grid.pieces + piece, 1), :] for piece in range(grid.pieces)], axis=1
        )
        places = places - within
        places = jnp.where((places >= 0) & (places < grid.pool_capacity), places, -1)
        halo_slots = sources - grid.slots
        source_dom = lax.shift_right_arithmetic(halo_slots, shift)
        halo_sources = grid.halo_place(source_dom) * grid.coarse_capacity + (halo_slots & (grid.coarse_capacity - 1))
        is_halo = halo_slots >= 0
        source_out[owner : owner + 1, :] = jnp.where(is_halo, halo_sources, -1)
        place_out[owner : owner + 1, :] = places
        own_sources = jnp.where(is_halo, -1, grid.slot_order(sources, place))

        table = owner_table(grid, packets, owner)
        rows = table[: grid.pool_capacity]
        if not grid.swapped:
            for other in range(1, grid.places):
                other_rows = table[other * grid.pool_capacity : (other + 1) * grid.pool_capacity]
                rows = jnp.where(place == other, other_rows, rows)
        rows_out[owner * grid.pool_capacity : (owner + 1) * grid.pool_capacity, :] = rows
        sender = dot(table, halved(weights_ref[0])).astype(BF16).T
        target = dot(rows, halved(weights_ref[1])).astype(BF16).T
        hot = jnp.concatenate([rows_hot(own_sources, grid.slots), rows_hot(places, grid.pool_capacity)], axis=0)
        picked_ref[owner] = dot(jnp.concatenate([sender, target], axis=1), hot)


def lift(table, prolonged, index_row):
    pooled_rows = prolonged.shape[1] // 2
    hot = rows_hot(index_row, pooled_rows)
    hot = jnp.concatenate([hot, hot], axis=0)
    return (table.astype(F32) + silu_of_half(dot(prolonged, hot))).astype(BF16)


def lift_halo_kernel(
    grid,
    picked_ref,
    source_ref,
    place_ref,
    rows_ref,
    ahead_ref,
    coarse_weights_ref,
    prolong_weight_ref,
    weights_ref,
    *rest,
):
    count = len(grid.steps)
    halo_refs, prolonged_ref, sent_refs = rest[:count], rest[count], rest[count + 1 :]
    features = rows_ref.shape[1]
    update_weights = jnp.concatenate([halved(coarse_weights_ref[2]), halved(coarse_weights_ref[3])], axis=0)
    prolonged = []
    for owner in range(grid.owners):
        halo = jnp.concatenate([ref[owner * BLOCK : (owner + 1) * BLOCK, :] for ref in halo_refs], axis=1)
        picked = picked_ref[owner] + dot(halo, rows_hot(source_ref[owner : owner + 1, :], halo.shape[1]))
        message = silu_of_half(picked).astype(BF16)
        places = rows_hot(place_ref[owner : owner + 1, :], grid.pool_capacity)
        summed = dot_last(places, message).astype(BF16)
        rows = rows_ref[owner * grid.pool_capacity : (owner + 1) * grid.pool_capacity, :]
        update = dot(jnp.concatenate([summed, rows], axis=1), update_weights)
        coarse = (rows.astype(F32) + silu_of_half(update)).astype(BF16)
        prolonged.append(dot(coarse, halved(prolong_weight_ref[...])))
    prolonged = jnp.concatenate(prolonged, axis=0)
    high = prolonged.astype(BF16)
    low = (prolonged - high.astype(F32)).astype(BF16)
    parts = jnp.concatenate([high, low], axis=0).T
    prolonged_ref[...] = parts
    weight = turned(weights_ref[1, 0])
    index_row = ahead_ref[features : features + 1, :].astype(F32).astype(I32)
    lifted = lift(ahead_ref[:features, :], parts, index_row)
    terms = dot(weight, lifted).astype(BF16)
    capacity = sent_refs[0].shape[1]
    for index, out_ref in enumerate(sent_refs):
        out_ref[...] = terms[:, index * capacity : (index + 1) * capacity]


def lift_near_kernel(
    grid,
    first_ref,
    prolonged_ref,
    prolong_ref,
    source_ref,
    place_ref,
    weights_ref,
    lifted_ref,
    target_ref,
    sums_ref,
    terms_ref,
):
    indices = prolong_ref[...]
    shift = (4 * grid.pool_capacity).bit_length() - 1
    indices = lax.shift_right_logical(indices, shift) * grid.pool_capacity + (indices & (grid.pool_capacity - 1))
    row = jnp.concatenate([indices[block : block + 1, :] for block in range(indices.shape[0])], axis=1)
    lifted = lift(first_ref[...], prolonged_ref[...], row)
    lifted_ref[...] = lifted
    near_edges(lifted, source_ref, place_ref, weights_ref, 1, target_ref, sums_ref, terms_ref)


def call(kernel, outs, scratch=(), flops=0, name=None, **specs):
    return pl.pallas_call(
        kernel,
        out_shape=tuple(jax.ShapeDtypeStruct(shape, dtype) for shape, dtype in outs),
        scratch_shapes=list(scratch),
        compiler_params=pltpu.CompilerParams(vmem_limit_bytes=VMEM_BYTES),
        cost_estimate=pl.CostEstimate(flops=flops, bytes_accessed=4 << 20, transcendentals=0),
        name=name,
        **specs,
    )


def swap_dom(grid, arrays):
    return [
        lax.ppermute(array, "dom", [(dom, grid.partner(dom, step)) for dom in range(grid.dom_count)])
        for array, step in zip(arrays, grid.steps)
    ]


def trade_packets(grid, packet):
    if grid.swapped:
        pairs = [(0, 1), (1, 0)]
        over = lax.ppermute(packet, "sub", pairs)
        across = lax.ppermute(packet, "chip", pairs)
        return [packet, across, over, lax.ppermute(over, "chip", pairs)]
    gathered = lax.all_gather(packet, ("sub", "chip"), axis=0, tiled=False)
    return [gathered[place] for place in range(grid.places)]


def body(
    mesh,
    fine_nodes,
    fine_src,
    fine_dst,
    halo_send,
    pool_send,
    coarse_src,
    coarse_dst,
    coarse_send,
    prolong_idx,
    fine_weights,
    coarse_weights,
    prolong_weight,
):
    node_count, features = fine_nodes.shape
    grid = Grid(mesh, pool_send.shape[2], coarse_send.shape[2], coarse_src.shape[0], coarse_src.shape[1])
    halo_capacity = halo_send.shape[2]
    steps = len(grid.steps)
    table = ((features, node_count), BF16)
    sums_table = ((features, node_count), F32)
    halo_outs = [((features, halo_capacity), BF16)] * steps
    two_tables = pltpu.VMEM((2 * features, node_count), BF16)
    prolong_rows = prolong_idx.reshape(node_count // BLOCK, BLOCK)
    big = 1 << 30
    in_hbm = pl.BlockSpec(memory_space=pltpu.HBM)

    nodes, *sent = call(
        functools.partial(send_kernel, grid),
        [table, *halo_outs],
        [
            pltpu.VMEM((node_count, features), BF16),
            pltpu.VMEM(halo_send.shape[1:], I32),
            pltpu.VMEM((features, features), BF16),
            pltpu.SemaphoreType.DMA((3,)),
        ],
        flops=big,
        name="send",
        in_specs=[in_hbm] * 3,
    )(fine_nodes, halo_send, fine_weights)
    halo = swap_dom(grid, sent)
    target, sums = call(
        functools.partial(near_kernel, 0), [table, sums_table], [two_tables], flops=4 * big, name="near"
    )(nodes, fine_src, fine_dst, fine_weights)
    first, packet = call(
        functools.partial(far_pool_kernel, grid),
        [table, ((grid.packet, features), BF16)],
        [two_tables],
        flops=2 * big,
        name="far_pool",
    )(
        nodes,
        target,
        fine_src,
        fine_dst,
        sums,
        fine_weights,
        pool_send,
        coarse_src,
        coarse_dst,
        coarse_send,
        *halo,
    )
    packets = trade_packets(grid, packet)
    (ahead,) = call(
        functools.partial(ahead_kernel, grid), [((features + 16, steps * halo_capacity), BF16)], flops=big, name="ahead"
    )(first, prolong_rows, halo_send)
    lists_scratch = pltpu.VMEM((grid.packed_rows, BLOCK), I32)
    sent = call(
        functools.partial(coarse_send_kernel, grid),
        [((grid.owners * features, grid.coarse_capacity), BF16)] * steps,
        [lists_scratch],
        flops=big // 2,
        name="coarse_send",
    )(coarse_weights, *packets)
    coarse_halo = swap_dom(grid, sent)
    coarse_slots = coarse_src.shape[1]
    picked, sources, places, rows = call(
        functools.partial(coarse_own_kernel, grid),
        [
            ((grid.owners, features, coarse_slots), F32),
            ((grid.owners, coarse_slots), I32),
            ((grid.owners, coarse_slots), I32),
            ((grid.pooled_rows, features), BF16),
        ],
        [lists_scratch],
        flops=4 * big,
        name="coarse_own",
    )(coarse_weights, *packets)
    prolonged, *sent = call(
        functools.partial(lift_halo_kernel, grid),
        [((features, 2 * grid.pooled_rows), BF16), *halo_outs],
        flops=big,
        name="lift_halo",
    )(picked, sources, places, rows, ahead, coarse_weights, prolong_weight, fine_weights, *coarse_halo)
    halo = swap_dom(grid, sent)
    lifted, target, sums = call(
        functools.partial(lift_near_kernel, grid),
        [table, table, sums_table],
        [two_tables],
        flops=4 * big,
        name="lift_near",
    )(first, prolonged, prolong_rows, fine_src, fine_dst, fine_weights)
    (fine_out,) = call(
        functools.partial(far_kernel, grid), [((node_count, features), BF16)], [two_tables], flops=2 * big, name="far"
    )(lifted, target, fine_src, fine_dst, sums, fine_weights, *halo)
    return fine_out


def solution(mesh):
    split = ("groups", "dom", "sub", "chip")
    return jax.shard_map(
        functools.partial(body, mesh),
        mesh=mesh,
        in_specs=(
            P(split, None),
            P(split, None),
            P(split, None),
            P(split, None, None),
            P(split, None, None),
            P(split, None),
            P(split, None),
            P(split, None, None),
            P(split),
            P(),
            P(),
            P(),
        ),
        out_specs=P(split, None),
        check_vma=False,
    )
```

```python
import functools

import jax
import jax.numpy as jnp
from jax import lax
from jax.experimental import pallas as pl
from jax.experimental.pallas import tpu as pltpu
from jax.sharding import PartitionSpec as P

BF16 = jnp.bfloat16
F32 = jnp.float32
I32 = jnp.int32
BLOCK = 128
VMEM_BYTES = 32 << 20
BATCH = 4
PARTS = 4
PAIR = 2


def dot(left, right):
    return jnp.dot(left, right, preferred_element_type=F32)


def dot_last(left, right):
    return lax.dot_general(left, right, (((1,), (1,)), ((), ())), preferred_element_type=F32)


def rows_hot(index_row, height):
    shape = (height, index_row.shape[1])
    index = jnp.broadcast_to(index_row, shape).astype(jnp.int16)
    return jnp.where(
        index == lax.broadcasted_iota(jnp.int16, shape, 0), jnp.ones((), BF16), jnp.zeros((), BF16)
    )


def silu_of_half(half):
    return half + half * jnp.tanh(half)


def halved(weight):
    return weight * jnp.asarray(0.5, BF16)


class Grid:
    def __init__(self, mesh, halo_capacity, pool_capacity, coarse_capacity, coarse_blocks, slot_count):
        self.dom_count = mesh.shape["dom"]
        self.sub_count = mesh.shape["sub"]
        self.chip_count = mesh.shape["chip"]
        self.places = self.sub_count * self.chip_count
        self.mirrored = self.dom_count == 4
        self.steps = (2, 3, 1) if self.mirrored else (1, self.dom_count - 1, 2)
        self.owners = len(range(0, self.places, 4))
        self.swapped = self.sub_count == 2 and self.chip_count == 2
        self.halo_capacity = halo_capacity
        self.pool_capacity = pool_capacity
        self.coarse_capacity = coarse_capacity
        self.blocks = coarse_blocks
        self.pieces = slot_count // BLOCK
        self.slots = self.places * pool_capacity
        self.pooled_rows = self.owners * pool_capacity
        self.list_rows = 2 * coarse_blocks * self.pieces + self.dom_count
        self.packed_rows = -(-self.list_rows // 16) * 16
        self.packet = self.pooled_rows + 2 * self.packed_rows

    def partner(self, dom, step):
        return dom ^ step if self.mirrored else (dom + step) % self.dom_count

    def partner_here(self, step):
        own = lax.axis_index("dom")
        return own ^ step if self.mirrored else lax.rem(own + step, self.dom_count)

    def halo_place(self, source_dom):
        own = lax.axis_index("dom")
        if self.mirrored:
            step = source_dom ^ own
        else:
            step = own - source_dom
            step = jnp.where(step < 0, step + self.dom_count, step)
        place = jnp.zeros_like(step)
        for index, value in enumerate(self.steps):
            place = jnp.where(step == value, index, place)
        return place

    def own_place(self):
        return lax.axis_index("sub") * self.chip_count + lax.axis_index("chip")

    def slot_order(self, slots, place):
        return slots ^ (place * self.pool_capacity) if self.swapped else slots


def turned(weight):
    return halved(weight).T


def send_kernel(grid, latent_hbm, lists_hbm, weights_hbm, *rest):
    sent_refs = rest[: len(grid.steps)]
    latent_ref, lists_ref, weight_ref, arrived = rest[len(grid.steps) :]
    node_count = latent_ref.shape[0]
    part = node_count // PARTS
    copies = [
        pltpu.make_async_copy(lists_hbm.at[0], lists_ref, arrived.at[0]),
        pltpu.make_async_copy(weights_hbm.at[0, 0], weight_ref, arrived.at[1]),
    ]
    for index in range(PARTS):
        rows = pl.ds(index * part, part)
        copies.append(pltpu.make_async_copy(latent_hbm.at[rows], latent_ref.at[rows], arrived.at[2 + index]))
    for copy in copies:
        copy.start()
    copies[0].wait()
    copies[1].wait()
    weight = turned(weight_ref[...])
    tables = []
    for index in range(PARTS):
        copies[2 + index].wait()
        tables.append(latent_ref[index * part : (index + 1) * part, :].T)
    table = jnp.concatenate(tables, axis=1)
    for step, out_ref in zip(grid.steps, sent_refs):
        index_row = lists_ref[pl.ds(grid.partner_here(step), 1), :]
        picked = dot(table, rows_hot(index_row, table.shape[1])).astype(BF16)
        out_ref[...] = dot(weight, picked).astype(BF16)


def far_rows(source_ref, place_ref, batch):
    local_count = source_ref.shape[1] * 3 // 4
    sources, places = [], []
    for index in range(BATCH):
        row = slice(batch * BATCH + index, batch * BATCH + index + 1)
        sources.append(source_ref[row, local_count:])
        place = place_ref[row, local_count:]
        places.append(jnp.where(place >= 0, place + index * BLOCK, -1))
    return jnp.concatenate(sources, axis=1), jnp.concatenate(places, axis=1)


def near_edges(table, source_ref, place_ref, places_ref, weights_ref, layer, aimed_ref, sums_ref, terms_ref):
    features, node_count = table.shape
    block_count, slot_count = source_ref.shape
    local_count = slot_count * 3 // 4
    window = min(3 * BLOCK, node_count)
    both = jnp.concatenate([turned(weights_ref[layer, 0]), turned(weights_ref[layer, 1])], axis=0)
    terms_ref[...] = dot(both, table).astype(BF16)

    def far_targets(batch):
        columns = slice(batch * BATCH * BLOCK, (batch + 1) * BATCH * BLOCK)
        hot = rows_hot(places_ref[batch : batch + 1, :], BATCH * BLOCK)
        aimed_ref[:, batch * hot.shape[1] : (batch + 1) * hot.shape[1]] = dot(
            terms_ref[features:, columns], hot
        ).astype(BF16)

    def messages(block):
        start = min(max(block * BLOCK - BLOCK, 0), node_count - window)
        terms = jnp.concatenate(
            [
                terms_ref[:features, start : start + window],
                terms_ref[features:, block * BLOCK : (block + 1) * BLOCK],
            ],
            axis=1,
        )
        places = rows_hot(place_ref[block : block + 1, :local_count], BLOCK)
        sources = rows_hot(source_ref[block : block + 1, :local_count] - start, window)
        picked = dot(terms, jnp.concatenate([sources, places], axis=0))
        return silu_of_half(picked).astype(BF16)

    def add_up(block, message):
        places = rows_hot(place_ref[block : block + 1, :local_count], BLOCK)
        sums_ref[:, block * BLOCK : (block + 1) * BLOCK] = dot_last(message, places)

    waiting = None
    for block in range(block_count):
        message = messages(block)
        if waiting is not None:
            add_up(*waiting)
        waiting = (block, message)
        if block % BATCH == 0:
            far_targets(block // BATCH)
    add_up(*waiting)


def near_kernel(
    grid,
    latent_ref,
    source_ref,
    place_ref,
    weights_ref,
    coarse_source_ref,
    coarse_place_ref,
    coarse_send_ref,
    table_ref,
    sources_ref,
    places_ref,
    aimed_ref,
    sums_ref,
    packed_ref,
    terms_ref,
):
    table = latent_ref[...].T
    table_ref[...] = table
    halo_capacity = grid.halo_capacity
    for batch in range(source_ref.shape[0] // BATCH):
        sources, places = far_rows(source_ref, place_ref, batch)
        slots = sources - table.shape[1]
        source_dom = lax.shift_right_logical(slots, halo_capacity.bit_length() - 1)
        sources_ref[batch : batch + 1, :] = grid.halo_place(source_dom) * halo_capacity + (
            slots & (halo_capacity - 1)
        )
        places_ref[batch : batch + 1, :] = places
    near_edges(table, source_ref, place_ref, places_ref, weights_ref, 0, aimed_ref, sums_ref, terms_ref)

    pieces = lane_rows(coarse_source_ref) + [coarse_send_ref[0]] + lane_rows(coarse_place_ref)
    spare = grid.packed_rows - grid.list_rows
    if spare:
        pieces.append(jnp.zeros((spare, BLOCK), I32))
    whole = jnp.concatenate(pieces, axis=0) + 1
    high = lax.shift_right_logical(whole, 8)
    packed_ref[...] = jnp.concatenate([high.astype(F32), (whole & 255).astype(F32)], axis=0).astype(BF16)


def far_edges(layer, table_ref, aimed_ref, sources_ref, places_ref, sums_ref, weights_ref, halo_refs, both_ref, write):
    features, node_count = table_ref.shape
    batch_count, slot_count = sources_ref.shape
    halo = jnp.concatenate([ref[...] for ref in halo_refs], axis=1)
    update_weights = jnp.concatenate([turned(weights_ref[layer, 2]), turned(weights_ref[layer, 3])], axis=1)
    pair_slots = slot_count * PAIR // BATCH
    pair_rows = PAIR * BLOCK
    batch_rows = BATCH * BLOCK
    both_ref[features:, :] = table_ref[...]

    def messages(batch):
        aimed = aimed_ref[:, batch * slot_count : (batch + 1) * slot_count].astype(F32)
        hot = rows_hot(sources_ref[batch : batch + 1, :], halo.shape[1])
        return silu_of_half(dot(halo, hot) + aimed).astype(BF16)

    def add_up(batch, message):
        for pair in range(BATCH // PAIR):
            slots = slice(pair * pair_slots, (pair + 1) * pair_slots)
            first = batch * batch_rows + pair * pair_rows
            columns = slice(first, first + pair_rows)
            hot = rows_hot(places_ref[batch : batch + 1, slots] - pair * pair_rows, pair_rows)
            both_ref[:features, columns] = (sums_ref[:, columns] + dot_last(message[:, slots], hot)).astype(BF16)

    def update(batch):
        columns = slice(batch * batch_rows, (batch + 1) * batch_rows)
        change = silu_of_half(dot(update_weights, both_ref[:, columns]))
        write(columns, (both_ref[features:, columns].astype(F32) + change).astype(BF16))

    message = messages(0)
    for batch in range(batch_count):
        following = messages(batch + 1) if batch + 1 < batch_count else None
        add_up(batch, message)
        if batch:
            update(batch - 1)
        message = following
    update(batch_count - 1)


def lane_rows(ref):
    pieces = []
    for block in range(ref.shape[0]):
        for start in range(0, ref.shape[1], BLOCK):
            pieces.append(ref[block : block + 1, start : start + BLOCK])
    return pieces


def far_pool_kernel(
    grid, table_ref, aimed_ref, sources_ref, places_ref, sums_ref, weights_ref, pool_ref, packed_ref, *rest
):
    halo_refs, (first_ref, packet_ref, both_ref) = rest[:-3], rest[-3:]

    def write(columns, value):
        first_ref[:, columns] = value

    packet_ref[grid.pooled_rows :, :] = packed_ref[...]
    far_edges(0, table_ref, aimed_ref, sources_ref, places_ref, sums_ref, weights_ref, halo_refs, both_ref, write)
    for owner in range(grid.owners):
        hot = rows_hot(pool_ref[0, 4 * owner : 4 * owner + 1, :], first_ref.shape[1])
        pooled = dot(first_ref[...], hot).astype(BF16).T
        packet_ref[owner * grid.pool_capacity : (owner + 1) * grid.pool_capacity, :] = pooled


def far_kernel(table_ref, aimed_ref, sources_ref, places_ref, sums_ref, weights_ref, *rest):
    halo_refs, (out_hbm, both_ref, rows_ref, written) = rest[:-4], rest[-4:]
    copies = []

    def write(columns, value):
        rows_ref[columns, :] = value.T
        rows = pl.ds(columns.start, columns.stop - columns.start)
        copies.append(pltpu.make_async_copy(rows_ref.at[rows], out_hbm.at[rows], written.at[len(copies)]))
        copies[-1].start()

    far_edges(1, table_ref, aimed_ref, sources_ref, places_ref, sums_ref, weights_ref, halo_refs, both_ref, write)
    for copy in copies:
        copy.wait()


def ahead_kernel(grid, first_ref, prolong_ref, lists_ref, out_ref):
    indices = prolong_ref[...]
    shift = (4 * grid.pool_capacity).bit_length() - 1
    indices = lax.shift_right_logical(indices, shift) * grid.pool_capacity + (indices & (grid.pool_capacity - 1))
    indices = indices.astype(F32)
    row = jnp.concatenate([indices[block : block + 1, :] for block in range(indices.shape[0])], axis=1)
    extra = jnp.concatenate([row, jnp.zeros((15, row.shape[1]), F32)], axis=0).astype(BF16)
    table = jnp.concatenate([first_ref[...], extra], axis=0)
    capacity = lists_ref.shape[2]
    for index, step in enumerate(grid.steps):
        index_row = lists_ref[0, pl.ds(grid.partner_here(step), 1), :]
        picked = dot(table, rows_hot(index_row, table.shape[1]))
        out_ref[:, index * capacity : (index + 1) * capacity] = picked.astype(BF16)


def owner_lists(grid, packets, owner, place):
    if grid.swapped:
        rows = packets[0][grid.pooled_rows :, :].astype(F32)
        for other in range(1, grid.places):
            rows = jnp.where(place == other, packets[other][grid.pooled_rows :, :].astype(F32), rows)
    else:
        rows = packets[4 * owner][grid.pooled_rows :, :].astype(F32)
    whole = rows[: grid.packed_rows] * 256.0 + rows[grid.packed_rows :]
    return whole.astype(I32) - 1


def owner_table(grid, packets, owner):
    start = owner * grid.pool_capacity
    return jnp.concatenate([packet[start : start + grid.pool_capacity, :] for packet in packets], axis=0)


def coarse_send_kernel(grid, weights_ref, *refs):
    packets = refs[: grid.places]
    outs = refs[grid.places : grid.places + len(grid.steps)]
    lists_ref = refs[-1]
    place = grid.own_place()
    first_list = grid.blocks * grid.pieces
    for owner in range(grid.owners):
        lists_ref[...] = owner_lists(grid, packets, owner, place)
        table = owner_table(grid, packets, owner)
        terms = dot(table, halved(weights_ref[0])).astype(BF16).T
        for step, out_ref in zip(grid.steps, outs):
            index_row = grid.slot_order(lists_ref[pl.ds(first_list + grid.partner_here(step), 1), :], place)
            picked = dot(terms, rows_hot(index_row, grid.slots))
            out_ref[owner * BLOCK : (owner + 1) * BLOCK, :] = picked.astype(BF16)


def coarse_own_kernel(grid, weights_ref, *refs):
    packets = refs[: grid.places]
    picked_ref, source_out, place_out, rows_out, lists_ref = refs[grid.places :]
    place = grid.own_place()
    first_slot = place * grid.pool_capacity
    block = lax.shift_right_logical(first_slot, BLOCK.bit_length() - 1)
    within = first_slot & (BLOCK - 1)
    shift = grid.coarse_capacity.bit_length() - 1
    for owner in range(grid.owners):
        lists_ref[...] = owner_lists(grid, packets, owner, place)
        sources = jnp.concatenate(
            [lists_ref[pl.ds(block * grid.pieces + piece, 1), :] for piece in range(grid.pieces)], axis=1
        )
        offset = grid.blocks * grid.pieces + grid.dom_count
        places = jnp.concatenate(
            [lists_ref[pl.ds(offset + block * grid.pieces + piece, 1), :] for piece in range(grid.pieces)], axis=1
        )
        places = places - within
        places = jnp.where((places >= 0) & (places < grid.pool_capacity), places, -1)
        halo_slots = sources - grid.slots
        source_dom = lax.shift_right_arithmetic(halo_slots, shift)
        halo_sources = grid.halo_place(source_dom) * grid.coarse_capacity + (halo_slots & (grid.coarse_capacity - 1))
        is_halo = halo_slots >= 0
        source_out[owner : owner + 1, :] = jnp.where(is_halo, halo_sources, -1)
        place_out[owner : owner + 1, :] = places
        own_sources = jnp.where(is_halo, -1, grid.slot_order(sources, place))

        table = owner_table(grid, packets, owner)
        rows = table[: grid.pool_capacity]
        if not grid.swapped:
            for other in range(1, grid.places):
                other_rows = table[other * grid.pool_capacity : (other + 1) * grid.pool_capacity]
                rows = jnp.where(place == other, other_rows, rows)
        rows_out[owner] = rows.T
        sender = dot(table, halved(weights_ref[0])).astype(BF16).T
        target = dot(rows, halved(weights_ref[1])).astype(BF16).T
        hot = jnp.concatenate([rows_hot(own_sources, grid.slots), rows_hot(places, grid.pool_capacity)], axis=0)
        picked_ref[owner] = dot(jnp.concatenate([sender, target], axis=1), hot)


def lift(table, prolonged, index_row):
    pooled_rows = prolonged.shape[1] // 2
    hot = rows_hot(index_row, pooled_rows)
    hot = jnp.concatenate([hot, hot], axis=0)
    return (table.astype(F32) + silu_of_half(dot(prolonged, hot))).astype(BF16)


def lift_halo_kernel(
    grid,
    picked_ref,
    source_ref,
    place_ref,
    rows_ref,
    ahead_ref,
    coarse_weights_ref,
    prolong_weight_ref,
    weights_ref,
    *rest,
):
    count = len(grid.steps)
    halo_refs, prolonged_ref, sent_refs = rest[:count], rest[count], rest[count + 1 :]
    features = rows_ref.shape[1]
    update_weights = jnp.concatenate([turned(coarse_weights_ref[2]), turned(coarse_weights_ref[3])], axis=1)
    prolong_weight = turned(prolong_weight_ref[...])
    prolonged = []
    for owner in range(grid.owners):
        halo = jnp.concatenate([ref[owner * BLOCK : (owner + 1) * BLOCK, :] for ref in halo_refs], axis=1)
        picked = picked_ref[owner] + dot(halo, rows_hot(source_ref[owner : owner + 1, :], halo.shape[1]))
        message = silu_of_half(picked).astype(BF16)
        places = rows_hot(place_ref[owner : owner + 1, :], grid.pool_capacity)
        summed = dot_last(message, places).astype(BF16)
        rows = rows_ref[owner]
        update = dot(update_weights, jnp.concatenate([summed, rows], axis=0))
        coarse = (rows.astype(F32) + silu_of_half(update)).astype(BF16)
        prolonged.append(dot(prolong_weight, coarse))
    prolonged = jnp.concatenate(prolonged, axis=1)
    high = prolonged.astype(BF16)
    low = (prolonged - high.astype(F32)).astype(BF16)
    parts = jnp.concatenate([high, low], axis=1)
    prolonged_ref[...] = parts
    weight = turned(weights_ref[1, 0])
    index_row = ahead_ref[features : features + 1, :].astype(F32).astype(I32)
    lifted = lift(ahead_ref[:features, :], parts, index_row)
    terms = dot(weight, lifted).astype(BF16)
    capacity = sent_refs[0].shape[1]
    for index, out_ref in enumerate(sent_refs):
        out_ref[...] = terms[:, index * capacity : (index + 1) * capacity]


def lift_near_kernel(
    grid,
    first_ref,
    prolonged_ref,
    prolong_ref,
    source_ref,
    place_ref,
    places_ref,
    weights_ref,
    lifted_ref,
    aimed_ref,
    sums_ref,
    terms_ref,
):
    indices = prolong_ref[...]
    shift = (4 * grid.pool_capacity).bit_length() - 1
    indices = lax.shift_right_logical(indices, shift) * grid.pool_capacity + (indices & (grid.pool_capacity - 1))
    row = jnp.concatenate([indices[block : block + 1, :] for block in range(indices.shape[0])], axis=1)
    lifted = lift(first_ref[...], prolonged_ref[...], row)
    lifted_ref[...] = lifted
    near_edges(lifted, source_ref, place_ref, places_ref, weights_ref, 1, aimed_ref, sums_ref, terms_ref)


def call(kernel, outs, scratch=(), flops=0, name=None, limit=VMEM_BYTES, **specs):
    return pl.pallas_call(
        kernel,
        out_shape=tuple(jax.ShapeDtypeStruct(shape, dtype) for shape, dtype in outs),
        scratch_shapes=list(scratch),
        compiler_params=pltpu.CompilerParams(vmem_limit_bytes=limit),
        cost_estimate=pl.CostEstimate(flops=flops, bytes_accessed=4 << 20, transcendentals=0),
        name=name,
        **specs,
    )


def swap_dom(grid, arrays, order=(0, 1, 2)):
    arrived = {}
    for index in order:
        step = grid.steps[index]
        arrived[index] = lax.ppermute(
            arrays[index], "dom", [(dom, grid.partner(dom, step)) for dom in range(grid.dom_count)]
        )
    return [arrived[index] for index in range(len(arrays))]


def trade_packets(grid, packet):
    if grid.swapped:
        pairs = [(0, 1), (1, 0)]
        over = lax.ppermute(packet, "sub", pairs)
        across = lax.ppermute(packet, "chip", pairs)
        both = lax.ppermute(packet, ("sub", "chip"), [(0, 3), (1, 2), (2, 1), (3, 0)])
        return [packet, across, over, both]
    gathered = lax.all_gather(packet, ("sub", "chip"), axis=0, tiled=False)
    return [gathered[place] for place in range(grid.places)]


def body(
    mesh,
    fine_nodes,
    fine_src,
    fine_dst,
    halo_send,
    pool_send,
    coarse_src,
    coarse_dst,
    coarse_send,
    prolong_idx,
    fine_weights,
    coarse_weights,
    prolong_weight,
):
    node_count, features = fine_nodes.shape
    halo_capacity = halo_send.shape[2]
    coarse_blocks, coarse_slots = coarse_src.shape
    grid = Grid(mesh, halo_capacity, pool_send.shape[2], coarse_send.shape[2], coarse_blocks, coarse_slots)
    steps = len(grid.steps)
    block_count, slot_count = fine_src.shape
    far_count = slot_count - slot_count * 3 // 4
    table = ((features, node_count), BF16)
    sums_table = ((features, node_count), F32)
    aimed_table = ((features, block_count * far_count), BF16)
    far_lists = ((block_count // BATCH, BATCH * far_count), I32)
    halo_outs = [((features, halo_capacity), BF16)] * steps
    two_tables = pltpu.VMEM((2 * features, node_count), BF16)
    prolong_rows = prolong_idx.reshape(node_count // BLOCK, BLOCK)
    big = 1 << 30
    in_hbm = pl.BlockSpec(memory_space=pltpu.HBM)

    sent = call(
        functools.partial(send_kernel, grid),
        halo_outs,
        [
            pltpu.VMEM((node_count, features), BF16),
            pltpu.VMEM(halo_send.shape[1:], I32),
            pltpu.VMEM((features, features), BF16),
            pltpu.SemaphoreType.DMA((2 + PARTS,)),
        ],
        flops=big,
        name="send",
        limit=63 << 20,
        in_specs=[in_hbm] * 3,
    )(fine_nodes, halo_send, fine_weights)
    halo = swap_dom(grid, sent)
    nodes, far_sources, far_places, aimed, sums, packed = call(
        functools.partial(near_kernel, grid),
        [table, far_lists, far_lists, aimed_table, sums_table, ((2 * grid.packed_rows, features), BF16)],
        [two_tables],
        flops=4 * big,
        name="near",
    )(fine_nodes, fine_src, fine_dst, fine_weights, coarse_src, coarse_dst, coarse_send)
    first, packet = call(
        functools.partial(far_pool_kernel, grid),
        [table, ((grid.packet, features), BF16)],
        [two_tables],
        flops=2 * big,
        name="far_pool",
    )(nodes, aimed, far_sources, far_places, sums, fine_weights, pool_send, packed, *halo)
    packets = trade_packets(grid, packet)
    (ahead,) = call(
        functools.partial(ahead_kernel, grid), [((features + 16, steps * halo_capacity), BF16)], flops=big, name="ahead"
    )(first, prolong_rows, halo_send)
    lists_scratch = pltpu.VMEM((grid.packed_rows, BLOCK), I32)
    sent = call(
        functools.partial(coarse_send_kernel, grid),
        [((grid.owners * features, grid.coarse_capacity), BF16)] * steps,
        [lists_scratch],
        flops=big // 2,
        name="coarse_send",
    )(coarse_weights, *packets)
    coarse_halo = swap_dom(grid, sent)
    picked, sources, places, rows = call(
        functools.partial(coarse_own_kernel, grid),
        [
            ((grid.owners, features, coarse_slots), F32),
            ((grid.owners, coarse_slots), I32),
            ((grid.owners, coarse_slots), I32),
            ((grid.owners, features, grid.pool_capacity), BF16),
        ],
        [lists_scratch],
        flops=4 * big,
        name="coarse_own",
    )(coarse_weights, *packets)
    prolonged, *sent = call(
        functools.partial(lift_halo_kernel, grid),
        [((features, 2 * grid.pooled_rows), BF16), *halo_outs],
        flops=big,
        name="lift_halo",
    )(picked, sources, places, rows, ahead, coarse_weights, prolong_weight, fine_weights, *coarse_halo)
    halo = swap_dom(grid, sent)
    lifted, aimed, sums = call(
        functools.partial(lift_near_kernel, grid),
        [table, aimed_table, sums_table],
        [two_tables],
        flops=4 * big,
        name="lift_near",
    )(first, prolonged, prolong_rows, fine_src, fine_dst, far_places, fine_weights)
    (fine_out,) = call(
        far_kernel,
        [((node_count, features), BF16)],
        [
            two_tables,
            pltpu.VMEM((node_count, features), BF16),
            pltpu.SemaphoreType.DMA((block_count // BATCH,)),
        ],
        flops=2 * big,
        name="far",
        out_specs=(pl.BlockSpec(memory_space=pltpu.HBM),),
    )(lifted, aimed, far_sources, far_places, sums, fine_weights, *halo)
    return fine_out


def solution(mesh):
    split = ("groups", "dom", "sub", "chip")
    return jax.shard_map(
        functools.partial(body, mesh),
        mesh=mesh,
        in_specs=(
            P(split, None),
            P(split, None),
            P(split, None),
            P(split, None, None),
            P(split, None, None),
            P(split, None),
            P(split, None),
            P(split, None, None),
            P(split),
            P(),
            P(),
            P(),
        ),
        out_specs=P(split, None),
        check_vma=False,
    )
```

```python
import functools

import jax
import jax.numpy as jnp
from jax import lax
from jax.experimental import pallas as pl
from jax.experimental.pallas import tpu as pltpu
from jax.sharding import PartitionSpec as P

BF16 = jnp.bfloat16
F32 = jnp.float32
I32 = jnp.int32
BLOCK = 128
VMEM_BYTES = 32 << 20
BATCH = 4
PARTS = 4
PAIR = 2


def dot(left, right):
    return jnp.dot(left, right, preferred_element_type=F32)


def dot_last(left, right):
    return lax.dot_general(left, right, (((1,), (1,)), ((), ())), preferred_element_type=F32)


def rows_hot(index_row, height):
    shape = (height, index_row.shape[1])
    index = jnp.broadcast_to(index_row, shape).astype(jnp.int16)
    return jnp.where(
        index == lax.broadcasted_iota(jnp.int16, shape, 0), jnp.ones((), BF16), jnp.zeros((), BF16)
    )


def silu_of_half(half):
    return half + half * jnp.tanh(half)


def halved(weight):
    return weight * jnp.asarray(0.5, BF16)


class Grid:
    def __init__(self, mesh, halo_capacity, pool_capacity, coarse_capacity, coarse_blocks, slot_count):
        self.dom_count = mesh.shape["dom"]
        self.sub_count = mesh.shape["sub"]
        self.chip_count = mesh.shape["chip"]
        self.places = self.sub_count * self.chip_count
        self.mirrored = self.dom_count == 4
        self.steps = (2, 3, 1) if self.mirrored else (1, self.dom_count - 1, 2)
        self.owners = len(range(0, self.places, 4))
        self.swapped = self.sub_count == 2 and self.chip_count == 2
        self.halo_capacity = halo_capacity
        self.pool_capacity = pool_capacity
        self.coarse_capacity = coarse_capacity
        self.blocks = coarse_blocks
        self.pieces = slot_count // BLOCK
        self.slots = self.places * pool_capacity
        self.pooled_rows = self.owners * pool_capacity
        self.list_rows = 2 * coarse_blocks * self.pieces + self.dom_count
        self.packed_rows = -(-self.list_rows // 16) * 16
        self.packet = self.pooled_rows + 2 * self.packed_rows

    def partner(self, dom, step):
        return dom ^ step if self.mirrored else (dom + step) % self.dom_count

    def partner_here(self, step):
        own = lax.axis_index("dom")
        return own ^ step if self.mirrored else lax.rem(own + step, self.dom_count)

    def halo_place(self, source_dom):
        own = lax.axis_index("dom")
        if self.mirrored:
            step = source_dom ^ own
        else:
            step = own - source_dom
            step = jnp.where(step < 0, step + self.dom_count, step)
        place = jnp.zeros_like(step)
        for index, value in enumerate(self.steps):
            place = jnp.where(step == value, index, place)
        return place

    def own_place(self):
        return lax.axis_index("sub") * self.chip_count + lax.axis_index("chip")

    def slot_order(self, slots, place):
        return slots ^ (place * self.pool_capacity) if self.swapped else slots


def turned(weight):
    return halved(weight).T


def send_kernel(grid, latent_hbm, lists_hbm, weights_hbm, *rest):
    sent_refs = rest[: len(grid.steps)]
    latent_ref, lists_ref, weight_ref, arrived = rest[len(grid.steps) :]
    node_count = latent_ref.shape[0]
    part = node_count // PARTS
    copies = [
        pltpu.make_async_copy(lists_hbm.at[0], lists_ref, arrived.at[0]),
        pltpu.make_async_copy(weights_hbm.at[0, 0], weight_ref, arrived.at[1]),
    ]
    for index in range(PARTS):
        rows = pl.ds(index * part, part)
        copies.append(pltpu.make_async_copy(latent_hbm.at[rows], latent_ref.at[rows], arrived.at[2 + index]))
    for copy in copies:
        copy.start()
    copies[0].wait()
    copies[1].wait()
    weight = turned(weight_ref[...])
    tables = []
    for index in range(PARTS):
        copies[2 + index].wait()
        tables.append(latent_ref[index * part : (index + 1) * part, :].T)
    table = jnp.concatenate(tables, axis=1)
    index_row = jnp.concatenate(
        [lists_ref[pl.ds(grid.partner_here(step), 1), :] for step in grid.steps], axis=1
    )
    picked = dot(table, rows_hot(index_row, node_count)).astype(BF16)
    terms = dot(weight, picked).astype(BF16)
    capacity = lists_ref.shape[1]
    for index, out_ref in enumerate(sent_refs):
        out_ref[...] = terms[:, index * capacity : (index + 1) * capacity]


def far_rows(source_ref, place_ref, batch):
    local_count = source_ref.shape[1] * 3 // 4
    sources, places = [], []
    for index in range(BATCH):
        row = slice(batch * BATCH + index, batch * BATCH + index + 1)
        sources.append(source_ref[row, local_count:])
        place = place_ref[row, local_count:]
        places.append(jnp.where(place >= 0, place + index * BLOCK, -1))
    return jnp.concatenate(sources, axis=1), jnp.concatenate(places, axis=1)


def near_edges(table, source_ref, place_ref, places_ref, weights_ref, layer, aimed_ref, sums_ref, terms_ref):
    features, node_count = table.shape
    block_count, slot_count = source_ref.shape
    local_count = slot_count * 3 // 4
    window = min(3 * BLOCK, node_count)
    both = jnp.concatenate([turned(weights_ref[layer, 0]), turned(weights_ref[layer, 1])], axis=0)
    terms_ref[...] = dot(both, table).astype(BF16)

    def far_targets(batch):
        columns = slice(batch * BATCH * BLOCK, (batch + 1) * BATCH * BLOCK)
        hot = rows_hot(places_ref[batch : batch + 1, :], BATCH * BLOCK)
        aimed_ref[:, batch * hot.shape[1] : (batch + 1) * hot.shape[1]] = dot(
            terms_ref[features:, columns], hot
        ).astype(BF16)

    def messages(block):
        start = min(max(block * BLOCK - BLOCK, 0), node_count - window)
        terms = jnp.concatenate(
            [
                terms_ref[:features, start : start + window],
                terms_ref[features:, block * BLOCK : (block + 1) * BLOCK],
            ],
            axis=1,
        )
        places = rows_hot(place_ref[block : block + 1, :local_count], BLOCK)
        sources = rows_hot(source_ref[block : block + 1, :local_count] - start, window)
        picked = dot(terms, jnp.concatenate([sources, places], axis=0))
        return silu_of_half(picked).astype(BF16)

    def add_up(block, message):
        places = rows_hot(place_ref[block : block + 1, :local_count], BLOCK)
        sums_ref[:, block * BLOCK : (block + 1) * BLOCK] = dot_last(message, places)

    waiting = None
    for block in range(block_count):
        message = messages(block)
        if waiting is not None:
            add_up(*waiting)
        waiting = (block, message)
        if block % BATCH == 0:
            far_targets(block // BATCH)
    add_up(*waiting)


def near_kernel(
    grid,
    latent_ref,
    source_ref,
    place_ref,
    weights_ref,
    coarse_source_ref,
    coarse_place_ref,
    coarse_send_ref,
    pool_ref,
    table_ref,
    sources_ref,
    places_ref,
    aimed_ref,
    sums_ref,
    packed_ref,
    pooled_ref,
    terms_ref,
):
    table = latent_ref[...].T
    table_ref[...] = table
    halo_capacity = grid.halo_capacity
    for batch in range(source_ref.shape[0] // BATCH):
        sources, places = far_rows(source_ref, place_ref, batch)
        slots = sources - table.shape[1]
        source_dom = lax.shift_right_logical(slots, halo_capacity.bit_length() - 1)
        sources_ref[batch : batch + 1, :] = grid.halo_place(source_dom) * halo_capacity + (
            slots & (halo_capacity - 1)
        )
        places_ref[batch : batch + 1, :] = places
    near_edges(table, source_ref, place_ref, places_ref, weights_ref, 0, aimed_ref, sums_ref, terms_ref)

    pieces = lane_rows(coarse_source_ref) + [coarse_send_ref[0]] + lane_rows(coarse_place_ref)
    spare = grid.packed_rows - grid.list_rows
    if spare:
        pieces.append(jnp.zeros((spare, BLOCK), I32))
    whole = jnp.concatenate(pieces, axis=0) + 1
    high = lax.shift_right_logical(whole, 8)
    packed_ref[...] = jnp.concatenate([high.astype(F32), (whole & 255).astype(F32)], axis=0).astype(BF16)
    for owner in range(grid.owners):
        pooled_ref[owner : owner + 1, :] = pool_ref[0, 4 * owner : 4 * owner + 1, :]


def far_edges(layer, table_ref, aimed_ref, sources_ref, places_ref, sums_ref, weights_ref, halo_refs, both_ref, write):
    features, node_count = table_ref.shape
    batch_count, slot_count = sources_ref.shape
    halo = jnp.concatenate([ref[...] for ref in halo_refs], axis=1)
    update_weights = jnp.concatenate([turned(weights_ref[layer, 2]), turned(weights_ref[layer, 3])], axis=1)
    pair_slots = slot_count * PAIR // BATCH
    pair_rows = PAIR * BLOCK
    batch_rows = BATCH * BLOCK
    both_ref[features:, :] = table_ref[...]

    def messages(batch):
        aimed = aimed_ref[:, batch * slot_count : (batch + 1) * slot_count].astype(F32)
        hot = rows_hot(sources_ref[batch : batch + 1, :], halo.shape[1])
        return silu_of_half(dot(halo, hot) + aimed).astype(BF16)

    def add_up(batch, message):
        for pair in range(BATCH // PAIR):
            slots = slice(pair * pair_slots, (pair + 1) * pair_slots)
            first = batch * batch_rows + pair * pair_rows
            columns = slice(first, first + pair_rows)
            hot = rows_hot(places_ref[batch : batch + 1, slots] - pair * pair_rows, pair_rows)
            both_ref[:features, columns] = (sums_ref[:, columns] + dot_last(message[:, slots], hot)).astype(BF16)

    def update(batch):
        columns = slice(batch * batch_rows, (batch + 1) * batch_rows)
        change = silu_of_half(dot(update_weights, both_ref[:, columns]))
        write(columns, (both_ref[features:, columns].astype(F32) + change).astype(BF16))

    message = messages(0)
    for batch in range(batch_count):
        following = messages(batch + 1) if batch + 1 < batch_count else None
        add_up(batch, message)
        if batch:
            update(batch - 1)
        message = following
    update(batch_count - 1)


def lane_rows(ref):
    pieces = []
    for block in range(ref.shape[0]):
        for start in range(0, ref.shape[1], BLOCK):
            pieces.append(ref[block : block + 1, start : start + BLOCK])
    return pieces


def far_pool_kernel(
    grid, table_ref, aimed_ref, sources_ref, places_ref, sums_ref, weights_ref, pool_ref, packed_ref, *rest
):
    halo_refs, (first_ref, packet_ref, both_ref) = rest[:-3], rest[-3:]

    def write(columns, value):
        first_ref[:, columns] = value

    packet_ref[grid.pooled_rows :, :] = packed_ref[...]
    far_edges(0, table_ref, aimed_ref, sources_ref, places_ref, sums_ref, weights_ref, halo_refs, both_ref, write)
    for owner in range(grid.owners):
        hot = rows_hot(pool_ref[owner : owner + 1, :], first_ref.shape[1])
        pooled = dot(first_ref[...], hot).astype(BF16).T
        packet_ref[owner * grid.pool_capacity : (owner + 1) * grid.pool_capacity, :] = pooled


def far_kernel(table_ref, aimed_ref, sources_ref, places_ref, sums_ref, weights_ref, *rest):
    halo_refs, (out_hbm, both_ref, rows_ref, written) = rest[:-4], rest[-4:]
    copies = []

    def write(columns, value):
        rows_ref[columns, :] = value.T
        rows = pl.ds(columns.start, columns.stop - columns.start)
        copies.append(pltpu.make_async_copy(rows_ref.at[rows], out_hbm.at[rows], written.at[len(copies)]))
        copies[-1].start()

    far_edges(1, table_ref, aimed_ref, sources_ref, places_ref, sums_ref, weights_ref, halo_refs, both_ref, write)
    for copy in copies:
        copy.wait()


def ahead_kernel(grid, first_ref, prolong_ref, lists_ref, out_ref):
    indices = prolong_ref[...]
    shift = (4 * grid.pool_capacity).bit_length() - 1
    indices = lax.shift_right_logical(indices, shift) * grid.pool_capacity + (indices & (grid.pool_capacity - 1))
    indices = indices.astype(F32)
    row = jnp.concatenate([indices[block : block + 1, :] for block in range(indices.shape[0])], axis=1)
    extra = jnp.concatenate([row, jnp.zeros((15, row.shape[1]), F32)], axis=0).astype(BF16)
    table = jnp.concatenate([first_ref[...], extra], axis=0)
    capacity = lists_ref.shape[2]
    for index, step in enumerate(grid.steps):
        index_row = lists_ref[0, pl.ds(grid.partner_here(step), 1), :]
        picked = dot(table, rows_hot(index_row, table.shape[1]))
        out_ref[:, index * capacity : (index + 1) * capacity] = picked.astype(BF16)


def owner_lists(grid, packets, owner, place):
    if grid.swapped:
        rows = packets[0][grid.pooled_rows :, :].astype(F32)
        for other in range(1, grid.places):
            rows = jnp.where(place == other, packets[other][grid.pooled_rows :, :].astype(F32), rows)
    else:
        rows = packets[4 * owner][grid.pooled_rows :, :].astype(F32)
    whole = rows[: grid.packed_rows] * 256.0 + rows[grid.packed_rows :]
    return whole.astype(I32) - 1


def owner_table(grid, packets, owner):
    start = owner * grid.pool_capacity
    return jnp.concatenate([packet[start : start + grid.pool_capacity, :] for packet in packets], axis=0)


def coarse_send_kernel(grid, weights_ref, *refs):
    packets = refs[: grid.places]
    outs = refs[grid.places : grid.places + len(grid.steps)]
    lists_ref = refs[-1]
    place = grid.own_place()
    first_list = grid.blocks * grid.pieces
    for owner in range(grid.owners):
        lists_ref[...] = owner_lists(grid, packets, owner, place)
        table = owner_table(grid, packets, owner)
        terms = dot(table, halved(weights_ref[0])).astype(BF16).T
        for step, out_ref in zip(grid.steps, outs):
            index_row = grid.slot_order(lists_ref[pl.ds(first_list + grid.partner_here(step), 1), :], place)
            picked = dot(terms, rows_hot(index_row, grid.slots))
            out_ref[owner * BLOCK : (owner + 1) * BLOCK, :] = picked.astype(BF16)


def coarse_own_kernel(grid, weights_ref, *refs):
    packets = refs[: grid.places]
    picked_ref, source_out, place_out, rows_out, lists_ref = refs[grid.places :]
    place = grid.own_place()
    first_slot = place * grid.pool_capacity
    block = lax.shift_right_logical(first_slot, BLOCK.bit_length() - 1)
    within = first_slot & (BLOCK - 1)
    shift = grid.coarse_capacity.bit_length() - 1
    for owner in range(grid.owners):
        lists_ref[...] = owner_lists(grid, packets, owner, place)
        sources = jnp.concatenate(
            [lists_ref[pl.ds(block * grid.pieces + piece, 1), :] for piece in range(grid.pieces)], axis=1
        )
        offset = grid.blocks * grid.pieces + grid.dom_count
        places = jnp.concatenate(
            [lists_ref[pl.ds(offset + block * grid.pieces + piece, 1), :] for piece in range(grid.pieces)], axis=1
        )
        places = places - within
        places = jnp.where((places >= 0) & (places < grid.pool_capacity), places, -1)
        halo_slots = sources - grid.slots
        source_dom = lax.shift_right_arithmetic(halo_slots, shift)
        halo_sources = grid.halo_place(source_dom) * grid.coarse_capacity + (halo_slots & (grid.coarse_capacity - 1))
        is_halo = halo_slots >= 0
        source_out[owner : owner + 1, :] = jnp.where(is_halo, halo_sources, -1)
        place_out[owner : owner + 1, :] = places
        own_sources = jnp.where(is_halo, -1, grid.slot_order(sources, place))

        table = owner_table(grid, packets, owner)
        rows = table[: grid.pool_capacity]
        if not grid.swapped:
            for other in range(1, grid.places):
                other_rows = table[other * grid.pool_capacity : (other + 1) * grid.pool_capacity]
                rows = jnp.where(place == other, other_rows, rows)
        rows_out[owner] = rows.T
        sender = dot(table, halved(weights_ref[0])).astype(BF16).T
        target = dot(rows, halved(weights_ref[1])).astype(BF16).T
        hot = jnp.concatenate([rows_hot(own_sources, grid.slots), rows_hot(places, grid.pool_capacity)], axis=0)
        picked_ref[owner] = dot(jnp.concatenate([sender, target], axis=1), hot)


def lift(table, prolonged, index_row):
    pooled_rows = prolonged.shape[1] // 2
    hot = rows_hot(index_row, pooled_rows)
    hot = jnp.concatenate([hot, hot], axis=0)
    return (table.astype(F32) + silu_of_half(dot(prolonged, hot))).astype(BF16)


def lift_halo_kernel(
    grid,
    picked_ref,
    source_ref,
    place_ref,
    rows_ref,
    ahead_ref,
    coarse_weights_ref,
    prolong_weight_ref,
    weights_ref,
    *rest,
):
    count = len(grid.steps)
    halo_refs, prolonged_ref, sent_refs = rest[:count], rest[count], rest[count + 1 :]
    features = rows_ref.shape[1]
    update_weights = jnp.concatenate([turned(coarse_weights_ref[2]), turned(coarse_weights_ref[3])], axis=1)
    prolong_weight = turned(prolong_weight_ref[...])
    prolonged = []
    for owner in range(grid.owners):
        halo = jnp.concatenate([ref[owner * BLOCK : (owner + 1) * BLOCK, :] for ref in halo_refs], axis=1)
        picked = picked_ref[owner] + dot(halo, rows_hot(source_ref[owner : owner + 1, :], halo.shape[1]))
        message = silu_of_half(picked).astype(BF16)
        places = rows_hot(place_ref[owner : owner + 1, :], grid.pool_capacity)
        summed = dot_last(message, places).astype(BF16)
        rows = rows_ref[owner]
        update = dot(update_weights, jnp.concatenate([summed, rows], axis=0))
        coarse = (rows.astype(F32) + silu_of_half(update)).astype(BF16)
        prolonged.append(dot(prolong_weight, coarse))
    prolonged = jnp.concatenate(prolonged, axis=1)
    high = prolonged.astype(BF16)
    low = (prolonged - high.astype(F32)).astype(BF16)
    parts = jnp.concatenate([high, low], axis=1)
    prolonged_ref[...] = parts
    weight = turned(weights_ref[1, 0])
    index_row = ahead_ref[features : features + 1, :].astype(F32).astype(I32)
    lifted = lift(ahead_ref[:features, :], parts, index_row)
    terms = dot(weight, lifted).astype(BF16)
    capacity = sent_refs[0].shape[1]
    for index, out_ref in enumerate(sent_refs):
        out_ref[...] = terms[:, index * capacity : (index + 1) * capacity]


def lift_near_kernel(
    grid,
    first_ref,
    prolonged_ref,
    prolong_ref,
    source_ref,
    place_ref,
    places_ref,
    weights_ref,
    lifted_ref,
    aimed_ref,
    sums_ref,
    terms_ref,
):
    indices = prolong_ref[...]
    shift = (4 * grid.pool_capacity).bit_length() - 1
    indices = lax.shift_right_logical(indices, shift) * grid.pool_capacity + (indices & (grid.pool_capacity - 1))
    row = jnp.concatenate([indices[block : block + 1, :] for block in range(indices.shape[0])], axis=1)
    lifted = lift(first_ref[...], prolonged_ref[...], row)
    lifted_ref[...] = lifted
    near_edges(lifted, source_ref, place_ref, places_ref, weights_ref, 1, aimed_ref, sums_ref, terms_ref)


def call(kernel, outs, scratch=(), flops=0, name=None, limit=VMEM_BYTES, **specs):
    return pl.pallas_call(
        kernel,
        out_shape=tuple(jax.ShapeDtypeStruct(shape, dtype) for shape, dtype in outs),
        scratch_shapes=list(scratch),
        compiler_params=pltpu.CompilerParams(vmem_limit_bytes=limit),
        cost_estimate=pl.CostEstimate(flops=flops, bytes_accessed=4 << 20, transcendentals=0),
        name=name,
        **specs,
    )


def swap_dom(grid, arrays, order=(0, 1, 2)):
    arrived = {}
    for index in order:
        step = grid.steps[index]
        arrived[index] = lax.ppermute(
            arrays[index], "dom", [(dom, grid.partner(dom, step)) for dom in range(grid.dom_count)]
        )
    return [arrived[index] for index in range(len(arrays))]


def trade_packets(grid, packet):
    if grid.swapped:
        pairs = [(0, 1), (1, 0)]
        over = lax.ppermute(packet, "sub", pairs)
        across = lax.ppermute(packet, "chip", pairs)
        both = lax.ppermute(packet, ("sub", "chip"), [(0, 3), (1, 2), (2, 1), (3, 0)])
        return [packet, across, over, both]
    gathered = lax.all_gather(packet, ("sub", "chip"), axis=0, tiled=False)
    return [gathered[place] for place in range(grid.places)]


def body(
    mesh,
    fine_nodes,
    fine_src,
    fine_dst,
    halo_send,
    pool_send,
    coarse_src,
    coarse_dst,
    coarse_send,
    prolong_idx,
    fine_weights,
    coarse_weights,
    prolong_weight,
):
    node_count, features = fine_nodes.shape
    halo_capacity = halo_send.shape[2]
    coarse_blocks, coarse_slots = coarse_src.shape
    grid = Grid(mesh, halo_capacity, pool_send.shape[2], coarse_send.shape[2], coarse_blocks, coarse_slots)
    steps = len(grid.steps)
    block_count, slot_count = fine_src.shape
    far_count = slot_count - slot_count * 3 // 4
    table = ((features, node_count), BF16)
    sums_table = ((features, node_count), F32)
    aimed_table = ((features, block_count * far_count), BF16)
    far_lists = ((block_count // BATCH, BATCH * far_count), I32)
    halo_outs = [((features, halo_capacity), BF16)] * steps
    two_tables = pltpu.VMEM((2 * features, node_count), BF16)
    prolong_rows = prolong_idx.reshape(node_count // BLOCK, BLOCK)
    big = 1 << 30
    in_hbm = pl.BlockSpec(memory_space=pltpu.HBM)

    sent = call(
        functools.partial(send_kernel, grid),
        halo_outs,
        [
            pltpu.VMEM((node_count, features), BF16),
            pltpu.VMEM(halo_send.shape[1:], I32),
            pltpu.VMEM((features, features), BF16),
            pltpu.SemaphoreType.DMA((2 + PARTS,)),
        ],
        flops=big,
        name="send",
        limit=63 << 20,
        in_specs=[in_hbm] * 3,
    )(fine_nodes, halo_send, fine_weights)
    halo = swap_dom(grid, sent)
    nodes, far_sources, far_places, aimed, sums, packed, pool_lists = call(
        functools.partial(near_kernel, grid),
        [
            table,
            far_lists,
            far_lists,
            aimed_table,
            sums_table,
            ((2 * grid.packed_rows, features), BF16),
            ((grid.owners, grid.pool_capacity), I32),
        ],
        [two_tables],
        flops=4 * big,
        name="near",
    )(fine_nodes, fine_src, fine_dst, fine_weights, coarse_src, coarse_dst, coarse_send, pool_send)
    first, packet = call(
        functools.partial(far_pool_kernel, grid),
        [table, ((grid.packet, features), BF16)],
        [two_tables],
        flops=2 * big,
        name="far_pool",
    )(nodes, aimed, far_sources, far_places, sums, fine_weights, pool_lists, packed, *halo)
    packets = trade_packets(grid, packet)
    (ahead,) = call(
        functools.partial(ahead_kernel, grid), [((features + 16, steps * halo_capacity), BF16)], flops=big, name="ahead"
    )(first, prolong_rows, halo_send)
    lists_scratch = pltpu.VMEM((grid.packed_rows, BLOCK), I32)
    sent = call(
        functools.partial(coarse_send_kernel, grid),
        [((grid.owners * features, grid.coarse_capacity), BF16)] * steps,
        [lists_scratch],
        flops=big // 2,
        name="coarse_send",
    )(coarse_weights, *packets)
    coarse_halo = swap_dom(grid, sent)
    picked, sources, places, rows = call(
        functools.partial(coarse_own_kernel, grid),
        [
            ((grid.owners, features, coarse_slots), F32),
            ((grid.owners, coarse_slots), I32),
            ((grid.owners, coarse_slots), I32),
            ((grid.owners, features, grid.pool_capacity), BF16),
        ],
        [lists_scratch],
        flops=4 * big,
        name="coarse_own",
    )(coarse_weights, *packets)
    prolonged, *sent = call(
        functools.partial(lift_halo_kernel, grid),
        [((features, 2 * grid.pooled_rows), BF16), *halo_outs],
        flops=big,
        name="lift_halo",
    )(picked, sources, places, rows, ahead, coarse_weights, prolong_weight, fine_weights, *coarse_halo)
    halo = swap_dom(grid, sent)
    lifted, aimed, sums = call(
        functools.partial(lift_near_kernel, grid),
        [table, aimed_table, sums_table],
        [two_tables],
        flops=4 * big,
        name="lift_near",
    )(first, prolonged, prolong_rows, fine_src, fine_dst, far_places, fine_weights)
    (fine_out,) = call(
        far_kernel,
        [((node_count, features), BF16)],
        [
            two_tables,
            pltpu.VMEM((node_count, features), BF16),
            pltpu.SemaphoreType.DMA((block_count // BATCH,)),
        ],
        flops=2 * big,
        name="far",
        out_specs=(pl.BlockSpec(memory_space=pltpu.HBM),),
    )(lifted, aimed, far_sources, far_places, sums, fine_weights, *halo)
    return fine_out


def solution(mesh):
    split = ("groups", "dom", "sub", "chip")
    return jax.shard_map(
        functools.partial(body, mesh),
        mesh=mesh,
        in_specs=(
            P(split, None),
            P(split, None),
            P(split, None),
            P(split, None, None),
            P(split, None, None),
            P(split, None),
            P(split, None),
            P(split, None, None),
            P(split),
            P(),
            P(),
            P(),
        ),
        out_specs=P(split, None),
        check_vma=False,
    )
```

```python
import functools

import jax
import jax.numpy as jnp
from jax import lax
from jax.experimental import pallas as pl
from jax.experimental.pallas import tpu as pltpu
from jax.sharding import PartitionSpec as P

BF16 = jnp.bfloat16
F32 = jnp.float32
I32 = jnp.int32
BLOCK = 128
VMEM_BYTES = 32 << 20
BATCH = 4
PARTS = 4
PAIR = 2


def dot(left, right):
    return jnp.dot(left, right, preferred_element_type=F32)


def dot_last(left, right):
    return lax.dot_general(left, right, (((1,), (1,)), ((), ())), preferred_element_type=F32)


def rows_hot(index_row, height):
    shape = (height, index_row.shape[1])
    index = jnp.broadcast_to(index_row, shape).astype(jnp.int16)
    return jnp.where(
        index == lax.broadcasted_iota(jnp.int16, shape, 0), jnp.ones((), BF16), jnp.zeros((), BF16)
    )


def silu_of_half(half):
    return half + half * jnp.tanh(half)


def halved(weight):
    return weight * jnp.asarray(0.5, BF16)


class Grid:
    def __init__(self, mesh, halo_capacity, pool_capacity, coarse_capacity, coarse_blocks, slot_count):
        self.dom_count = mesh.shape["dom"]
        self.sub_count = mesh.shape["sub"]
        self.chip_count = mesh.shape["chip"]
        self.places = self.sub_count * self.chip_count
        self.mirrored = self.dom_count == 4
        self.steps = (2, 3, 1) if self.mirrored else (1, self.dom_count - 1, 2)
        self.owners = len(range(0, self.places, 4))
        self.swapped = self.sub_count == 2 and self.chip_count == 2
        self.halo_capacity = halo_capacity
        self.pool_capacity = pool_capacity
        self.coarse_capacity = coarse_capacity
        self.blocks = coarse_blocks
        self.pieces = slot_count // BLOCK
        self.slots = self.places * pool_capacity
        self.pooled_rows = self.owners * pool_capacity
        self.sent_blocks = 1 if self.swapped else coarse_blocks
        self.list_rows = 2 * self.sent_blocks * self.pieces + self.dom_count
        self.packed_rows = -(-self.list_rows // 16) * 16
        self.packet = self.pooled_rows + self.packed_rows
        self.packets = 2 if self.swapped else 1
        self.octaves = -(-(self.slots + self.dom_count * coarse_capacity) // BLOCK)

    def partner(self, dom, step):
        return dom ^ step if self.mirrored else (dom + step) % self.dom_count

    def partner_here(self, step):
        own = lax.axis_index("dom")
        return own ^ step if self.mirrored else lax.rem(own + step, self.dom_count)

    def halo_place(self, source_dom):
        own = lax.axis_index("dom")
        if self.mirrored:
            step = source_dom ^ own
        else:
            step = own - source_dom
            step = jnp.where(step < 0, step + self.dom_count, step)
        place = jnp.zeros_like(step)
        for index, value in enumerate(self.steps):
            place = jnp.where(step == value, index, place)
        return place

    def block_of(self, place):
        return lax.div(place * self.pool_capacity, BLOCK)

    def own_place(self):
        return lax.axis_index("sub") * self.chip_count + lax.axis_index("chip")

    def slot_order(self, slots, place):
        return slots ^ (place * self.pool_capacity) if self.swapped else slots


def turned(weight):
    return halved(weight).T


def turn_kernel(latent_hbm, table_ref, latent_ref, arrived):
    part = latent_ref.shape[0] // PARTS
    copies = []
    for index in range(PARTS):
        rows = pl.ds(index * part, part)
        copies.append(pltpu.make_async_copy(latent_hbm.at[rows], latent_ref.at[rows], arrived.at[index]))
        copies[-1].start()
    for index, copy in enumerate(copies):
        copy.wait()
        rows = slice(index * part, (index + 1) * part)
        table_ref[:, rows] = latent_ref[rows, :].T


def send_kernel(grid, table_ref, lists_ref, weights_ref, *sent_refs):
    index_row = jnp.concatenate([lists_ref[0, pl.ds(grid.partner_here(step), 1), :] for step in grid.steps], axis=1)
    picked = dot(table_ref[...], rows_hot(index_row, table_ref.shape[1])).astype(BF16)
    terms = dot(turned(weights_ref[0, 0]), picked).astype(BF16)
    capacity = lists_ref.shape[2]
    for index, out_ref in enumerate(sent_refs):
        out_ref[...] = terms[:, index * capacity : (index + 1) * capacity]


def far_rows(source_ref, place_ref, batch):
    local_count = source_ref.shape[1] * 3 // 4
    sources, places = [], []
    for index in range(BATCH):
        row = slice(batch * BATCH + index, batch * BATCH + index + 1)
        sources.append(source_ref[row, local_count:])
        place = place_ref[row, local_count:]
        places.append(jnp.where(place >= 0, place + index * BLOCK, -1))
    return jnp.concatenate(sources, axis=1), jnp.concatenate(places, axis=1)


def near_edges(table, source_ref, place_ref, places_ref, weights_ref, layer, aimed_ref, sums_ref, terms_ref):
    features, node_count = table.shape
    block_count, slot_count = source_ref.shape
    local_count = slot_count * 3 // 4
    window = min(3 * BLOCK, node_count)
    both = jnp.concatenate([turned(weights_ref[layer, 0]), turned(weights_ref[layer, 1])], axis=0)
    terms_ref[...] = dot(both, table).astype(BF16)

    def far_targets(batch):
        columns = slice(batch * BATCH * BLOCK, (batch + 1) * BATCH * BLOCK)
        hot = rows_hot(places_ref[batch : batch + 1, :], BATCH * BLOCK)
        aimed_ref[:, batch * hot.shape[1] : (batch + 1) * hot.shape[1]] = dot(
            terms_ref[features:, columns], hot
        ).astype(BF16)

    def messages(block):
        start = min(max(block * BLOCK - BLOCK, 0), node_count - window)
        terms = jnp.concatenate(
            [
                terms_ref[:features, start : start + window],
                terms_ref[features:, block * BLOCK : (block + 1) * BLOCK],
            ],
            axis=1,
        )
        places = rows_hot(place_ref[block : block + 1, :local_count], BLOCK)
        sources = rows_hot(source_ref[block : block + 1, :local_count] - start, window)
        picked = dot(terms, jnp.concatenate([sources, places], axis=0))
        return silu_of_half(picked).astype(BF16)

    def add_up(block, message):
        places = rows_hot(place_ref[block : block + 1, :local_count], BLOCK)
        sums_ref[:, block * BLOCK : (block + 1) * BLOCK] = dot_last(message, places)

    waiting = None
    for block in range(block_count):
        message = messages(block)
        if waiting is not None:
            add_up(*waiting)
        waiting = (block, message)
        if block % BATCH == 0:
            far_targets(block // BATCH)
    add_up(*waiting)


def near_kernel(
    grid,
    table_ref,
    source_ref,
    place_ref,
    weights_ref,
    coarse_source_ref,
    coarse_place_ref,
    coarse_send_ref,
    pool_ref,
    sources_ref,
    places_ref,
    aimed_ref,
    sums_ref,
    pooled_ref,
    *rest,
):
    packed_refs, terms_ref = rest[:-1], rest[-1]
    table = table_ref[...]
    halo_capacity = grid.halo_capacity
    for batch in range(source_ref.shape[0] // BATCH):
        sources, places = far_rows(source_ref, place_ref, batch)
        slots = sources - table.shape[1]
        source_dom = lax.shift_right_logical(slots, halo_capacity.bit_length() - 1)
        sources_ref[batch : batch + 1, :] = grid.halo_place(source_dom) * halo_capacity + (
            slots & (halo_capacity - 1)
        )
        places_ref[batch : batch + 1, :] = places
    near_edges(table, source_ref, place_ref, places_ref, weights_ref, 0, aimed_ref, sums_ref, terms_ref)

    place = grid.own_place()
    for index, packed_ref in enumerate(packed_refs):
        if grid.swapped:
            block = grid.block_of(place ^ (2 * index))
            sources, places = coarse_source_ref[pl.ds(block, 1), :], coarse_place_ref[pl.ds(block, 1), :]
        else:
            sources, places = coarse_source_ref[...], coarse_place_ref[...]
        lists = jnp.minimum(coarse_send_ref[0], grid.slots - 1)
        pieces = lane_rows(sources) + [lists] + lane_rows(places + 1)
        spare = grid.packed_rows - grid.list_rows
        if spare:
            pieces.append(jnp.zeros((spare, BLOCK), I32))
        whole = jnp.concatenate(pieces, axis=0)
        coded = lax.shift_left((whole & (BLOCK - 1)) + BLOCK, lax.shift_right_logical(whole, BLOCK.bit_length() - 1))
        packed_ref[...] = coded.astype(F32).astype(BF16)
    for owner in range(grid.owners):
        pooled_ref[owner : owner + 1, :] = pool_ref[0, 4 * owner : 4 * owner + 1, :]


def far_edges(layer, table_ref, aimed_ref, sources_ref, places_ref, sums_ref, weights_ref, halo_refs, both_ref, write):
    features, node_count = table_ref.shape
    batch_count, slot_count = sources_ref.shape
    halo = jnp.concatenate([ref[...] for ref in halo_refs], axis=1)
    update_weights = jnp.concatenate([turned(weights_ref[layer, 2]), turned(weights_ref[layer, 3])], axis=1)
    pair_slots = slot_count * PAIR // BATCH
    pair_rows = PAIR * BLOCK
    batch_rows = BATCH * BLOCK
    both_ref[features:, :] = table_ref[...]

    def messages(batch):
        aimed = aimed_ref[:, batch * slot_count : (batch + 1) * slot_count].astype(F32)
        hot = rows_hot(sources_ref[batch : batch + 1, :], halo.shape[1])
        return silu_of_half(dot(halo, hot) + aimed).astype(BF16)

    def add_up(batch, message):
        for pair in range(BATCH // PAIR):
            slots = slice(pair * pair_slots, (pair + 1) * pair_slots)
            first = batch * batch_rows + pair * pair_rows
            columns = slice(first, first + pair_rows)
            hot = rows_hot(places_ref[batch : batch + 1, slots] - pair * pair_rows, pair_rows)
            both_ref[:features, columns] = (sums_ref[:, columns] + dot_last(message[:, slots], hot)).astype(BF16)

    def update(batch):
        columns = slice(batch * batch_rows, (batch + 1) * batch_rows)
        change = silu_of_half(dot(update_weights, both_ref[:, columns]))
        write(columns, (both_ref[features:, columns].astype(F32) + change).astype(BF16))

    message = messages(0)
    for batch in range(batch_count):
        following = messages(batch + 1) if batch + 1 < batch_count else None
        add_up(batch, message)
        if batch:
            update(batch - 1)
        message = following
    update(batch_count - 1)


def lane_rows(values):
    pieces = []
    for block in range(values.shape[0]):
        for start in range(0, values.shape[1], BLOCK):
            pieces.append(values[block : block + 1, start : start + BLOCK])
    return pieces


def far_pool_kernel(
    grid, table_ref, aimed_ref, sources_ref, places_ref, sums_ref, weights_ref, pool_ref, *rest
):
    count = grid.packets
    packed_refs, halo_refs = rest[:count], rest[count : count + len(grid.steps)]
    first_ref, packet_refs, both_ref = rest[-2 - count], rest[-1 - count : -1], rest[-1]

    def write(columns, value):
        first_ref[:, columns] = value

    for packet_ref, packed_ref in zip(packet_refs, packed_refs):
        packet_ref[grid.pooled_rows :, :] = packed_ref[...]
    far_edges(0, table_ref, aimed_ref, sources_ref, places_ref, sums_ref, weights_ref, halo_refs, both_ref, write)
    for owner in range(grid.owners):
        hot = rows_hot(pool_ref[owner : owner + 1, :], first_ref.shape[1])
        pooled = dot(first_ref[...], hot).astype(BF16).T
        for packet_ref in packet_refs:
            packet_ref[owner * grid.pool_capacity : (owner + 1) * grid.pool_capacity, :] = pooled


def far_kernel(table_ref, aimed_ref, sources_ref, places_ref, sums_ref, weights_ref, *rest):
    halo_refs, (out_hbm, both_ref, rows_ref, written) = rest[:-4], rest[-4:]
    copies = []

    def write(columns, value):
        rows_ref[columns, :] = value.T
        rows = pl.ds(columns.start, columns.stop - columns.start)
        copies.append(pltpu.make_async_copy(rows_ref.at[rows], out_hbm.at[rows], written.at[len(copies)]))
        copies[-1].start()

    far_edges(1, table_ref, aimed_ref, sources_ref, places_ref, sums_ref, weights_ref, halo_refs, both_ref, write)
    for copy in copies:
        copy.wait()


def ahead_kernel(grid, first_ref, prolong_ref, lists_ref, out_ref):
    indices = prolong_ref[...]
    shift = (4 * grid.pool_capacity).bit_length() - 1
    indices = lax.shift_right_logical(indices, shift) * grid.pool_capacity + (indices & (grid.pool_capacity - 1))
    indices = indices.astype(F32)
    row = jnp.concatenate([indices[block : block + 1, :] for block in range(indices.shape[0])], axis=1)
    extra = jnp.concatenate([row, jnp.zeros((15, row.shape[1]), F32)], axis=0).astype(BF16)
    table = jnp.concatenate([first_ref[...], extra], axis=0)
    capacity = lists_ref.shape[2]
    for index, step in enumerate(grid.steps):
        index_row = lists_ref[0, pl.ds(grid.partner_here(step), 1), :]
        picked = dot(table, rows_hot(index_row, table.shape[1]))
        out_ref[:, index * capacity : (index + 1) * capacity] = picked.astype(BF16)


def owner_lists(grid, packets, owner, place):
    if grid.swapped:
        rows = packets[0][grid.pooled_rows :, :].astype(F32)
        for other in range(1, grid.places):
            rows = jnp.where(place == other, packets[other][grid.pooled_rows :, :].astype(F32), rows)
    else:
        rows = packets[4 * owner][grid.pooled_rows :, :].astype(F32)
    coded = rows.astype(I32)
    octave = jnp.zeros_like(coded)
    for power in range(1, grid.octaves):
        octave = octave + jnp.where(coded >= BLOCK << power, 1, 0)
    return octave * BLOCK + lax.shift_right_logical(coded, octave) - BLOCK


def owner_table(grid, packets, owner):
    start = owner * grid.pool_capacity
    return jnp.concatenate([packet[start : start + grid.pool_capacity, :] for packet in packets], axis=0)


def coarse_send_kernel(grid, weights_ref, *refs):
    packets = refs[: grid.places]
    outs = refs[grid.places : grid.places + len(grid.steps)]
    lists_ref = refs[-1]
    place = grid.own_place()
    first_list = grid.sent_blocks * grid.pieces
    capacity = grid.coarse_capacity
    for owner in range(grid.owners):
        lists_ref[...] = owner_lists(grid, packets, owner, place)
        table = owner_table(grid, packets, owner)
        terms = dot(table, halved(weights_ref[0])).astype(BF16).T
        index_row = jnp.concatenate(
            [lists_ref[pl.ds(first_list + grid.partner_here(step), 1), :] for step in grid.steps], axis=1
        )
        picked = dot(terms, rows_hot(grid.slot_order(index_row, place), grid.slots)).astype(BF16)
        for index, out_ref in enumerate(outs):
            out_ref[owner * BLOCK : (owner + 1) * BLOCK, :] = picked[:, index * capacity : (index + 1) * capacity]


def coarse_own_kernel(grid, weights_ref, *refs):
    packets = refs[: grid.places]
    picked_ref, source_out, place_out, rows_out, lists_ref = refs[grid.places :]
    place = grid.own_place()
    first_slot = place * grid.pool_capacity
    block = 0 if grid.swapped else grid.block_of(place)
    within = first_slot & (BLOCK - 1)
    shift = grid.coarse_capacity.bit_length() - 1
    for owner in range(grid.owners):
        lists_ref[...] = owner_lists(grid, packets, owner, place)
        sources = jnp.concatenate(
            [lists_ref[pl.ds(block * grid.pieces + piece, 1), :] for piece in range(grid.pieces)], axis=1
        )
        offset = grid.sent_blocks * grid.pieces + grid.dom_count
        places = jnp.concatenate(
            [lists_ref[pl.ds(offset + block * grid.pieces + piece, 1), :] for piece in range(grid.pieces)], axis=1
        )
        places = places - 1 - within
        places = jnp.where((places >= 0) & (places < grid.pool_capacity), places, -1)
        halo_slots = sources - grid.slots
        source_dom = lax.shift_right_arithmetic(halo_slots, shift)
        halo_sources = grid.halo_place(source_dom) * grid.coarse_capacity + (halo_slots & (grid.coarse_capacity - 1))
        is_halo = halo_slots >= 0
        source_out[owner : owner + 1, :] = jnp.where(is_halo, halo_sources, -1)
        place_out[owner : owner + 1, :] = places
        own_sources = jnp.where(is_halo, -1, grid.slot_order(sources, place))

        table = owner_table(grid, packets, owner)
        rows = table[: grid.pool_capacity]
        if not grid.swapped:
            for other in range(1, grid.places):
                other_rows = table[other * grid.pool_capacity : (other + 1) * grid.pool_capacity]
                rows = jnp.where(place == other, other_rows, rows)
        rows_out[owner] = rows.T
        sender = dot(table, halved(weights_ref[0])).astype(BF16).T
        target = dot(rows, halved(weights_ref[1])).astype(BF16).T
        hot = jnp.concatenate([rows_hot(own_sources, grid.slots), rows_hot(places, grid.pool_capacity)], axis=0)
        picked_ref[owner] = dot(jnp.concatenate([sender, target], axis=1), hot)


def lift(table, prolonged, index_row):
    pooled_rows = prolonged.shape[1] // 2
    hot = rows_hot(index_row, pooled_rows)
    hot = jnp.concatenate([hot, hot], axis=0)
    return (table.astype(F32) + silu_of_half(dot(prolonged, hot))).astype(BF16)


def lift_halo_kernel(
    grid,
    picked_ref,
    source_ref,
    place_ref,
    rows_ref,
    ahead_ref,
    coarse_weights_ref,
    prolong_weight_ref,
    weights_ref,
    *rest,
):
    count = len(grid.steps)
    halo_refs, prolonged_ref, sent_refs = rest[:count], rest[count], rest[count + 1 :]
    features = rows_ref.shape[1]
    update_weights = jnp.concatenate([turned(coarse_weights_ref[2]), turned(coarse_weights_ref[3])], axis=1)
    prolong_weight = turned(prolong_weight_ref[...])
    prolonged = []
    for owner in range(grid.owners):
        halo = jnp.concatenate([ref[owner * BLOCK : (owner + 1) * BLOCK, :] for ref in halo_refs], axis=1)
        picked = picked_ref[owner] + dot(halo, rows_hot(source_ref[owner : owner + 1, :], halo.shape[1]))
        message = silu_of_half(picked).astype(BF16)
        places = rows_hot(place_ref[owner : owner + 1, :], grid.pool_capacity)
        summed = dot_last(message, places).astype(BF16)
        rows = rows_ref[owner]
        update = dot(update_weights, jnp.concatenate([summed, rows], axis=0))
        coarse = (rows.astype(F32) + silu_of_half(update)).astype(BF16)
        prolonged.append(dot(prolong_weight, coarse))
    prolonged = jnp.concatenate(prolonged, axis=1)
    high = prolonged.astype(BF16)
    low = (prolonged - high.astype(F32)).astype(BF16)
    parts = jnp.concatenate([high, low], axis=1)
    prolonged_ref[...] = parts
    weight = turned(weights_ref[1, 0])
    index_row = ahead_ref[features : features + 1, :].astype(F32).astype(I32)
    lifted = lift(ahead_ref[:features, :], parts, index_row)
    terms = dot(weight, lifted).astype(BF16)
    capacity = sent_refs[0].shape[1]
    for index, out_ref in enumerate(sent_refs):
        out_ref[...] = terms[:, index * capacity : (index + 1) * capacity]


def lift_near_kernel(
    grid,
    first_ref,
    prolonged_ref,
    prolong_ref,
    source_ref,
    place_ref,
    places_ref,
    weights_ref,
    lifted_ref,
    aimed_ref,
    sums_ref,
    terms_ref,
):
    indices = prolong_ref[...]
    shift = (4 * grid.pool_capacity).bit_length() - 1
    indices = lax.shift_right_logical(indices, shift) * grid.pool_capacity + (indices & (grid.pool_capacity - 1))
    row = jnp.concatenate([indices[block : block + 1, :] for block in range(indices.shape[0])], axis=1)
    lifted = lift(first_ref[...], prolonged_ref[...], row)
    lifted_ref[...] = lifted
    near_edges(lifted, source_ref, place_ref, places_ref, weights_ref, 1, aimed_ref, sums_ref, terms_ref)


def call(kernel, outs, scratch=(), flops=0, name=None, limit=VMEM_BYTES, **specs):
    return pl.pallas_call(
        kernel,
        out_shape=tuple(jax.ShapeDtypeStruct(shape, dtype) for shape, dtype in outs),
        scratch_shapes=list(scratch),
        compiler_params=pltpu.CompilerParams(vmem_limit_bytes=limit),
        cost_estimate=pl.CostEstimate(flops=flops, bytes_accessed=4 << 20, transcendentals=0),
        name=name,
        **specs,
    )


def swap_dom(grid, arrays, order=(0, 1, 2)):
    arrived = {}
    for index in order:
        step = grid.steps[index]
        arrived[index] = lax.ppermute(
            arrays[index], "dom", [(dom, grid.partner(dom, step)) for dom in range(grid.dom_count)]
        )
    return [arrived[index] for index in range(len(arrays))]


def trade_packets(grid, packets):
    if grid.swapped:
        pairs = [(0, 1), (1, 0)]
        near, far = packets
        over = lax.ppermute(far, "sub", pairs)
        across = lax.ppermute(near, "chip", pairs)
        both = lax.ppermute(far, ("sub", "chip"), [(0, 3), (1, 2), (2, 1), (3, 0)])
        return [near, across, over, both]
    gathered = lax.all_gather(packets[0], ("sub", "chip"), axis=0, tiled=False)
    return [gathered[place] for place in range(grid.places)]


def body(
    mesh,
    fine_nodes,
    fine_src,
    fine_dst,
    halo_send,
    pool_send,
    coarse_src,
    coarse_dst,
    coarse_send,
    prolong_idx,
    fine_weights,
    coarse_weights,
    prolong_weight,
):
    node_count, features = fine_nodes.shape
    halo_capacity = halo_send.shape[2]
    coarse_blocks, coarse_slots = coarse_src.shape
    grid = Grid(mesh, halo_capacity, pool_send.shape[2], coarse_send.shape[2], coarse_blocks, coarse_slots)
    steps = len(grid.steps)
    block_count, slot_count = fine_src.shape
    far_count = slot_count - slot_count * 3 // 4
    table = ((features, node_count), BF16)
    sums_table = ((features, node_count), F32)
    aimed_table = ((features, block_count * far_count), BF16)
    far_lists = ((block_count // BATCH, BATCH * far_count), I32)
    halo_outs = [((features, halo_capacity), BF16)] * steps
    two_tables = pltpu.VMEM((2 * features, node_count), BF16)
    prolong_rows = prolong_idx.reshape(node_count // BLOCK, BLOCK)
    big = 1 << 30
    in_hbm = pl.BlockSpec(memory_space=pltpu.HBM)

    (nodes,) = call(
        turn_kernel,
        [table],
        [pltpu.VMEM((node_count, features), BF16), pltpu.SemaphoreType.DMA((PARTS,))],
        name="turn",
        limit=5300 * 10486,
        in_specs=[in_hbm],
    )(fine_nodes)
    sent = call(functools.partial(send_kernel, grid), halo_outs, flops=big, name="send")(
        nodes, halo_send, fine_weights
    )
    halo = swap_dom(grid, sent)
    far_sources, far_places, aimed, sums, pool_lists, *packed = call(
        functools.partial(near_kernel, grid),
        [
            far_lists,
            far_lists,
            aimed_table,
            sums_table,
            ((grid.owners, grid.pool_capacity), I32),
            *[((grid.packed_rows, features), BF16)] * grid.packets,
        ],
        [two_tables],
        flops=4 * big,
        name="near",
    )(nodes, fine_src, fine_dst, fine_weights, coarse_src, coarse_dst, coarse_send, pool_send)
    first, *packets = call(
        functools.partial(far_pool_kernel, grid),
        [table, *[((grid.packet, features), BF16)] * grid.packets],
        [two_tables],
        flops=2 * big,
        name="far_pool",
    )(nodes, aimed, far_sources, far_places, sums, fine_weights, pool_lists, *packed, *halo)
    packets = trade_packets(grid, packets)
    (ahead,) = call(
        functools.partial(ahead_kernel, grid), [((features + 16, steps * halo_capacity), BF16)], flops=big, name="ahead"
    )(first, prolong_rows, halo_send)
    lists_scratch = pltpu.VMEM((grid.packed_rows, BLOCK), I32)
    sent = call(
        functools.partial(coarse_send_kernel, grid),
        [((grid.owners * features, grid.coarse_capacity), BF16)] * steps,
        [lists_scratch],
        flops=big // 2,
        name="coarse_send",
    )(coarse_weights, *packets)
    coarse_halo = swap_dom(grid, sent)
    picked, sources, places, rows = call(
        functools.partial(coarse_own_kernel, grid),
        [
            ((grid.owners, features, coarse_slots), F32),
            ((grid.owners, coarse_slots), I32),
            ((grid.owners, coarse_slots), I32),
            ((grid.owners, features, grid.pool_capacity), BF16),
        ],
        [lists_scratch],
        flops=4 * big,
        name="coarse_own",
    )(coarse_weights, *packets)
    prolonged, *sent = call(
        functools.partial(lift_halo_kernel, grid),
        [((features, 2 * grid.pooled_rows), BF16), *halo_outs],
        flops=big,
        name="lift_halo",
    )(picked, sources, places, rows, ahead, coarse_weights, prolong_weight, fine_weights, *coarse_halo)
    halo = swap_dom(grid, sent)
    lifted, aimed, sums = call(
        functools.partial(lift_near_kernel, grid),
        [table, aimed_table, sums_table],
        [two_tables],
        flops=4 * big,
        name="lift_near",
    )(first, prolonged, prolong_rows, fine_src, fine_dst, far_places, fine_weights)
    (fine_out,) = call(
        far_kernel,
        [((node_count, features), BF16)],
        [
            two_tables,
            pltpu.VMEM((node_count, features), BF16),
            pltpu.SemaphoreType.DMA((block_count // BATCH,)),
        ],
        flops=2 * big,
        name="far",
        out_specs=(pl.BlockSpec(memory_space=pltpu.HBM),),
    )(lifted, aimed, far_sources, far_places, sums, fine_weights, *halo)
    return fine_out


def solution(mesh):
    split = ("groups", "dom", "sub", "chip")
    return jax.shard_map(
        functools.partial(body, mesh),
        mesh=mesh,
        in_specs=(
            P(split, None),
            P(split, None),
            P(split, None),
            P(split, None, None),
            P(split, None, None),
            P(split, None),
            P(split, None),
            P(split, None, None),
            P(split),
            P(),
            P(),
            P(),
        ),
        out_specs=P(split, None),
        check_vma=False,
    )
```

```python
import functools

import jax
import jax.numpy as jnp
from jax import lax
from jax.experimental import pallas as pl
from jax.experimental.pallas import tpu as pltpu
from jax.sharding import PartitionSpec as P

BF16 = jnp.bfloat16
F32 = jnp.float32
I32 = jnp.int32
BLOCK = 128
VMEM_BYTES = 32 << 20
BATCH = 4
PARTS = 2
PAIR = 1


def dot(left, right):
    return jnp.dot(left, right, preferred_element_type=F32)


def dot_last(left, right):
    return lax.dot_general(left, right, (((1,), (1,)), ((), ())), preferred_element_type=F32)


def rows_hot(index_row, height):
    shape = (height, index_row.shape[1])
    index = jnp.broadcast_to(index_row, shape).astype(jnp.int16)
    return jnp.where(
        index == lax.broadcasted_iota(jnp.int16, shape, 0), jnp.ones((), BF16), jnp.zeros((), BF16)
    )


def silu_of_half(half):
    return half + half * jnp.tanh(half)


def halved(weight):
    return weight * jnp.asarray(0.5, BF16)


class Grid:
    def __init__(self, mesh, halo_capacity, pool_capacity, coarse_capacity, coarse_blocks, slot_count):
        self.dom_count = mesh.shape["dom"]
        self.sub_count = mesh.shape["sub"]
        self.chip_count = mesh.shape["chip"]
        self.places = self.sub_count * self.chip_count
        self.mirrored = self.dom_count == 4
        self.steps = (2, 3, 1) if self.mirrored else (1, self.dom_count - 1, 2)
        self.owners = len(range(0, self.places, 4))
        self.swapped = self.sub_count == 2 and self.chip_count == 2
        self.halo_capacity = halo_capacity
        self.pool_capacity = pool_capacity
        self.coarse_capacity = coarse_capacity
        self.blocks = coarse_blocks
        self.pieces = slot_count // BLOCK
        self.slots = self.places * pool_capacity
        self.pooled_rows = self.owners * pool_capacity
        self.sent_blocks = 1 if self.swapped else coarse_blocks
        self.list_rows = 2 * self.sent_blocks * self.pieces + self.dom_count
        self.packed_rows = -(-self.list_rows // 16) * 16
        self.packet = self.pooled_rows + self.packed_rows
        self.packets = 2 if self.swapped else 1
        self.octaves = -(-(self.slots + self.dom_count * coarse_capacity) // BLOCK)

    def partner(self, dom, step):
        return dom ^ step if self.mirrored else (dom + step) % self.dom_count

    def partner_here(self, step):
        own = lax.axis_index("dom")
        return own ^ step if self.mirrored else lax.rem(own + step, self.dom_count)

    def halo_place(self, source_dom):
        own = lax.axis_index("dom")
        if self.mirrored:
            step = source_dom ^ own
        else:
            step = own - source_dom
            step = jnp.where(step < 0, step + self.dom_count, step)
        place = jnp.zeros_like(step)
        for index, value in enumerate(self.steps):
            place = jnp.where(step == value, index, place)
        return place

    def block_of(self, place):
        return lax.div(place * self.pool_capacity, BLOCK)

    def own_place(self):
        return lax.axis_index("sub") * self.chip_count + lax.axis_index("chip")

    def slot_order(self, slots, place):
        return slots ^ (place * self.pool_capacity) if self.swapped else slots


def turned(weight):
    return halved(weight).T


def turn_kernel(latent_hbm, table_ref, latent_ref, arrived):
    part = latent_ref.shape[0] // PARTS
    copies = []
    for index in range(PARTS):
        rows = pl.ds(index * part, part)
        copies.append(pltpu.make_async_copy(latent_hbm.at[rows], latent_ref.at[rows], arrived.at[index]))
        copies[-1].start()
    for index, copy in enumerate(copies):
        copy.wait()
        rows = slice(index * part, (index + 1) * part)
        table_ref[:, rows] = latent_ref[rows, :].T


def send_kernel(grid, table_ref, lists_ref, weights_ref, *sent_refs):
    index_row = jnp.concatenate([lists_ref[0, pl.ds(grid.partner_here(step), 1), :] for step in grid.steps], axis=1)
    picked = dot(table_ref[...], rows_hot(index_row, table_ref.shape[1])).astype(BF16)
    terms = dot(turned(weights_ref[0, 0]), picked).astype(BF16)
    capacity = lists_ref.shape[2]
    for index, out_ref in enumerate(sent_refs):
        out_ref[...] = terms[:, index * capacity : (index + 1) * capacity]


def far_rows(source_ref, place_ref, batch):
    local_count = source_ref.shape[1] * 3 // 4
    sources, places = [], []
    for index in range(BATCH):
        row = slice(batch * BATCH + index, batch * BATCH + index + 1)
        sources.append(source_ref[row, local_count:])
        place = place_ref[row, local_count:]
        places.append(jnp.where(place >= 0, place + index * BLOCK, -1))
    return jnp.concatenate(sources, axis=1), jnp.concatenate(places, axis=1)


def near_edges(table, source_ref, place_ref, weights_ref, layer, aimed_ref, sums_ref, terms_ref):
    features, node_count = table.shape
    block_count, slot_count = source_ref.shape
    local_count = slot_count * 3 // 4
    window = min(3 * BLOCK, node_count)
    both = jnp.concatenate([turned(weights_ref[layer, 0]), turned(weights_ref[layer, 1])], axis=0)
    terms_ref[...] = dot(both, table).astype(BF16)

    def messages(block):
        start = min(max(block * BLOCK - BLOCK, 0), node_count - window)
        terms = jnp.concatenate(
            [
                terms_ref[:features, start : start + window],
                terms_ref[features:, block * BLOCK : (block + 1) * BLOCK],
            ],
            axis=1,
        )
        places = rows_hot(place_ref[block : block + 1, :], BLOCK)
        sources = rows_hot(source_ref[block : block + 1, :] - start, window)
        picked = dot(terms, jnp.concatenate([sources, places], axis=0))
        far_count = slot_count - local_count
        aimed_ref[:, block * far_count : (block + 1) * far_count] = picked[:, local_count:].astype(BF16)
        return silu_of_half(picked[:, :local_count]).astype(BF16)

    def add_up(block, message):
        places = rows_hot(place_ref[block : block + 1, :local_count], BLOCK)
        sums_ref[:, block * BLOCK : (block + 1) * BLOCK] = dot_last(message, places)

    waiting = None
    for block in range(block_count):
        message = messages(block)
        if waiting is not None:
            add_up(*waiting)
        waiting = (block, message)
    add_up(*waiting)


def near_kernel(
    grid,
    table_ref,
    source_ref,
    place_ref,
    weights_ref,
    coarse_source_ref,
    coarse_place_ref,
    coarse_send_ref,
    pool_ref,
    sources_ref,
    places_ref,
    aimed_ref,
    sums_ref,
    pooled_ref,
    *rest,
):
    packed_refs, terms_ref = rest[:-1], rest[-1]
    table = table_ref[...]
    halo_capacity = grid.halo_capacity
    for batch in range(source_ref.shape[0] // BATCH):
        sources, places = far_rows(source_ref, place_ref, batch)
        slots = sources - table.shape[1]
        source_dom = lax.shift_right_logical(slots, halo_capacity.bit_length() - 1)
        sources_ref[batch : batch + 1, :] = grid.halo_place(source_dom) * halo_capacity + (
            slots & (halo_capacity - 1)
        )
        places_ref[batch : batch + 1, :] = places
    near_edges(table, source_ref, place_ref, weights_ref, 0, aimed_ref, sums_ref, terms_ref)

    place = grid.own_place()
    for index, packed_ref in enumerate(packed_refs):
        if grid.swapped:
            block = grid.block_of(place ^ (2 * index))
            sources, places = coarse_source_ref[pl.ds(block, 1), :], coarse_place_ref[pl.ds(block, 1), :]
        else:
            sources, places = coarse_source_ref[...], coarse_place_ref[...]
        lists = jnp.minimum(coarse_send_ref[0], grid.slots - 1)
        pieces = lane_rows(sources) + [lists] + lane_rows(places + 1)
        spare = grid.packed_rows - grid.list_rows
        if spare:
            pieces.append(jnp.zeros((spare, BLOCK), I32))
        whole = jnp.concatenate(pieces, axis=0)
        coded = lax.shift_left((whole & (BLOCK - 1)) + BLOCK, lax.shift_right_logical(whole, BLOCK.bit_length() - 1))
        packed_ref[...] = coded.astype(F32).astype(BF16)
    for owner in range(grid.owners):
        pooled_ref[owner : owner + 1, :] = pool_ref[0, 4 * owner : 4 * owner + 1, :]


def far_edges(layer, table_ref, aimed_ref, sources_ref, places_ref, sums_ref, weights_ref, halo_refs, both_ref, write):
    features, node_count = table_ref.shape
    batch_count, slot_count = sources_ref.shape
    halo = jnp.concatenate([ref[...] for ref in halo_refs], axis=1)
    update_weights = jnp.concatenate([turned(weights_ref[layer, 2]), turned(weights_ref[layer, 3])], axis=1)
    pair_slots = slot_count * PAIR // BATCH
    pair_rows = PAIR * BLOCK
    batch_rows = BATCH * BLOCK
    both_ref[features:, :] = table_ref[...]

    def messages(batch):
        aimed = aimed_ref[:, batch * slot_count : (batch + 1) * slot_count].astype(F32)
        hot = rows_hot(sources_ref[batch : batch + 1, :], halo.shape[1])
        return silu_of_half(dot(halo, hot) + aimed).astype(BF16)

    def add_up(batch, message):
        for pair in range(BATCH // PAIR):
            slots = slice(pair * pair_slots, (pair + 1) * pair_slots)
            first = batch * batch_rows + pair * pair_rows
            columns = slice(first, first + pair_rows)
            hot = rows_hot(places_ref[batch : batch + 1, slots] - pair * pair_rows, pair_rows)
            both_ref[:features, columns] = (sums_ref[:, columns] + dot_last(message[:, slots], hot)).astype(BF16)

    def update(batch):
        columns = slice(batch * batch_rows, (batch + 1) * batch_rows)
        change = silu_of_half(dot(update_weights, both_ref[:, columns]))
        write(columns, (both_ref[features:, columns].astype(F32) + change).astype(BF16))

    message = messages(0)
    for batch in range(batch_count):
        following = messages(batch + 1) if batch + 1 < batch_count else None
        add_up(batch, message)
        if batch:
            update(batch - 1)
        message = following
    update(batch_count - 1)


def lane_rows(values):
    pieces = []
    for block in range(values.shape[0]):
        for start in range(0, values.shape[1], BLOCK):
            pieces.append(values[block : block + 1, start : start + BLOCK])
    return pieces


def far_pool_kernel(
    grid, table_ref, aimed_ref, sources_ref, places_ref, sums_ref, weights_ref, pool_ref, *rest
):
    count = grid.packets
    packed_refs, halo_refs = rest[:count], rest[count : count + len(grid.steps)]
    first_ref, packet_refs, both_ref = rest[-2 - count], rest[-1 - count : -1], rest[-1]

    def write(columns, value):
        first_ref[:, columns] = value

    for packet_ref, packed_ref in zip(packet_refs, packed_refs):
        packet_ref[grid.pooled_rows :, :] = packed_ref[...]
    far_edges(0, table_ref, aimed_ref, sources_ref, places_ref, sums_ref, weights_ref, halo_refs, both_ref, write)
    for owner in range(grid.owners):
        hot = rows_hot(pool_ref[owner : owner + 1, :], first_ref.shape[1])
        pooled = dot(first_ref[...], hot).astype(BF16).T
        for packet_ref in packet_refs:
            packet_ref[owner * grid.pool_capacity : (owner + 1) * grid.pool_capacity, :] = pooled


def far_kernel(table_ref, aimed_ref, sources_ref, places_ref, sums_ref, weights_ref, *rest):
    halo_refs, (out_hbm, both_ref, rows_ref, written) = rest[:-4], rest[-4:]
    copies = []

    def write(columns, value):
        rows_ref[columns, :] = value.T
        rows = pl.ds(columns.start, columns.stop - columns.start)
        copies.append(pltpu.make_async_copy(rows_ref.at[rows], out_hbm.at[rows], written.at[len(copies)]))
        copies[-1].start()

    far_edges(1, table_ref, aimed_ref, sources_ref, places_ref, sums_ref, weights_ref, halo_refs, both_ref, write)
    for copy in copies:
        copy.wait()


def ahead_kernel(grid, first_ref, prolong_ref, lists_ref, out_ref):
    indices = prolong_ref[...]
    shift = (4 * grid.pool_capacity).bit_length() - 1
    indices = lax.shift_right_logical(indices, shift) * grid.pool_capacity + (indices & (grid.pool_capacity - 1))
    indices = indices.astype(F32)
    row = jnp.concatenate([indices[block : block + 1, :] for block in range(indices.shape[0])], axis=1)
    extra = jnp.concatenate([row, jnp.zeros((15, row.shape[1]), F32)], axis=0).astype(BF16)
    table = jnp.concatenate([first_ref[...], extra], axis=0)
    capacity = lists_ref.shape[2]
    for index, step in enumerate(grid.steps):
        index_row = lists_ref[0, pl.ds(grid.partner_here(step), 1), :]
        picked = dot(table, rows_hot(index_row, table.shape[1]))
        out_ref[:, index * capacity : (index + 1) * capacity] = picked.astype(BF16)


def owner_lists(grid, packets, owner, place):
    if grid.swapped:
        rows = packets[0][grid.pooled_rows :, :].astype(F32)
        for other in range(1, grid.places):
            rows = jnp.where(place == other, packets[other][grid.pooled_rows :, :].astype(F32), rows)
    else:
        rows = packets[4 * owner][grid.pooled_rows :, :].astype(F32)
    coded = rows.astype(I32)
    octave = jnp.zeros_like(coded)
    for power in range(1, grid.octaves):
        octave = octave + jnp.where(coded >= BLOCK << power, 1, 0)
    return octave * BLOCK + lax.shift_right_logical(coded, octave) - BLOCK


def owner_table(grid, packets, owner):
    start = owner * grid.pool_capacity
    return jnp.concatenate([packet[start : start + grid.pool_capacity, :] for packet in packets], axis=0)


def coarse_send_kernel(grid, weights_ref, *refs):
    packets = refs[: grid.places]
    outs = refs[grid.places : grid.places + len(grid.steps)]
    lists_ref = refs[-1]
    place = grid.own_place()
    first_list = grid.sent_blocks * grid.pieces
    capacity = grid.coarse_capacity
    for owner in range(grid.owners):
        lists_ref[...] = owner_lists(grid, packets, owner, place)
        table = owner_table(grid, packets, owner)
        terms = dot(table, halved(weights_ref[0])).astype(BF16).T
        index_row = jnp.concatenate(
            [lists_ref[pl.ds(first_list + grid.partner_here(step), 1), :] for step in grid.steps], axis=1
        )
        picked = dot(terms, rows_hot(grid.slot_order(index_row, place), grid.slots)).astype(BF16)
        for index, out_ref in enumerate(outs):
            out_ref[owner * BLOCK : (owner + 1) * BLOCK, :] = picked[:, index * capacity : (index + 1) * capacity]


def coarse_own_kernel(grid, weights_ref, *refs):
    packets = refs[: grid.places]
    picked_ref, source_out, place_out, rows_out, lists_ref = refs[grid.places :]
    place = grid.own_place()
    first_slot = place * grid.pool_capacity
    block = 0 if grid.swapped else grid.block_of(place)
    within = first_slot & (BLOCK - 1)
    shift = grid.coarse_capacity.bit_length() - 1
    for owner in range(grid.owners):
        lists_ref[...] = owner_lists(grid, packets, owner, place)
        sources = jnp.concatenate(
            [lists_ref[pl.ds(block * grid.pieces + piece, 1), :] for piece in range(grid.pieces)], axis=1
        )
        offset = grid.sent_blocks * grid.pieces + grid.dom_count
        places = jnp.concatenate(
            [lists_ref[pl.ds(offset + block * grid.pieces + piece, 1), :] for piece in range(grid.pieces)], axis=1
        )
        places = places - 1 - within
        places = jnp.where((places >= 0) & (places < grid.pool_capacity), places, -1)
        halo_slots = sources - grid.slots
        source_dom = lax.shift_right_arithmetic(halo_slots, shift)
        halo_sources = grid.halo_place(source_dom) * grid.coarse_capacity + (halo_slots & (grid.coarse_capacity - 1))
        is_halo = halo_slots >= 0
        source_out[owner : owner + 1, :] = jnp.where(is_halo, halo_sources, -1)
        place_out[owner : owner + 1, :] = places
        own_sources = jnp.where(is_halo, -1, grid.slot_order(sources, place))

        table = owner_table(grid, packets, owner)
        rows = table[: grid.pool_capacity]
        if not grid.swapped:
            for other in range(1, grid.places):
                other_rows = table[other * grid.pool_capacity : (other + 1) * grid.pool_capacity]
                rows = jnp.where(place == other, other_rows, rows)
        rows_out[owner] = rows.T
        sender = dot(table, halved(weights_ref[0])).astype(BF16).T
        target = dot(rows, halved(weights_ref[1])).astype(BF16).T
        hot = jnp.concatenate([rows_hot(own_sources, grid.slots), rows_hot(places, grid.pool_capacity)], axis=0)
        picked_ref[owner] = dot(jnp.concatenate([sender, target], axis=1), hot)


def lift(table, prolonged, index_row):
    pooled_rows = prolonged.shape[1] // 2
    hot = rows_hot(index_row, pooled_rows)
    hot = jnp.concatenate([hot, hot], axis=0)
    return (table.astype(F32) + dot(prolonged, hot)).astype(BF16)


def lift_halo_kernel(
    grid,
    picked_ref,
    source_ref,
    place_ref,
    rows_ref,
    ahead_ref,
    coarse_weights_ref,
    prolong_weight_ref,
    weights_ref,
    *rest,
):
    count = len(grid.steps)
    halo_refs, prolonged_ref, sent_refs = rest[:count], rest[count], rest[count + 1 :]
    features = rows_ref.shape[1]
    update_weights = jnp.concatenate([turned(coarse_weights_ref[2]), turned(coarse_weights_ref[3])], axis=1)
    prolong_weight = turned(prolong_weight_ref[...])
    prolonged = []
    for owner in range(grid.owners):
        halo = jnp.concatenate([ref[owner * BLOCK : (owner + 1) * BLOCK, :] for ref in halo_refs], axis=1)
        picked = picked_ref[owner] + dot(halo, rows_hot(source_ref[owner : owner + 1, :], halo.shape[1]))
        message = silu_of_half(picked).astype(BF16)
        places = rows_hot(place_ref[owner : owner + 1, :], grid.pool_capacity)
        summed = dot_last(message, places).astype(BF16)
        rows = rows_ref[owner]
        update = dot(update_weights, jnp.concatenate([summed, rows], axis=0))
        coarse = (rows.astype(F32) + silu_of_half(update)).astype(BF16)
        prolonged.append(silu_of_half(dot(prolong_weight, coarse)))
    prolonged = jnp.concatenate(prolonged, axis=1)
    high = prolonged.astype(BF16)
    low = (prolonged - high.astype(F32)).astype(BF16)
    parts = jnp.concatenate([high, low], axis=1)
    prolonged_ref[...] = parts
    weight = turned(weights_ref[1, 0])
    index_row = ahead_ref[features : features + 1, :].astype(F32).astype(I32)
    lifted = lift(ahead_ref[:features, :], parts, index_row)
    terms = dot(weight, lifted).astype(BF16)
    capacity = sent_refs[0].shape[1]
    for index, out_ref in enumerate(sent_refs):
        out_ref[...] = terms[:, index * capacity : (index + 1) * capacity]


def lift_near_kernel(
    grid,
    first_ref,
    prolonged_ref,
    prolong_ref,
    source_ref,
    place_ref,
    weights_ref,
    lifted_ref,
    aimed_ref,
    sums_ref,
    terms_ref,
):
    indices = prolong_ref[...]
    shift = (4 * grid.pool_capacity).bit_length() - 1
    indices = lax.shift_right_logical(indices, shift) * grid.pool_capacity + (indices & (grid.pool_capacity - 1))
    row = jnp.concatenate([indices[block : block + 1, :] for block in range(indices.shape[0])], axis=1)
    lifted = lift(first_ref[...], prolonged_ref[...], row)
    lifted_ref[...] = lifted
    near_edges(lifted, source_ref, place_ref, weights_ref, 1, aimed_ref, sums_ref, terms_ref)


def call(kernel, outs, scratch=(), flops=0, name=None, limit=VMEM_BYTES, **specs):
    return pl.pallas_call(
        kernel,
        out_shape=tuple(jax.ShapeDtypeStruct(shape, dtype) for shape, dtype in outs),
        scratch_shapes=list(scratch),
        compiler_params=pltpu.CompilerParams(vmem_limit_bytes=limit),
        cost_estimate=pl.CostEstimate(flops=flops, bytes_accessed=4 << 20, transcendentals=0),
        name=name,
        **specs,
    )


def swap_dom(grid, arrays, order=(0, 1, 2)):
    arrived = {}
    for index in order:
        step = grid.steps[index]
        arrived[index] = lax.ppermute(
            arrays[index], "dom", [(dom, grid.partner(dom, step)) for dom in range(grid.dom_count)]
        )
    return [arrived[index] for index in range(len(arrays))]


def trade_packets(grid, packets):
    if grid.swapped:
        pairs = [(0, 1), (1, 0)]
        near, far = packets
        over = lax.ppermute(far, "sub", pairs)
        across = lax.ppermute(near, "chip", pairs)
        both = lax.ppermute(far, ("sub", "chip"), [(0, 3), (1, 2), (2, 1), (3, 0)])
        return [near, across, over, both]
    gathered = lax.all_gather(packets[0], ("sub", "chip"), axis=0, tiled=False)
    return [gathered[place] for place in range(grid.places)]


def body(
    mesh,
    fine_nodes,
    fine_src,
    fine_dst,
    halo_send,
    pool_send,
    coarse_src,
    coarse_dst,
    coarse_send,
    prolong_idx,
    fine_weights,
    coarse_weights,
    prolong_weight,
):
    node_count, features = fine_nodes.shape
    halo_capacity = halo_send.shape[2]
    coarse_blocks, coarse_slots = coarse_src.shape
    grid = Grid(mesh, halo_capacity, pool_send.shape[2], coarse_send.shape[2], coarse_blocks, coarse_slots)
    steps = len(grid.steps)
    block_count, slot_count = fine_src.shape
    far_count = slot_count - slot_count * 3 // 4
    table = ((features, node_count), BF16)
    sums_table = ((features, node_count), F32)
    aimed_table = ((features, block_count * far_count), BF16)
    far_lists = ((block_count // BATCH, BATCH * far_count), I32)
    halo_outs = [((features, halo_capacity), BF16)] * steps
    two_tables = pltpu.VMEM((2 * features, node_count), BF16)
    prolong_rows = prolong_idx.reshape(node_count // BLOCK, BLOCK)
    big = 1 << 30
    in_hbm = pl.BlockSpec(memory_space=pltpu.HBM)

    (nodes,) = call(
        turn_kernel,
        [table],
        [pltpu.VMEM((node_count, features), BF16), pltpu.SemaphoreType.DMA((PARTS,))],
        name="turn",
        limit=5300 * 10486,
        in_specs=[in_hbm],
    )(fine_nodes)
    sent = call(functools.partial(send_kernel, grid), halo_outs, flops=big, name="send")(
        nodes, halo_send, fine_weights
    )
    halo = swap_dom(grid, sent)
    far_sources, far_places, aimed, sums, pool_lists, *packed = call(
        functools.partial(near_kernel, grid),
        [
            far_lists,
            far_lists,
            aimed_table,
            sums_table,
            ((grid.owners, grid.pool_capacity), I32),
            *[((grid.packed_rows, features), BF16)] * grid.packets,
        ],
        [two_tables],
        flops=4 * big,
        name="near",
    )(nodes, fine_src, fine_dst, fine_weights, coarse_src, coarse_dst, coarse_send, pool_send)
    first, *packets = call(
        functools.partial(far_pool_kernel, grid),
        [table, *[((grid.packet, features), BF16)] * grid.packets],
        [two_tables],
        flops=2 * big,
        name="far_pool",
    )(nodes, aimed, far_sources, far_places, sums, fine_weights, pool_lists, *packed, *halo)
    packets = trade_packets(grid, packets)
    (ahead,) = call(
        functools.partial(ahead_kernel, grid), [((features + 16, steps * halo_capacity), BF16)], flops=big, name="ahead"
    )(first, prolong_rows, halo_send)
    lists_scratch = pltpu.VMEM((grid.packed_rows, BLOCK), I32)
    sent = call(
        functools.partial(coarse_send_kernel, grid),
        [((grid.owners * features, grid.coarse_capacity), BF16)] * steps,
        [lists_scratch],
        flops=big // 2,
        name="coarse_send",
    )(coarse_weights, *packets)
    coarse_halo = swap_dom(grid, sent)
    picked, sources, places, rows = call(
        functools.partial(coarse_own_kernel, grid),
        [
            ((grid.owners, features, coarse_slots), F32),
            ((grid.owners, coarse_slots), I32),
            ((grid.owners, coarse_slots), I32),
            ((grid.owners, features, grid.pool_capacity), BF16),
        ],
        [lists_scratch],
        flops=4 * big,
        name="coarse_own",
    )(coarse_weights, *packets)
    prolonged, *sent = call(
        functools.partial(lift_halo_kernel, grid),
        [((features, 2 * grid.pooled_rows), BF16), *halo_outs],
        flops=big,
        name="lift_halo",
    )(picked, sources, places, rows, ahead, coarse_weights, prolong_weight, fine_weights, *coarse_halo)
    halo = swap_dom(grid, sent)
    lifted, aimed, sums = call(
        functools.partial(lift_near_kernel, grid),
        [table, aimed_table, sums_table],
        [two_tables],
        flops=4 * big,
        name="lift_near",
    )(first, prolonged, prolong_rows, fine_src, fine_dst, fine_weights)
    (fine_out,) = call(
        far_kernel,
        [((node_count, features), BF16)],
        [
            two_tables,
            pltpu.VMEM((node_count, features), BF16),
            pltpu.SemaphoreType.DMA((block_count // BATCH,)),
        ],
        flops=2 * big,
        name="far",
        out_specs=(pl.BlockSpec(memory_space=pltpu.HBM),),
    )(lifted, aimed, far_sources, far_places, sums, fine_weights, *halo)
    return fine_out


def solution(mesh):
    split = ("groups", "dom", "sub", "chip")
    return jax.shard_map(
        functools.partial(body, mesh),
        mesh=mesh,
        in_specs=(
            P(split, None),
            P(split, None),
            P(split, None),
            P(split, None, None),
            P(split, None, None),
            P(split, None),
            P(split, None),
            P(split, None, None),
            P(split),
            P(),
            P(),
            P(),
        ),
        out_specs=P(split, None),
        check_vma=False,
    )
```

```python
import functools

import jax
import jax.numpy as jnp
from jax import lax
from jax.experimental import pallas as pl
from jax.experimental.pallas import tpu as pltpu
from jax.sharding import PartitionSpec as P

BF16 = jnp.bfloat16
F32 = jnp.float32
I32 = jnp.int32
BLOCK = 128
VMEM_BYTES = 32 << 20
BATCH = 4
FIRST_ORDER, SECOND_ORDER = (1, 0, 2), (1, 2, 0)
PARTS = 2
PAIR = 1


def dot(left, right):
    return jnp.dot(left, right, preferred_element_type=F32)


def dot_last(left, right):
    return lax.dot_general(left, right, (((1,), (1,)), ((), ())), preferred_element_type=F32)


def rows_hot(index_row, height):
    shape = (height, index_row.shape[1])
    index = jnp.broadcast_to(index_row, shape).astype(jnp.int16)
    return jnp.where(
        index == lax.broadcasted_iota(jnp.int16, shape, 0), jnp.ones((), BF16), jnp.zeros((), BF16)
    )


def silu_of_half(half):
    return half + half * jnp.tanh(half)


def halved(weight):
    return weight * jnp.asarray(0.5, BF16)


class Grid:
    def __init__(self, mesh, halo_capacity, pool_capacity, coarse_capacity, coarse_blocks, slot_count):
        self.dom_count = mesh.shape["dom"]
        self.sub_count = mesh.shape["sub"]
        self.chip_count = mesh.shape["chip"]
        self.places = self.sub_count * self.chip_count
        self.mirrored = self.dom_count == 4
        self.steps = (2, 3, 1) if self.mirrored else (1, self.dom_count - 1, 2)
        self.owners = len(range(0, self.places, 4))
        self.swapped = self.sub_count == 2 and self.chip_count == 2
        self.halo_capacity = halo_capacity
        self.pool_capacity = pool_capacity
        self.coarse_capacity = coarse_capacity
        self.blocks = coarse_blocks
        self.pieces = slot_count // BLOCK
        self.slots = self.places * pool_capacity
        self.pooled_rows = self.owners * pool_capacity
        self.sent_blocks = 1 if self.swapped else coarse_blocks
        self.list_rows = 2 * self.sent_blocks * self.pieces + self.dom_count
        self.packed_rows = -(-self.list_rows // 16) * 16
        self.packet = self.pooled_rows + self.packed_rows
        self.packets = 2 if self.swapped else 1
        self.octaves = -(-(self.slots + self.dom_count * coarse_capacity) // BLOCK)

    def partner(self, dom, step):
        return dom ^ step if self.mirrored else (dom + step) % self.dom_count

    def partner_here(self, step):
        own = lax.axis_index("dom")
        return own ^ step if self.mirrored else lax.rem(own + step, self.dom_count)

    def halo_place(self, source_dom):
        own = lax.axis_index("dom")
        if self.mirrored:
            step = source_dom ^ own
        else:
            step = own - source_dom
            step = jnp.where(step < 0, step + self.dom_count, step)
        place = jnp.zeros_like(step)
        for index, value in enumerate(self.steps):
            place = jnp.where(step == value, index, place)
        return place

    def block_of(self, place):
        return lax.div(place * self.pool_capacity, BLOCK)

    def own_place(self):
        return lax.axis_index("sub") * self.chip_count + lax.axis_index("chip")

    def slot_order(self, slots, place):
        return slots ^ (place * self.pool_capacity) if self.swapped else slots


def handed(halos, order):
    return [halos[turn] for turn in order]


def taken(refs, order):
    return [refs[order.index(turn)] for turn in range(len(refs))]


def turned(weight):
    return halved(weight).T


def turn_kernel(latent_hbm, table_ref, latent_ref, arrived):
    part = latent_ref.shape[0] // PARTS
    copies = []
    for index in range(PARTS):
        rows = pl.ds(index * part, part)
        copies.append(pltpu.make_async_copy(latent_hbm.at[rows], latent_ref.at[rows], arrived.at[index]))
        copies[-1].start()
    for index, copy in enumerate(copies):
        copy.wait()
        rows = slice(index * part, (index + 1) * part)
        table_ref[:, rows] = latent_ref[rows, :].T


def send_kernel(grid, table_ref, lists_ref, weights_ref, *sent_refs):
    index_row = jnp.concatenate([lists_ref[0, pl.ds(grid.partner_here(step), 1), :] for step in grid.steps], axis=1)
    picked = dot(table_ref[...], rows_hot(index_row, table_ref.shape[1])).astype(BF16)
    terms = dot(turned(weights_ref[0, 0]), picked).astype(BF16)
    capacity = lists_ref.shape[2]
    for index, out_ref in enumerate(sent_refs):
        out_ref[...] = terms[:, index * capacity : (index + 1) * capacity]


def far_rows(source_ref, place_ref, batch):
    local_count = source_ref.shape[1] * 3 // 4
    sources, places = [], []
    for index in range(BATCH):
        row = slice(batch * BATCH + index, batch * BATCH + index + 1)
        sources.append(source_ref[row, local_count:])
        place = place_ref[row, local_count:]
        places.append(jnp.where(place >= 0, place + index * BLOCK, -1))
    return jnp.concatenate(sources, axis=1), jnp.concatenate(places, axis=1)


def near_edges(table, source_ref, place_ref, weights_ref, layer, aimed_ref, sums_ref, terms_ref):
    features, node_count = table.shape
    block_count, slot_count = source_ref.shape
    local_count = slot_count * 3 // 4
    window = min(3 * BLOCK, node_count)
    both = jnp.concatenate([turned(weights_ref[layer, 0]), turned(weights_ref[layer, 1])], axis=0)
    terms_ref[...] = dot(both, table).astype(BF16)

    def messages(block):
        start = min(max(block * BLOCK - BLOCK, 0), node_count - window)
        terms = jnp.concatenate(
            [
                terms_ref[:features, start : start + window],
                terms_ref[features:, block * BLOCK : (block + 1) * BLOCK],
            ],
            axis=1,
        )
        places = rows_hot(place_ref[block : block + 1, :], BLOCK)
        sources = rows_hot(source_ref[block : block + 1, :] - start, window)
        picked = dot(terms, jnp.concatenate([sources, places], axis=0))
        far_count = slot_count - local_count
        aimed_ref[:, block * far_count : (block + 1) * far_count] = picked[:, local_count:].astype(BF16)
        return silu_of_half(picked[:, :local_count]).astype(BF16)

    def add_up(block, message):
        places = rows_hot(place_ref[block : block + 1, :local_count], BLOCK)
        sums_ref[:, block * BLOCK : (block + 1) * BLOCK] = dot_last(message, places)

    waiting = None
    for block in range(block_count):
        message = messages(block)
        if waiting is not None:
            add_up(*waiting)
        waiting = (block, message)
    add_up(*waiting)


def near_kernel(
    grid,
    table_ref,
    source_ref,
    place_ref,
    weights_ref,
    coarse_source_ref,
    coarse_place_ref,
    coarse_send_ref,
    pool_ref,
    sources_ref,
    places_ref,
    aimed_ref,
    sums_ref,
    pooled_ref,
    *rest,
):
    packed_refs, terms_ref = rest[:-1], rest[-1]
    table = table_ref[...]
    halo_capacity = grid.halo_capacity
    for batch in range(source_ref.shape[0] // BATCH):
        sources, places = far_rows(source_ref, place_ref, batch)
        slots = sources - table.shape[1]
        source_dom = lax.shift_right_logical(slots, halo_capacity.bit_length() - 1)
        sources_ref[batch : batch + 1, :] = grid.halo_place(source_dom) * halo_capacity + (
            slots & (halo_capacity - 1)
        )
        places_ref[batch : batch + 1, :] = places
    near_edges(table, source_ref, place_ref, weights_ref, 0, aimed_ref, sums_ref, terms_ref)

    place = grid.own_place()
    for index, packed_ref in enumerate(packed_refs):
        if grid.swapped:
            block = grid.block_of(place ^ (2 * index))
            sources, places = coarse_source_ref[pl.ds(block, 1), :], coarse_place_ref[pl.ds(block, 1), :]
        else:
            sources, places = coarse_source_ref[...], coarse_place_ref[...]
        lists = jnp.minimum(coarse_send_ref[0], grid.slots - 1)
        pieces = lane_rows(sources) + [lists] + lane_rows(places + 1)
        spare = grid.packed_rows - grid.list_rows
        if spare:
            pieces.append(jnp.zeros((spare, BLOCK), I32))
        whole = jnp.concatenate(pieces, axis=0)
        coded = lax.shift_left((whole & (BLOCK - 1)) + BLOCK, lax.shift_right_logical(whole, BLOCK.bit_length() - 1))
        packed_ref[...] = coded.astype(F32).astype(BF16)
    for owner in range(grid.owners):
        pooled_ref[owner : owner + 1, :] = pool_ref[0, 4 * owner : 4 * owner + 1, :]


def far_edges(layer, table_ref, aimed_ref, sources_ref, places_ref, sums_ref, weights_ref, halo_refs, both_ref, write):
    features, node_count = table_ref.shape
    batch_count, slot_count = sources_ref.shape
    halo = jnp.concatenate([ref[...] for ref in halo_refs], axis=1)
    update_weights = jnp.concatenate([turned(weights_ref[layer, 2]), turned(weights_ref[layer, 3])], axis=1)
    pair_slots = slot_count * PAIR // BATCH
    pair_rows = PAIR * BLOCK
    batch_rows = BATCH * BLOCK
    both_ref[features:, :] = table_ref[...]

    def messages(batch):
        aimed = aimed_ref[:, batch * slot_count : (batch + 1) * slot_count].astype(F32)
        hot = rows_hot(sources_ref[batch : batch + 1, :], halo.shape[1])
        return silu_of_half(dot(halo, hot) + aimed).astype(BF16)

    def add_up(batch, message):
        for pair in range(BATCH // PAIR):
            slots = slice(pair * pair_slots, (pair + 1) * pair_slots)
            first = batch * batch_rows + pair * pair_rows
            columns = slice(first, first + pair_rows)
            hot = rows_hot(places_ref[batch : batch + 1, slots] - pair * pair_rows, pair_rows)
            both_ref[:features, columns] = (sums_ref[:, columns] + dot_last(message[:, slots], hot)).astype(BF16)

    def update(batch):
        columns = slice(batch * batch_rows, (batch + 1) * batch_rows)
        change = silu_of_half(dot(update_weights, both_ref[:, columns]))
        write(columns, (both_ref[features:, columns].astype(F32) + change).astype(BF16))

    message = messages(0)
    for batch in range(batch_count):
        following = messages(batch + 1) if batch + 1 < batch_count else None
        add_up(batch, message)
        if batch:
            update(batch - 1)
        message = following
    update(batch_count - 1)


def lane_rows(values):
    pieces = []
    for block in range(values.shape[0]):
        for start in range(0, values.shape[1], BLOCK):
            pieces.append(values[block : block + 1, start : start + BLOCK])
    return pieces


def far_pool_kernel(
    grid, table_ref, aimed_ref, sources_ref, places_ref, sums_ref, weights_ref, pool_ref, *rest
):
    count = grid.packets
    packed_refs, halo_refs = rest[:count], taken(rest[count : count + len(grid.steps)], FIRST_ORDER)
    first_ref, packet_refs, both_ref = rest[-2 - count], rest[-1 - count : -1], rest[-1]

    def write(columns, value):
        first_ref[:, columns] = value

    for packet_ref, packed_ref in zip(packet_refs, packed_refs):
        packet_ref[grid.pooled_rows :, :] = packed_ref[...]
    far_edges(0, table_ref, aimed_ref, sources_ref, places_ref, sums_ref, weights_ref, halo_refs, both_ref, write)
    for owner in range(grid.owners):
        hot = rows_hot(pool_ref[owner : owner + 1, :], first_ref.shape[1])
        pooled = dot(first_ref[...], hot).astype(BF16).T
        for packet_ref in packet_refs:
            packet_ref[owner * grid.pool_capacity : (owner + 1) * grid.pool_capacity, :] = pooled


def far_kernel(table_ref, aimed_ref, sources_ref, places_ref, sums_ref, weights_ref, *rest):
    halo_refs, (out_hbm, both_ref, rows_ref, written) = taken(rest[:-4], SECOND_ORDER), rest[-4:]
    copies = []

    def write(columns, value):
        rows_ref[columns, :] = value.T
        rows = pl.ds(columns.start, columns.stop - columns.start)
        copies.append(pltpu.make_async_copy(rows_ref.at[rows], out_hbm.at[rows], written.at[len(copies)]))
        copies[-1].start()

    far_edges(1, table_ref, aimed_ref, sources_ref, places_ref, sums_ref, weights_ref, halo_refs, both_ref, write)
    for copy in copies:
        copy.wait()


def ahead_kernel(grid, first_ref, prolong_ref, lists_ref, out_ref):
    indices = prolong_ref[...]
    shift = (4 * grid.pool_capacity).bit_length() - 1
    indices = lax.shift_right_logical(indices, shift) * grid.pool_capacity + (indices & (grid.pool_capacity - 1))
    indices = indices.astype(F32)
    row = jnp.concatenate([indices[block : block + 1, :] for block in range(indices.shape[0])], axis=1)
    extra = jnp.concatenate([row, jnp.zeros((15, row.shape[1]), F32)], axis=0).astype(BF16)
    table = jnp.concatenate([first_ref[...], extra], axis=0)
    capacity = lists_ref.shape[2]
    for index, step in enumerate(grid.steps):
        index_row = lists_ref[0, pl.ds(grid.partner_here(step), 1), :]
        picked = dot(table, rows_hot(index_row, table.shape[1]))
        out_ref[:, index * capacity : (index + 1) * capacity] = picked.astype(BF16)


def owner_lists(grid, packets, owner, place):
    if grid.swapped:
        rows = packets[0][grid.pooled_rows :, :].astype(F32)
        for other in range(1, grid.places):
            rows = jnp.where(place == other, packets[other][grid.pooled_rows :, :].astype(F32), rows)
    else:
        rows = packets[4 * owner][grid.pooled_rows :, :].astype(F32)
    coded = rows.astype(I32)
    octave = jnp.zeros_like(coded)
    for power in range(1, grid.octaves):
        octave = octave + jnp.where(coded >= BLOCK << power, 1, 0)
    return octave * BLOCK + lax.shift_right_logical(coded, octave) - BLOCK


def owner_table(grid, packets, owner):
    start = owner * grid.pool_capacity
    return jnp.concatenate([packet[start : start + grid.pool_capacity, :] for packet in packets], axis=0)


def coarse_send_kernel(grid, weights_ref, *refs):
    packets = refs[: grid.places]
    outs = refs[grid.places : grid.places + len(grid.steps)]
    lists_ref = refs[-1]
    place = grid.own_place()
    first_list = grid.sent_blocks * grid.pieces
    capacity = grid.coarse_capacity
    for owner in range(grid.owners):
        lists_ref[...] = owner_lists(grid, packets, owner, place)
        table = owner_table(grid, packets, owner)
        terms = dot(table, halved(weights_ref[0])).astype(BF16).T
        index_row = jnp.concatenate(
            [lists_ref[pl.ds(first_list + grid.partner_here(step), 1), :] for step in grid.steps], axis=1
        )
        picked = dot(terms, rows_hot(grid.slot_order(index_row, place), grid.slots)).astype(BF16)
        for index, out_ref in enumerate(outs):
            out_ref[owner * BLOCK : (owner + 1) * BLOCK, :] = picked[:, index * capacity : (index + 1) * capacity]


def coarse_own_kernel(grid, weights_ref, *refs):
    packets = refs[: grid.places]
    picked_ref, source_out, place_out, rows_out, lists_ref = refs[grid.places :]
    place = grid.own_place()
    first_slot = place * grid.pool_capacity
    block = 0 if grid.swapped else grid.block_of(place)
    within = first_slot & (BLOCK - 1)
    shift = grid.coarse_capacity.bit_length() - 1
    for owner in range(grid.owners):
        lists_ref[...] = owner_lists(grid, packets, owner, place)
        sources = jnp.concatenate(
            [lists_ref[pl.ds(block * grid.pieces + piece, 1), :] for piece in range(grid.pieces)], axis=1
        )
        offset = grid.sent_blocks * grid.pieces + grid.dom_count
        places = jnp.concatenate(
            [lists_ref[pl.ds(offset + block * grid.pieces + piece, 1), :] for piece in range(grid.pieces)], axis=1
        )
        places = places - 1 - within
        places = jnp.where((places >= 0) & (places < grid.pool_capacity), places, -1)
        halo_slots = sources - grid.slots
        source_dom = lax.shift_right_arithmetic(halo_slots, shift)
        halo_sources = grid.halo_place(source_dom) * grid.coarse_capacity + (halo_slots & (grid.coarse_capacity - 1))
        is_halo = halo_slots >= 0
        source_out[owner : owner + 1, :] = jnp.where(is_halo, halo_sources, -1)
        place_out[owner : owner + 1, :] = places
        own_sources = jnp.where(is_halo, -1, grid.slot_order(sources, place))

        table = owner_table(grid, packets, owner)
        rows = table[: grid.pool_capacity]
        if not grid.swapped:
            for other in range(1, grid.places):
                other_rows = table[other * grid.pool_capacity : (other + 1) * grid.pool_capacity]
                rows = jnp.where(place == other, other_rows, rows)
        rows_out[owner] = rows.T
        sender = dot(table, halved(weights_ref[0])).astype(BF16).T
        target = dot(rows, halved(weights_ref[1])).astype(BF16).T
        hot = jnp.concatenate([rows_hot(own_sources, grid.slots), rows_hot(places, grid.pool_capacity)], axis=0)
        picked_ref[owner] = dot(jnp.concatenate([sender, target], axis=1), hot)


def lift(table, prolonged, index_row):
    pooled_rows = prolonged.shape[1] // 2
    hot = rows_hot(index_row, pooled_rows)
    hot = jnp.concatenate([hot, hot], axis=0)
    return (table.astype(F32) + dot(prolonged, hot)).astype(BF16)


def lift_halo_kernel(
    grid,
    picked_ref,
    source_ref,
    place_ref,
    rows_ref,
    ahead_ref,
    coarse_weights_ref,
    prolong_weight_ref,
    weights_ref,
    *rest,
):
    count = len(grid.steps)
    halo_refs, prolonged_ref, sent_refs = rest[:count], rest[count], rest[count + 1 :]
    features = rows_ref.shape[1]
    update_weights = jnp.concatenate([turned(coarse_weights_ref[2]), turned(coarse_weights_ref[3])], axis=1)
    prolong_weight = turned(prolong_weight_ref[...])
    prolonged = []
    for owner in range(grid.owners):
        halo = jnp.concatenate([ref[owner * BLOCK : (owner + 1) * BLOCK, :] for ref in halo_refs], axis=1)
        picked = picked_ref[owner] + dot(halo, rows_hot(source_ref[owner : owner + 1, :], halo.shape[1]))
        message = silu_of_half(picked).astype(BF16)
        places = rows_hot(place_ref[owner : owner + 1, :], grid.pool_capacity)
        summed = dot_last(message, places).astype(BF16)
        rows = rows_ref[owner]
        update = dot(update_weights, jnp.concatenate([summed, rows], axis=0))
        coarse = (rows.astype(F32) + silu_of_half(update)).astype(BF16)
        prolonged.append(silu_of_half(dot(prolong_weight, coarse)))
    prolonged = jnp.concatenate(prolonged, axis=1)
    high = prolonged.astype(BF16)
    low = (prolonged - high.astype(F32)).astype(BF16)
    parts = jnp.concatenate([high, low], axis=1)
    prolonged_ref[...] = parts
    weight = turned(weights_ref[1, 0])
    index_row = ahead_ref[features : features + 1, :].astype(F32).astype(I32)
    lifted = lift(ahead_ref[:features, :], parts, index_row)
    terms = dot(weight, lifted).astype(BF16)
    capacity = sent_refs[0].shape[1]
    for index, out_ref in enumerate(sent_refs):
        out_ref[...] = terms[:, index * capacity : (index + 1) * capacity]


def lift_near_kernel(
    grid,
    first_ref,
    prolonged_ref,
    prolong_ref,
    source_ref,
    place_ref,
    weights_ref,
    lifted_ref,
    aimed_ref,
    sums_ref,
    terms_ref,
):
    indices = prolong_ref[...]
    shift = (4 * grid.pool_capacity).bit_length() - 1
    indices = lax.shift_right_logical(indices, shift) * grid.pool_capacity + (indices & (grid.pool_capacity - 1))
    row = jnp.concatenate([indices[block : block + 1, :] for block in range(indices.shape[0])], axis=1)
    lifted = lift(first_ref[...], prolonged_ref[...], row)
    lifted_ref[...] = lifted
    near_edges(lifted, source_ref, place_ref, weights_ref, 1, aimed_ref, sums_ref, terms_ref)


def call(kernel, outs, scratch=(), flops=0, name=None, limit=VMEM_BYTES, **specs):
    return pl.pallas_call(
        kernel,
        out_shape=tuple(jax.ShapeDtypeStruct(shape, dtype) for shape, dtype in outs),
        scratch_shapes=list(scratch),
        compiler_params=pltpu.CompilerParams(vmem_limit_bytes=limit),
        cost_estimate=pl.CostEstimate(flops=flops, bytes_accessed=4 << 20, transcendentals=0),
        name=name,
        **specs,
    )


def swap_dom(grid, arrays):
    return [
        lax.ppermute(array, "dom", [(dom, grid.partner(dom, step)) for dom in range(grid.dom_count)])
        for array, step in zip(arrays, grid.steps)
    ]


def trade_packets(grid, packets):
    if grid.swapped:
        pairs = [(0, 1), (1, 0)]
        near, far = packets
        over = lax.ppermute(far, "sub", pairs)
        across = lax.ppermute(near, "chip", pairs)
        both = lax.ppermute(far, ("sub", "chip"), [(0, 3), (1, 2), (2, 1), (3, 0)])
        return [near, across, over, both]
    gathered = lax.all_gather(packets[0], ("sub", "chip"), axis=0, tiled=False)
    return [gathered[place] for place in range(grid.places)]


def body(
    mesh,
    fine_nodes,
    fine_src,
    fine_dst,
    halo_send,
    pool_send,
    coarse_src,
    coarse_dst,
    coarse_send,
    prolong_idx,
    fine_weights,
    coarse_weights,
    prolong_weight,
):
    node_count, features = fine_nodes.shape
    halo_capacity = halo_send.shape[2]
    coarse_blocks, coarse_slots = coarse_src.shape
    grid = Grid(mesh, halo_capacity, pool_send.shape[2], coarse_send.shape[2], coarse_blocks, coarse_slots)
    steps = len(grid.steps)
    block_count, slot_count = fine_src.shape
    far_count = slot_count - slot_count * 3 // 4
    table = ((features, node_count), BF16)
    sums_table = ((features, node_count), F32)
    aimed_table = ((features, block_count * far_count), BF16)
    far_lists = ((block_count // BATCH, BATCH * far_count), I32)
    halo_outs = [((features, halo_capacity), BF16)] * steps
    two_tables = pltpu.VMEM((2 * features, node_count), BF16)
    prolong_rows = prolong_idx.reshape(node_count // BLOCK, BLOCK)
    big = 1 << 30
    in_hbm = pl.BlockSpec(memory_space=pltpu.HBM)

    (nodes,) = call(
        turn_kernel,
        [table],
        [pltpu.VMEM((node_count, features), BF16), pltpu.SemaphoreType.DMA((PARTS,))],
        name="turn",
        limit=5300 * 10486,
        in_specs=[in_hbm],
    )(fine_nodes)
    sent = call(functools.partial(send_kernel, grid), halo_outs, flops=big, name="send")(
        nodes, halo_send, fine_weights
    )
    halo = swap_dom(grid, sent)
    far_sources, far_places, aimed, sums, pool_lists, *packed = call(
        functools.partial(near_kernel, grid),
        [
            far_lists,
            far_lists,
            aimed_table,
            sums_table,
            ((grid.owners, grid.pool_capacity), I32),
            *[((grid.packed_rows, features), BF16)] * grid.packets,
        ],
        [two_tables],
        flops=4 * big,
        name="near",
    )(nodes, fine_src, fine_dst, fine_weights, coarse_src, coarse_dst, coarse_send, pool_send)
    first, *packets = call(
        functools.partial(far_pool_kernel, grid),
        [table, *[((grid.packet, features), BF16)] * grid.packets],
        [two_tables],
        flops=2 * big,
        name="far_pool",
    )(nodes, aimed, far_sources, far_places, sums, fine_weights, pool_lists, *packed, *handed(halo, FIRST_ORDER))
    packets = trade_packets(grid, packets)
    (ahead,) = call(
        functools.partial(ahead_kernel, grid), [((features + 16, steps * halo_capacity), BF16)], flops=big, name="ahead"
    )(first, prolong_rows, halo_send)
    lists_scratch = pltpu.VMEM((grid.packed_rows, BLOCK), I32)
    sent = call(
        functools.partial(coarse_send_kernel, grid),
        [((grid.owners * features, grid.coarse_capacity), BF16)] * steps,
        [lists_scratch],
        flops=big // 2,
        name="coarse_send",
    )(coarse_weights, *packets)
    coarse_halo = swap_dom(grid, sent)
    picked, sources, places, rows = call(
        functools.partial(coarse_own_kernel, grid),
        [
            ((grid.owners, features, coarse_slots), F32),
            ((grid.owners, coarse_slots), I32),
            ((grid.owners, coarse_slots), I32),
            ((grid.owners, features, grid.pool_capacity), BF16),
        ],
        [lists_scratch],
        flops=4 * big,
        name="coarse_own",
    )(coarse_weights, *packets)
    prolonged, *sent = call(
        functools.partial(lift_halo_kernel, grid),
        [((features, 2 * grid.pooled_rows), BF16), *halo_outs],
        flops=big,
        name="lift_halo",
    )(picked, sources, places, rows, ahead, coarse_weights, prolong_weight, fine_weights, *coarse_halo)
    halo = swap_dom(grid, sent)
    lifted, aimed, sums = call(
        functools.partial(lift_near_kernel, grid),
        [table, aimed_table, sums_table],
        [two_tables],
        flops=4 * big,
        name="lift_near",
    )(first, prolonged, prolong_rows, fine_src, fine_dst, fine_weights)
    (fine_out,) = call(
        far_kernel,
        [((node_count, features), BF16)],
        [
            two_tables,
            pltpu.VMEM((node_count, features), BF16),
            pltpu.SemaphoreType.DMA((block_count // BATCH,)),
        ],
        flops=2 * big,
        name="far",
        out_specs=(pl.BlockSpec(memory_space=pltpu.HBM),),
    )(lifted, aimed, far_sources, far_places, sums, fine_weights, *handed(halo, SECOND_ORDER))
    return fine_out


def solution(mesh):
    split = ("groups", "dom", "sub", "chip")
    return jax.shard_map(
        functools.partial(body, mesh),
        mesh=mesh,
        in_specs=(
            P(split, None),
            P(split, None),
            P(split, None),
            P(split, None, None),
            P(split, None, None),
            P(split, None),
            P(split, None),
            P(split, None, None),
            P(split),
            P(),
            P(),
            P(),
        ),
        out_specs=P(split, None),
        check_vma=False,
    )
```

```python
import functools

import jax
import jax.numpy as jnp
from jax import lax
from jax.experimental import pallas as pl
from jax.experimental.pallas import tpu as pltpu
from jax.sharding import PartitionSpec as P

BF16 = jnp.bfloat16
F32 = jnp.float32
I32 = jnp.int32
BLOCK = 128
VMEM_BYTES = 32 << 20
BATCH = 4
FIRST_ORDER, SECOND_ORDER = (1, 0, 2), (1, 2, 0)
PARTS = 2
PAIR = 1


def dot(left, right):
    return jnp.dot(left, right, preferred_element_type=F32)


def dot_last(left, right):
    return lax.dot_general(left, right, (((1,), (1,)), ((), ())), preferred_element_type=F32)


def rows_hot(index_row, height):
    shape = (height, index_row.shape[1])
    index = jnp.broadcast_to(index_row, shape).astype(jnp.int16)
    return jnp.where(
        index == lax.broadcasted_iota(jnp.int16, shape, 0), jnp.ones((), BF16), jnp.zeros((), BF16)
    )


def silu_of_half(half):
    return half + half * jnp.tanh(half)


def halved(weight):
    return weight * jnp.asarray(0.5, BF16)


class Grid:
    def __init__(self, mesh, halo_capacity, pool_capacity, coarse_capacity, coarse_blocks, slot_count):
        self.dom_count = mesh.shape["dom"]
        self.sub_count = mesh.shape["sub"]
        self.chip_count = mesh.shape["chip"]
        self.places = self.sub_count * self.chip_count
        self.mirrored = self.dom_count == 4
        self.steps = (2, 3, 1) if self.mirrored else (1, self.dom_count - 1, 2)
        self.owners = len(range(0, self.places, 4))
        self.swapped = self.sub_count == 2 and self.chip_count == 2
        self.halo_capacity = halo_capacity
        self.pool_capacity = pool_capacity
        self.coarse_capacity = coarse_capacity
        self.blocks = coarse_blocks
        self.pieces = slot_count // BLOCK
        self.slots = self.places * pool_capacity
        self.pooled_rows = self.owners * pool_capacity
        self.sent_blocks = 1 if self.swapped else coarse_blocks
        self.list_rows = 2 * self.sent_blocks * self.pieces + self.dom_count
        self.packed_rows = -(-self.list_rows // 16) * 16
        self.packet = self.pooled_rows + self.packed_rows
        self.packets = 2 if self.swapped else 1
        self.octaves = -(-(self.slots + self.dom_count * coarse_capacity) // BLOCK)

    def partner(self, dom, step):
        return dom ^ step if self.mirrored else (dom + step) % self.dom_count

    def partner_here(self, step):
        own = lax.axis_index("dom")
        return own ^ step if self.mirrored else lax.rem(own + step, self.dom_count)

    def halo_place(self, source_dom):
        own = lax.axis_index("dom")
        if self.mirrored:
            step = source_dom ^ own
        else:
            step = own - source_dom
            step = jnp.where(step < 0, step + self.dom_count, step)
        place = jnp.zeros_like(step)
        for index, value in enumerate(self.steps):
            place = jnp.where(step == value, index, place)
        return place

    def block_of(self, place):
        return lax.div(place * self.pool_capacity, BLOCK)

    def own_place(self):
        return lax.axis_index("sub") * self.chip_count + lax.axis_index("chip")

    def slot_order(self, slots, place):
        return slots ^ (place * self.pool_capacity) if self.swapped else slots


def handed(halos, order):
    return [halos[turn] for turn in order]


def taken(refs, order):
    return [refs[order.index(turn)] for turn in range(len(refs))]


def turned(weight):
    return halved(weight).T


def turned_update(weights_ref, *layer):
    return jnp.concatenate([turned(weights_ref[*layer, 2]), turned(weights_ref[*layer, 3])], axis=1)


def turn_kernel(latent_hbm, table_ref, latent_ref, arrived):
    part = latent_ref.shape[0] // PARTS
    copies = []
    for index in range(PARTS):
        rows = pl.ds(index * part, part)
        copies.append(pltpu.make_async_copy(latent_hbm.at[rows], latent_ref.at[rows], arrived.at[index]))
        copies[-1].start()
    for index, copy in enumerate(copies):
        copy.wait()
        rows = slice(index * part, (index + 1) * part)
        table_ref[:, rows] = latent_ref[rows, :].T


def send_kernel(grid, table_ref, lists_ref, weights_ref, *sent_refs):
    index_row = jnp.concatenate([lists_ref[0, pl.ds(grid.partner_here(step), 1), :] for step in grid.steps], axis=1)
    picked = dot(table_ref[...], rows_hot(index_row, table_ref.shape[1])).astype(BF16)
    terms = dot(turned(weights_ref[0, 0]), picked).astype(BF16)
    capacity = lists_ref.shape[2]
    for index, out_ref in enumerate(sent_refs):
        out_ref[...] = terms[:, index * capacity : (index + 1) * capacity]


def far_rows(source_ref, place_ref, batch):
    local_count = source_ref.shape[1] * 3 // 4
    sources, places = [], []
    for index in range(BATCH):
        row = slice(batch * BATCH + index, batch * BATCH + index + 1)
        sources.append(source_ref[row, local_count:])
        place = place_ref[row, local_count:]
        places.append(jnp.where(place >= 0, place + index * BLOCK, -1))
    return jnp.concatenate(sources, axis=1), jnp.concatenate(places, axis=1)


def near_edges(table, source_ref, place_ref, weights_ref, layer, aimed_ref, sums_ref, terms_ref):
    features, node_count = table.shape
    block_count, slot_count = source_ref.shape
    local_count = slot_count * 3 // 4
    window = min(3 * BLOCK, node_count)
    both = jnp.concatenate([turned(weights_ref[layer, 0]), turned(weights_ref[layer, 1])], axis=0)
    terms_ref[...] = dot(both, table).astype(BF16)

    def messages(block):
        start = min(max(block * BLOCK - BLOCK, 0), node_count - window)
        terms = jnp.concatenate(
            [
                terms_ref[:features, start : start + window],
                terms_ref[features:, block * BLOCK : (block + 1) * BLOCK],
            ],
            axis=1,
        )
        places = rows_hot(place_ref[block : block + 1, :], BLOCK)
        sources = rows_hot(source_ref[block : block + 1, :] - start, window)
        picked = dot(terms, jnp.concatenate([sources, places], axis=0))
        far_count = slot_count - local_count
        aimed_ref[:, block * far_count : (block + 1) * far_count] = picked[:, local_count:].astype(BF16)
        return silu_of_half(picked[:, :local_count]).astype(BF16)

    def add_up(block, message):
        places = rows_hot(place_ref[block : block + 1, :local_count], BLOCK)
        sums_ref[:, block * BLOCK : (block + 1) * BLOCK] = dot_last(message, places)

    waiting = None
    for block in range(block_count):
        message = messages(block)
        if waiting is not None:
            add_up(*waiting)
        waiting = (block, message)
    add_up(*waiting)


def near_kernel(
    grid,
    table_ref,
    source_ref,
    place_ref,
    weights_ref,
    coarse_source_ref,
    coarse_place_ref,
    coarse_send_ref,
    pool_ref,
    sources_ref,
    places_ref,
    aimed_ref,
    sums_ref,
    update_ref,
    pooled_ref,
    *rest,
):
    update_ref[...] = turned_update(weights_ref, 0)
    packed_refs, terms_ref = rest[:-1], rest[-1]
    table = table_ref[...]
    halo_capacity = grid.halo_capacity
    for batch in range(source_ref.shape[0] // BATCH):
        sources, places = far_rows(source_ref, place_ref, batch)
        slots = sources - table.shape[1]
        source_dom = lax.shift_right_logical(slots, halo_capacity.bit_length() - 1)
        sources_ref[batch : batch + 1, :] = grid.halo_place(source_dom) * halo_capacity + (
            slots & (halo_capacity - 1)
        )
        places_ref[batch : batch + 1, :] = places
    near_edges(table, source_ref, place_ref, weights_ref, 0, aimed_ref, sums_ref, terms_ref)

    place = grid.own_place()
    for index, packed_ref in enumerate(packed_refs):
        if grid.swapped:
            block = grid.block_of(place ^ (2 * index))
            sources, places = coarse_source_ref[pl.ds(block, 1), :], coarse_place_ref[pl.ds(block, 1), :]
        else:
            sources, places = coarse_source_ref[...], coarse_place_ref[...]
        lists = jnp.minimum(coarse_send_ref[0], grid.slots - 1)
        pieces = lane_rows(sources) + [lists] + lane_rows(places + 1)
        spare = grid.packed_rows - grid.list_rows
        if spare:
            pieces.append(jnp.zeros((spare, BLOCK), I32))
        whole = jnp.concatenate(pieces, axis=0)
        coded = lax.shift_left((whole & (BLOCK - 1)) + BLOCK, lax.shift_right_logical(whole, BLOCK.bit_length() - 1))
        packed_ref[...] = coded.astype(F32).astype(BF16)
    for owner in range(grid.owners):
        pooled_ref[owner : owner + 1, :] = pool_ref[0, 4 * owner : 4 * owner + 1, :]


def far_edges(table_ref, aimed_ref, sources_ref, places_ref, sums_ref, update_ref, halo_refs, both_ref, write):
    features, node_count = table_ref.shape
    batch_count, slot_count = sources_ref.shape
    halo = jnp.concatenate([ref[...] for ref in halo_refs], axis=1)
    pair_slots = slot_count * PAIR // BATCH
    pair_rows = PAIR * BLOCK
    batch_rows = BATCH * BLOCK
    both_ref[features:, :] = table_ref[...]

    def messages(batch):
        aimed = aimed_ref[:, batch * slot_count : (batch + 1) * slot_count].astype(F32)
        hot = rows_hot(sources_ref[batch : batch + 1, :], halo.shape[1])
        return silu_of_half(dot(halo, hot) + aimed).astype(BF16)

    def add_up(batch, message):
        for pair in range(BATCH // PAIR):
            slots = slice(pair * pair_slots, (pair + 1) * pair_slots)
            first = batch * batch_rows + pair * pair_rows
            columns = slice(first, first + pair_rows)
            hot = rows_hot(places_ref[batch : batch + 1, slots] - pair * pair_rows, pair_rows)
            both_ref[:features, columns] = (sums_ref[:, columns] + dot_last(message[:, slots], hot)).astype(BF16)

    def update(batch):
        columns = slice(batch * batch_rows, (batch + 1) * batch_rows)
        change = silu_of_half(dot(update_ref[...], both_ref[:, columns]))
        write(columns, (both_ref[features:, columns].astype(F32) + change).astype(BF16))

    message = messages(0)
    for batch in range(batch_count):
        following = messages(batch + 1) if batch + 1 < batch_count else None
        add_up(batch, message)
        if batch:
            update(batch - 1)
        message = following
    update(batch_count - 1)


def lane_rows(values):
    pieces = []
    for block in range(values.shape[0]):
        for start in range(0, values.shape[1], BLOCK):
            pieces.append(values[block : block + 1, start : start + BLOCK])
    return pieces


def far_pool_kernel(
    grid, table_ref, aimed_ref, sources_ref, places_ref, sums_ref, update_ref, pool_ref, *rest
):
    count = grid.packets
    packed_refs, halo_refs = rest[:count], taken(rest[count : count + len(grid.steps)], FIRST_ORDER)
    first_ref, packet_refs, both_ref = rest[-2 - count], rest[-1 - count : -1], rest[-1]

    def write(columns, value):
        first_ref[:, columns] = value

    for packet_ref, packed_ref in zip(packet_refs, packed_refs):
        packet_ref[grid.pooled_rows :, :] = packed_ref[...]
    far_edges(table_ref, aimed_ref, sources_ref, places_ref, sums_ref, update_ref, halo_refs, both_ref, write)
    for owner in range(grid.owners):
        hot = rows_hot(pool_ref[owner : owner + 1, :], first_ref.shape[1])
        pooled = dot(first_ref[...], hot).astype(BF16).T
        for packet_ref in packet_refs:
            packet_ref[owner * grid.pool_capacity : (owner + 1) * grid.pool_capacity, :] = pooled


def far_kernel(table_ref, aimed_ref, sources_ref, places_ref, sums_ref, update_ref, *rest):
    halo_refs, (out_hbm, both_ref, rows_ref, written) = taken(rest[:-4], SECOND_ORDER), rest[-4:]
    copies = []

    def write(columns, value):
        rows_ref[columns, :] = value.T
        rows = pl.ds(columns.start, columns.stop - columns.start)
        copies.append(pltpu.make_async_copy(rows_ref.at[rows], out_hbm.at[rows], written.at[len(copies)]))
        copies[-1].start()

    far_edges(table_ref, aimed_ref, sources_ref, places_ref, sums_ref, update_ref, halo_refs, both_ref, write)
    for copy in copies:
        copy.wait()


def ahead_kernel(grid, first_ref, prolong_ref, lists_ref, out_ref):
    indices = prolong_ref[...]
    shift = (4 * grid.pool_capacity).bit_length() - 1
    indices = lax.shift_right_logical(indices, shift) * grid.pool_capacity + (indices & (grid.pool_capacity - 1))
    indices = indices.astype(F32)
    row = jnp.concatenate([indices[block : block + 1, :] for block in range(indices.shape[0])], axis=1)
    extra = jnp.concatenate([row, jnp.zeros((15, row.shape[1]), F32)], axis=0).astype(BF16)
    table = jnp.concatenate([first_ref[...], extra], axis=0)
    capacity = lists_ref.shape[2]
    for index, step in enumerate(grid.steps):
        index_row = lists_ref[0, pl.ds(grid.partner_here(step), 1), :]
        picked = dot(table, rows_hot(index_row, table.shape[1]))
        out_ref[:, index * capacity : (index + 1) * capacity] = picked.astype(BF16)


def owner_lists(grid, packets, owner, place):
    if grid.swapped:
        rows = packets[0][grid.pooled_rows :, :].astype(F32)
        for other in range(1, grid.places):
            rows = jnp.where(place == other, packets[other][grid.pooled_rows :, :].astype(F32), rows)
    else:
        rows = packets[4 * owner][grid.pooled_rows :, :].astype(F32)
    coded = rows.astype(I32)
    octave = jnp.zeros_like(coded)
    for power in range(1, grid.octaves):
        octave = octave + jnp.where(coded >= BLOCK << power, 1, 0)
    return octave * BLOCK + lax.shift_right_logical(coded, octave) - BLOCK


def owner_table(grid, packets, owner):
    start = owner * grid.pool_capacity
    return jnp.concatenate([packet[start : start + grid.pool_capacity, :] for packet in packets], axis=0)


def coarse_send_kernel(grid, weights_ref, *refs):
    packets = refs[: grid.places]
    outs = refs[grid.places : grid.places + len(grid.steps)]
    lists_ref = refs[-1]
    place = grid.own_place()
    first_list = grid.sent_blocks * grid.pieces
    capacity = grid.coarse_capacity
    for owner in range(grid.owners):
        lists_ref[...] = owner_lists(grid, packets, owner, place)
        table = owner_table(grid, packets, owner)
        terms = dot(table, halved(weights_ref[0])).astype(BF16).T
        index_row = jnp.concatenate(
            [lists_ref[pl.ds(first_list + grid.partner_here(step), 1), :] for step in grid.steps], axis=1
        )
        picked = dot(terms, rows_hot(grid.slot_order(index_row, place), grid.slots)).astype(BF16)
        for index, out_ref in enumerate(outs):
            out_ref[owner * BLOCK : (owner + 1) * BLOCK, :] = picked[:, index * capacity : (index + 1) * capacity]


def coarse_own_kernel(grid, weights_ref, prolong_weight_ref, fine_weights_ref, *refs):
    packets = refs[: grid.places]
    picked_ref, source_out, place_out, rows_out, turned_out, lists_ref = refs[grid.places :]
    turned_out[...] = jnp.concatenate(
        [turned_update(weights_ref), turned(prolong_weight_ref[...]), turned(fine_weights_ref[1, 0])], axis=1
    )
    place = grid.own_place()
    first_slot = place * grid.pool_capacity
    block = 0 if grid.swapped else grid.block_of(place)
    within = first_slot & (BLOCK - 1)
    shift = grid.coarse_capacity.bit_length() - 1
    for owner in range(grid.owners):
        lists_ref[...] = owner_lists(grid, packets, owner, place)
        sources = jnp.concatenate(
            [lists_ref[pl.ds(block * grid.pieces + piece, 1), :] for piece in range(grid.pieces)], axis=1
        )
        offset = grid.sent_blocks * grid.pieces + grid.dom_count
        places = jnp.concatenate(
            [lists_ref[pl.ds(offset + block * grid.pieces + piece, 1), :] for piece in range(grid.pieces)], axis=1
        )
        places = places - 1 - within
        places = jnp.where((places >= 0) & (places < grid.pool_capacity), places, -1)
        halo_slots = sources - grid.slots
        source_dom = lax.shift_right_arithmetic(halo_slots, shift)
        halo_sources = grid.halo_place(source_dom) * grid.coarse_capacity + (halo_slots & (grid.coarse_capacity - 1))
        is_halo = halo_slots >= 0
        source_out[owner : owner + 1, :] = jnp.where(is_halo, halo_sources, -1)
        place_out[owner : owner + 1, :] = places
        own_sources = jnp.where(is_halo, -1, grid.slot_order(sources, place))

        table = owner_table(grid, packets, owner)
        rows = table[: grid.pool_capacity]
        if not grid.swapped:
            for other in range(1, grid.places):
                other_rows = table[other * grid.pool_capacity : (other + 1) * grid.pool_capacity]
                rows = jnp.where(place == other, other_rows, rows)
        rows_out[owner] = rows.T
        sender = dot(table, halved(weights_ref[0])).astype(BF16).T
        target = dot(rows, halved(weights_ref[1])).astype(BF16).T
        hot = jnp.concatenate([rows_hot(own_sources, grid.slots), rows_hot(places, grid.pool_capacity)], axis=0)
        picked_ref[owner] = dot(jnp.concatenate([sender, target], axis=1), hot)


def lift(table, prolonged, index_row):
    pooled_rows = prolonged.shape[1] // 2
    hot = rows_hot(index_row, pooled_rows)
    hot = jnp.concatenate([hot, hot], axis=0)
    return (table.astype(F32) + dot(prolonged, hot)).astype(BF16)


def lift_halo_kernel(
    grid,
    picked_ref,
    source_ref,
    place_ref,
    rows_ref,
    ahead_ref,
    turned_ref,
    *rest,
):
    count = len(grid.steps)
    halo_refs, prolonged_ref, sent_refs = rest[:count], rest[count], rest[count + 1 :]
    features = rows_ref.shape[1]
    update_weights = turned_ref[:, : 2 * features]
    prolong_weight = turned_ref[:, 2 * features : 3 * features]
    prolonged = []
    for owner in range(grid.owners):
        halo = jnp.concatenate([ref[owner * BLOCK : (owner + 1) * BLOCK, :] for ref in halo_refs], axis=1)
        picked = picked_ref[owner] + dot(halo, rows_hot(source_ref[owner : owner + 1, :], halo.shape[1]))
        message = silu_of_half(picked).astype(BF16)
        places = rows_hot(place_ref[owner : owner + 1, :], grid.pool_capacity)
        summed = dot_last(message, places).astype(BF16)
        rows = rows_ref[owner]
        update = dot(update_weights, jnp.concatenate([summed, rows], axis=0))
        coarse = (rows.astype(F32) + silu_of_half(update)).astype(BF16)
        prolonged.append(silu_of_half(dot(prolong_weight, coarse)))
    prolonged = jnp.concatenate(prolonged, axis=1)
    high = prolonged.astype(BF16)
    low = (prolonged - high.astype(F32)).astype(BF16)
    parts = jnp.concatenate([high, low], axis=1)
    prolonged_ref[...] = parts
    weight = turned_ref[:, 3 * features :]
    index_row = ahead_ref[features : features + 16, :].astype(F32).astype(I32)[:1]
    lifted = lift(ahead_ref[:features, :], parts, index_row)
    terms = dot(weight, lifted).astype(BF16)
    capacity = sent_refs[0].shape[1]
    for index, out_ref in enumerate(sent_refs):
        out_ref[...] = terms[:, index * capacity : (index + 1) * capacity]


def lift_near_kernel(
    grid,
    first_ref,
    prolonged_ref,
    prolong_ref,
    source_ref,
    place_ref,
    weights_ref,
    lifted_ref,
    aimed_ref,
    sums_ref,
    update_ref,
    terms_ref,
):
    update_ref[...] = turned_update(weights_ref, 1)
    indices = prolong_ref[...]
    shift = (4 * grid.pool_capacity).bit_length() - 1
    indices = lax.shift_right_logical(indices, shift) * grid.pool_capacity + (indices & (grid.pool_capacity - 1))
    row = jnp.concatenate([indices[block : block + 1, :] for block in range(indices.shape[0])], axis=1)
    lifted = lift(first_ref[...], prolonged_ref[...], row)
    lifted_ref[...] = lifted
    near_edges(lifted, source_ref, place_ref, weights_ref, 1, aimed_ref, sums_ref, terms_ref)


def call(kernel, outs, scratch=(), flops=0, name=None, limit=VMEM_BYTES, **specs):
    return pl.pallas_call(
        kernel,
        out_shape=tuple(jax.ShapeDtypeStruct(shape, dtype) for shape, dtype in outs),
        scratch_shapes=list(scratch),
        compiler_params=pltpu.CompilerParams(vmem_limit_bytes=limit),
        cost_estimate=pl.CostEstimate(flops=flops, bytes_accessed=4 << 20, transcendentals=0),
        name=name,
        **specs,
    )


def swap_dom(grid, arrays):
    return [
        lax.ppermute(array, "dom", [(dom, grid.partner(dom, step)) for dom in range(grid.dom_count)])
        for array, step in zip(arrays, grid.steps)
    ]


def trade_packets(grid, packets):
    if grid.swapped:
        pairs = [(0, 1), (1, 0)]
        near, far = packets
        over = lax.ppermute(far, "sub", pairs)
        across = lax.ppermute(near, "chip", pairs)
        both = lax.ppermute(far, ("sub", "chip"), [(0, 3), (1, 2), (2, 1), (3, 0)])
        return [near, across, over, both]
    gathered = lax.all_gather(packets[0], ("sub", "chip"), axis=0, tiled=False)
    return [gathered[place] for place in range(grid.places)]


def body(
    mesh,
    fine_nodes,
    fine_src,
    fine_dst,
    halo_send,
    pool_send,
    coarse_src,
    coarse_dst,
    coarse_send,
    prolong_idx,
    fine_weights,
    coarse_weights,
    prolong_weight,
):
    node_count, features = fine_nodes.shape
    halo_capacity = halo_send.shape[2]
    coarse_blocks, coarse_slots = coarse_src.shape
    grid = Grid(mesh, halo_capacity, pool_send.shape[2], coarse_send.shape[2], coarse_blocks, coarse_slots)
    steps = len(grid.steps)
    block_count, slot_count = fine_src.shape
    far_count = slot_count - slot_count * 3 // 4
    table = ((features, node_count), BF16)
    sums_table = ((features, node_count), F32)
    update_table = ((features, 2 * features), BF16)
    aimed_table = ((features, block_count * far_count), BF16)
    far_lists = ((block_count // BATCH, BATCH * far_count), I32)
    halo_outs = [((features, halo_capacity), BF16)] * steps
    two_tables = pltpu.VMEM((2 * features, node_count), BF16)
    prolong_rows = prolong_idx.reshape(node_count // BLOCK, BLOCK)
    big = 1 << 30
    in_hbm = pl.BlockSpec(memory_space=pltpu.HBM)

    (nodes,) = call(
        turn_kernel,
        [table],
        [pltpu.VMEM((node_count, features), BF16), pltpu.SemaphoreType.DMA((PARTS,))],
        name="turn",
        limit=5300 * 10486,
        in_specs=[in_hbm],
    )(fine_nodes)
    sent = call(functools.partial(send_kernel, grid), halo_outs, flops=big, name="send")(
        nodes, halo_send, fine_weights
    )
    halo = swap_dom(grid, sent)
    far_sources, far_places, aimed, sums, update, pool_lists, *packed = call(
        functools.partial(near_kernel, grid),
        [
            far_lists,
            far_lists,
            aimed_table,
            sums_table,
            update_table,
            ((grid.owners, grid.pool_capacity), I32),
            *[((grid.packed_rows, features), BF16)] * grid.packets,
        ],
        [two_tables],
        flops=4 * big,
        name="near",
    )(nodes, fine_src, fine_dst, fine_weights, coarse_src, coarse_dst, coarse_send, pool_send)
    first, *packets = call(
        functools.partial(far_pool_kernel, grid),
        [table, *[((grid.packet, features), BF16)] * grid.packets],
        [two_tables],
        flops=2 * big,
        name="far_pool",
    )(nodes, aimed, far_sources, far_places, sums, update, pool_lists, *packed, *handed(halo, FIRST_ORDER))
    packets = trade_packets(grid, packets)
    (ahead,) = call(
        functools.partial(ahead_kernel, grid), [((features + 16, steps * halo_capacity), BF16)], flops=big, name="ahead"
    )(first, prolong_rows, halo_send)
    lists_scratch = pltpu.VMEM((grid.packed_rows, BLOCK), I32)
    sent = call(
        functools.partial(coarse_send_kernel, grid),
        [((grid.owners * features, grid.coarse_capacity), BF16)] * steps,
        [lists_scratch],
        flops=big // 2,
        name="coarse_send",
    )(coarse_weights, *packets)
    coarse_halo = swap_dom(grid, sent)
    picked, sources, places, rows, weights = call(
        functools.partial(coarse_own_kernel, grid),
        [
            ((grid.owners, features, coarse_slots), F32),
            ((grid.owners, coarse_slots), I32),
            ((grid.owners, coarse_slots), I32),
            ((grid.owners, features, grid.pool_capacity), BF16),
            ((features, 4 * features), BF16),
        ],
        [lists_scratch],
        flops=4 * big,
        name="coarse_own",
    )(coarse_weights, prolong_weight, fine_weights, *packets)
    prolonged, *sent = call(
        functools.partial(lift_halo_kernel, grid),
        [((features, 2 * grid.pooled_rows), BF16), *halo_outs],
        flops=big,
        name="lift_halo",
    )(picked, sources, places, rows, ahead, weights, *coarse_halo)
    halo = swap_dom(grid, sent)
    lifted, aimed, sums, update = call(
        functools.partial(lift_near_kernel, grid),
        [table, aimed_table, sums_table, update_table],
        [two_tables],
        flops=4 * big,
        name="lift_near",
    )(first, prolonged, prolong_rows, fine_src, fine_dst, fine_weights)
    (fine_out,) = call(
        far_kernel,
        [((node_count, features), BF16)],
        [
            two_tables,
            pltpu.VMEM((node_count, features), BF16),
            pltpu.SemaphoreType.DMA((block_count // BATCH,)),
        ],
        flops=2 * big,
        name="far",
        out_specs=(pl.BlockSpec(memory_space=pltpu.HBM),),
    )(lifted, aimed, far_sources, far_places, sums, update, *handed(halo, SECOND_ORDER))
    return fine_out


def solution(mesh):
    split = ("groups", "dom", "sub", "chip")
    return jax.shard_map(
        functools.partial(body, mesh),
        mesh=mesh,
        in_specs=(
            P(split, None),
            P(split, None),
            P(split, None),
            P(split, None, None),
            P(split, None, None),
            P(split, None),
            P(split, None),
            P(split, None, None),
            P(split),
            P(),
            P(),
            P(),
        ),
        out_specs=P(split, None),
        check_vma=False,
    )
```

```python
import functools

import jax
import jax.numpy as jnp
from jax import lax
from jax.experimental import pallas as pl
from jax.experimental.pallas import tpu as pltpu
from jax.sharding import PartitionSpec as P

BF16 = jnp.bfloat16
F32 = jnp.float32
I32 = jnp.int32
BLOCK = 128
VMEM_BYTES = 32 << 20
BATCH = 8
FIRST_ORDER, SECOND_ORDER = (1, 0, 2), (1, 2, 0)
PARTS = 2
PAIR = 1


def dot(left, right):
    return jnp.dot(left, right, preferred_element_type=F32)


def dot_last(left, right):
    return lax.dot_general(left, right, (((1,), (1,)), ((), ())), preferred_element_type=F32)


def rows_hot(index_row, height):
    shape = (height, index_row.shape[1])
    index = jnp.broadcast_to(index_row, shape).astype(jnp.int16)
    return jnp.where(
        index == lax.broadcasted_iota(jnp.int16, shape, 0), jnp.ones((), BF16), jnp.zeros((), BF16)
    )


def silu_of_half(half):
    return half + half * jnp.tanh(half)


def halved(weight):
    return weight * jnp.asarray(0.5, BF16)


class Grid:
    def __init__(self, mesh, halo_capacity, pool_capacity, coarse_capacity, coarse_blocks, slot_count):
        self.dom_count = mesh.shape["dom"]
        self.sub_count = mesh.shape["sub"]
        self.chip_count = mesh.shape["chip"]
        self.places = self.sub_count * self.chip_count
        self.mirrored = self.dom_count == 4
        self.steps = (2, 3, 1) if self.mirrored else (1, self.dom_count - 1, 2)
        self.owners = len(range(0, self.places, 4))
        self.swapped = self.sub_count == 2 and self.chip_count == 2
        self.halo_capacity = halo_capacity
        self.pool_capacity = pool_capacity
        self.coarse_capacity = coarse_capacity
        self.blocks = coarse_blocks
        self.pieces = slot_count // BLOCK
        self.slots = self.places * pool_capacity
        self.pooled_rows = self.owners * pool_capacity
        self.sent_blocks = 1 if self.swapped else coarse_blocks
        self.list_rows = 2 * self.sent_blocks * self.pieces + self.dom_count
        self.packed_rows = -(-self.list_rows // 16) * 16
        self.packet = self.pooled_rows + self.packed_rows
        self.packets = 2 if self.swapped else 1
        self.octaves = -(-(self.slots + self.dom_count * coarse_capacity) // BLOCK)

    def partner(self, dom, step):
        return dom ^ step if self.mirrored else (dom + step) % self.dom_count

    def partner_here(self, step):
        own = lax.axis_index("dom")
        return own ^ step if self.mirrored else lax.rem(own + step, self.dom_count)

    def halo_place(self, source_dom):
        own = lax.axis_index("dom")
        if self.mirrored:
            step = source_dom ^ own
        else:
            step = own - source_dom
            step = jnp.where(step < 0, step + self.dom_count, step)
        place = jnp.zeros_like(step)
        for index, value in enumerate(self.steps):
            place = jnp.where(step == value, index, place)
        return place

    def block_of(self, place):
        return lax.div(place * self.pool_capacity, BLOCK)

    def own_place(self):
        return lax.axis_index("sub") * self.chip_count + lax.axis_index("chip")

    def slot_order(self, slots, place):
        return slots ^ (place * self.pool_capacity) if self.swapped else slots


def handed(halos, order):
    return [halos[turn] for turn in order]


def taken(refs, order):
    return [refs[order.index(turn)] for turn in range(len(refs))]


def turned(weight):
    return halved(weight).T


def turn_kernel(latent_hbm, table_ref, latent_ref, arrived):
    part = latent_ref.shape[0] // PARTS
    copies = []
    for index in range(PARTS):
        rows = pl.ds(index * part, part)
        copies.append(pltpu.make_async_copy(latent_hbm.at[rows], latent_ref.at[rows], arrived.at[index]))
        copies[-1].start()
    for index, copy in enumerate(copies):
        copy.wait()
        rows = slice(index * part, (index + 1) * part)
        table_ref[:, rows] = latent_ref[rows, :].T


def send_kernel(grid, table_ref, lists_ref, weights_ref, *sent_refs):
    index_row = jnp.concatenate([lists_ref[0, pl.ds(grid.partner_here(step), 1), :] for step in grid.steps], axis=1)
    picked = dot(table_ref[...], rows_hot(index_row, table_ref.shape[1])).astype(BF16)
    terms = dot(turned(weights_ref[0, 0]), picked).astype(BF16)
    capacity = lists_ref.shape[2]
    for index, out_ref in enumerate(sent_refs):
        out_ref[...] = terms[:, index * capacity : (index + 1) * capacity]


def far_rows(source_ref, place_ref, batch):
    local_count = source_ref.shape[1] * 3 // 4
    sources, places = [], []
    for index in range(BATCH):
        row = slice(batch * BATCH + index, batch * BATCH + index + 1)
        sources.append(source_ref[row, local_count:])
        place = place_ref[row, local_count:]
        places.append(jnp.where(place >= 0, place + index * BLOCK, -1))
    return jnp.concatenate(sources, axis=1), jnp.concatenate(places, axis=1)


def near_edges(table, source_ref, place_ref, weights_ref, layer, aimed_ref, sums_ref, terms_ref):
    features, node_count = table.shape
    block_count, slot_count = source_ref.shape
    local_count = slot_count * 3 // 4
    window = min(3 * BLOCK, node_count)
    both = jnp.concatenate([turned(weights_ref[layer, 0]), turned(weights_ref[layer, 1])], axis=0)
    terms_ref[...] = dot(both, table).astype(BF16)

    def messages(block):
        start = min(max(block * BLOCK - BLOCK, 0), node_count - window)
        terms = jnp.concatenate(
            [
                terms_ref[:features, start : start + window],
                terms_ref[features:, block * BLOCK : (block + 1) * BLOCK],
            ],
            axis=1,
        )
        places = rows_hot(place_ref[block : block + 1, :], BLOCK)
        sources = rows_hot(source_ref[block : block + 1, :] - start, window)
        picked = dot(terms, jnp.concatenate([sources, places], axis=0))
        far_count = slot_count - local_count
        aimed_ref[:, block * far_count : (block + 1) * far_count] = picked[:, local_count:].astype(BF16)
        return silu_of_half(picked[:, :local_count]).astype(BF16)

    def add_up(block, message):
        places = rows_hot(place_ref[block : block + 1, :local_count], BLOCK)
        sums_ref[:, block * BLOCK : (block + 1) * BLOCK] = dot_last(message, places)

    waiting = None
    for block in range(block_count):
        message = messages(block)
        if waiting is not None:
            add_up(*waiting)
        waiting = (block, message)
    add_up(*waiting)


def near_kernel(
    grid,
    table_ref,
    source_ref,
    place_ref,
    weights_ref,
    coarse_source_ref,
    coarse_place_ref,
    coarse_send_ref,
    pool_ref,
    sources_ref,
    places_ref,
    aimed_ref,
    sums_ref,
    pooled_ref,
    *rest,
):
    packed_refs, terms_ref = rest[:-1], rest[-1]
    table = table_ref[...]
    halo_capacity = grid.halo_capacity
    for batch in range(source_ref.shape[0] // BATCH):
        sources, places = far_rows(source_ref, place_ref, batch)
        slots = sources - table.shape[1]
        source_dom = lax.shift_right_logical(slots, halo_capacity.bit_length() - 1)
        sources_ref[batch : batch + 1, :] = grid.halo_place(source_dom) * halo_capacity + (
            slots & (halo_capacity - 1)
        )
        places_ref[batch : batch + 1, :] = places
    near_edges(table, source_ref, place_ref, weights_ref, 0, aimed_ref, sums_ref, terms_ref)

    place = grid.own_place()
    for index, packed_ref in enumerate(packed_refs):
        if grid.swapped:
            block = grid.block_of(place ^ (2 * index))
            sources, places = coarse_source_ref[pl.ds(block, 1), :], coarse_place_ref[pl.ds(block, 1), :]
        else:
            sources, places = coarse_source_ref[...], coarse_place_ref[...]
        lists = jnp.minimum(coarse_send_ref[0], grid.slots - 1)
        pieces = lane_rows(sources) + [lists] + lane_rows(places + 1)
        spare = grid.packed_rows - grid.list_rows
        if spare:
            pieces.append(jnp.zeros((spare, BLOCK), I32))
        whole = jnp.concatenate(pieces, axis=0)
        coded = lax.shift_left((whole & (BLOCK - 1)) + BLOCK, lax.shift_right_logical(whole, BLOCK.bit_length() - 1))
        packed_ref[...] = coded.astype(F32).astype(BF16)
    for owner in range(grid.owners):
        pooled_ref[owner : owner + 1, :] = pool_ref[0, 4 * owner : 4 * owner + 1, :]


def far_edges(layer, table_ref, aimed_ref, sources_ref, places_ref, sums_ref, weights_ref, halo_refs, both_ref, write):
    features, node_count = table_ref.shape
    batch_count, slot_count = sources_ref.shape
    halo = jnp.concatenate([ref[...] for ref in halo_refs], axis=1)
    update_weights = jnp.concatenate([turned(weights_ref[layer, 2]), turned(weights_ref[layer, 3])], axis=1)
    pair_slots = slot_count * PAIR // BATCH
    pair_rows = PAIR * BLOCK
    batch_rows = BATCH * BLOCK
    both_ref[features:, :] = table_ref[...]

    def messages(batch):
        aimed = aimed_ref[:, batch * slot_count : (batch + 1) * slot_count].astype(F32)
        hot = rows_hot(sources_ref[batch : batch + 1, :], halo.shape[1])
        return silu_of_half(dot(halo, hot) + aimed).astype(BF16)

    def add_up(batch, message):
        for pair in range(BATCH // PAIR):
            slots = slice(pair * pair_slots, (pair + 1) * pair_slots)
            first = batch * batch_rows + pair * pair_rows
            columns = slice(first, first + pair_rows)
            hot = rows_hot(places_ref[batch : batch + 1, slots] - pair * pair_rows, pair_rows)
            both_ref[:features, columns] = (sums_ref[:, columns] + dot_last(message[:, slots], hot)).astype(BF16)

    def update(batch):
        columns = slice(batch * batch_rows, (batch + 1) * batch_rows)
        change = silu_of_half(dot(update_weights, both_ref[:, columns]))
        write(columns, (both_ref[features:, columns].astype(F32) + change).astype(BF16))

    held = [messages(batch) for batch in range(batch_count)]
    for batch in range(batch_count):
        add_up(batch, held[batch])
    for batch in range(batch_count):
        update(batch)


def lane_rows(values):
    pieces = []
    for block in range(values.shape[0]):
        for start in range(0, values.shape[1], BLOCK):
            pieces.append(values[block : block + 1, start : start + BLOCK])
    return pieces


def far_pool_kernel(
    grid, table_ref, aimed_ref, sources_ref, places_ref, sums_ref, weights_ref, pool_ref, *rest
):
    count = grid.packets
    packed_refs, halo_refs = rest[:count], taken(rest[count : count + len(grid.steps)], FIRST_ORDER)
    first_ref, packet_refs, both_ref = rest[-2 - count], rest[-1 - count : -1], rest[-1]

    def write(columns, value):
        first_ref[:, columns] = value

    for packet_ref, packed_ref in zip(packet_refs, packed_refs):
        packet_ref[grid.pooled_rows :, :] = packed_ref[...]
    far_edges(0, table_ref, aimed_ref, sources_ref, places_ref, sums_ref, weights_ref, halo_refs, both_ref, write)
    for owner in range(grid.owners):
        hot = rows_hot(pool_ref[owner : owner + 1, :], first_ref.shape[1])
        pooled = dot(first_ref[...], hot).astype(BF16).T
        for packet_ref in packet_refs:
            packet_ref[owner * grid.pool_capacity : (owner + 1) * grid.pool_capacity, :] = pooled


def far_kernel(table_ref, aimed_ref, sources_ref, places_ref, sums_ref, weights_ref, *rest):
    halo_refs, (out_hbm, both_ref, rows_ref, written) = taken(rest[:-4], SECOND_ORDER), rest[-4:]
    copies = []

    def write(columns, value):
        rows_ref[columns, :] = value.T
        rows = pl.ds(columns.start, columns.stop - columns.start)
        copies.append(pltpu.make_async_copy(rows_ref.at[rows], out_hbm.at[rows], written.at[len(copies)]))
        copies[-1].start()

    far_edges(1, table_ref, aimed_ref, sources_ref, places_ref, sums_ref, weights_ref, halo_refs, both_ref, write)
    for copy in copies:
        copy.wait()


def ahead_kernel(grid, first_ref, prolong_ref, lists_ref, out_ref):
    indices = prolong_ref[...]
    shift = (4 * grid.pool_capacity).bit_length() - 1
    indices = lax.shift_right_logical(indices, shift) * grid.pool_capacity + (indices & (grid.pool_capacity - 1))
    indices = indices.astype(F32)
    row = jnp.concatenate([indices[block : block + 1, :] for block in range(indices.shape[0])], axis=1)
    extra = jnp.concatenate([row, jnp.zeros((15, row.shape[1]), F32)], axis=0).astype(BF16)
    table = jnp.concatenate([first_ref[...], extra], axis=0)
    capacity = lists_ref.shape[2]
    for index, step in enumerate(grid.steps):
        index_row = lists_ref[0, pl.ds(grid.partner_here(step), 1), :]
        picked = dot(table, rows_hot(index_row, table.shape[1]))
        out_ref[:, index * capacity : (index + 1) * capacity] = picked.astype(BF16)


def owner_lists(grid, packets, owner, place):
    if grid.swapped:
        rows = packets[0][grid.pooled_rows :, :].astype(F32)
        for other in range(1, grid.places):
            rows = jnp.where(place == other, packets[other][grid.pooled_rows :, :].astype(F32), rows)
    else:
        rows = packets[4 * owner][grid.pooled_rows :, :].astype(F32)
    coded = rows.astype(I32)
    octave = jnp.zeros_like(coded)
    for power in range(1, grid.octaves):
        octave = octave + jnp.where(coded >= BLOCK << power, 1, 0)
    return octave * BLOCK + lax.shift_right_logical(coded, octave) - BLOCK


def owner_table(grid, packets, owner):
    start = owner * grid.pool_capacity
    return jnp.concatenate([packet[start : start + grid.pool_capacity, :] for packet in packets], axis=0)


def coarse_send_kernel(grid, weights_ref, *refs):
    packets = refs[: grid.places]
    outs = refs[grid.places : grid.places + len(grid.steps)]
    lists_ref = refs[-1]
    place = grid.own_place()
    first_list = grid.sent_blocks * grid.pieces
    capacity = grid.coarse_capacity
    for owner in range(grid.owners):
        lists_ref[...] = owner_lists(grid, packets, owner, place)
        table = owner_table(grid, packets, owner)
        terms = dot(table, halved(weights_ref[0])).astype(BF16).T
        index_row = jnp.concatenate(
            [lists_ref[pl.ds(first_list + grid.partner_here(step), 1), :] for step in grid.steps], axis=1
        )
        picked = dot(terms, rows_hot(grid.slot_order(index_row, place), grid.slots)).astype(BF16)
        for index, out_ref in enumerate(outs):
            out_ref[owner * BLOCK : (owner + 1) * BLOCK, :] = picked[:, index * capacity : (index + 1) * capacity]


def coarse_own_kernel(grid, weights_ref, *refs):
    packets = refs[: grid.places]
    picked_ref, source_out, place_out, rows_out, lists_ref = refs[grid.places :]
    place = grid.own_place()
    first_slot = place * grid.pool_capacity
    block = 0 if grid.swapped else grid.block_of(place)
    within = first_slot & (BLOCK - 1)
    shift = grid.coarse_capacity.bit_length() - 1
    for owner in range(grid.owners):
        lists_ref[...] = owner_lists(grid, packets, owner, place)
        sources = jnp.concatenate(
            [lists_ref[pl.ds(block * grid.pieces + piece, 1), :] for piece in range(grid.pieces)], axis=1
        )
        offset = grid.sent_blocks * grid.pieces + grid.dom_count
        places = jnp.concatenate(
            [lists_ref[pl.ds(offset + block * grid.pieces + piece, 1), :] for piece in range(grid.pieces)], axis=1
        )
        places = places - 1 - within
        places = jnp.where((places >= 0) & (places < grid.pool_capacity), places, -1)
        halo_slots = sources - grid.slots
        source_dom = lax.shift_right_arithmetic(halo_slots, shift)
        halo_sources = grid.halo_place(source_dom) * grid.coarse_capacity + (halo_slots & (grid.coarse_capacity - 1))
        is_halo = halo_slots >= 0
        source_out[owner : owner + 1, :] = jnp.where(is_halo, halo_sources, -1)
        place_out[owner : owner + 1, :] = places
        own_sources = jnp.where(is_halo, -1, grid.slot_order(sources, place))

        table = owner_table(grid, packets, owner)
        rows = table[: grid.pool_capacity]
        if not grid.swapped:
            for other in range(1, grid.places):
                other_rows = table[other * grid.pool_capacity : (other + 1) * grid.pool_capacity]
                rows = jnp.where(place == other, other_rows, rows)
        rows_out[owner] = rows.T
        sender = dot(table, halved(weights_ref[0])).astype(BF16).T
        target = dot(rows, halved(weights_ref[1])).astype(BF16).T
        hot = jnp.concatenate([rows_hot(own_sources, grid.slots), rows_hot(places, grid.pool_capacity)], axis=0)
        picked_ref[owner] = dot(jnp.concatenate([sender, target], axis=1), hot)


def lift(table, prolonged, index_row):
    pooled_rows = prolonged.shape[1] // 2
    hot = rows_hot(index_row, pooled_rows)
    hot = jnp.concatenate([hot, hot], axis=0)
    return (table.astype(F32) + dot(prolonged, hot)).astype(BF16)


def lift_halo_kernel(
    grid,
    picked_ref,
    source_ref,
    place_ref,
    rows_ref,
    ahead_ref,
    coarse_weights_ref,
    prolong_weight_ref,
    weights_ref,
    *rest,
):
    count = len(grid.steps)
    halo_refs, prolonged_ref, sent_refs = rest[:count], rest[count], rest[count + 1 :]
    features = rows_ref.shape[1]
    update_weights = jnp.concatenate([turned(coarse_weights_ref[2]), turned(coarse_weights_ref[3])], axis=1)
    prolong_weight = turned(prolong_weight_ref[...])
    prolonged = []
    for owner in range(grid.owners):
        halo = jnp.concatenate([ref[owner * BLOCK : (owner + 1) * BLOCK, :] for ref in halo_refs], axis=1)
        picked = picked_ref[owner] + dot(halo, rows_hot(source_ref[owner : owner + 1, :], halo.shape[1]))
        message = silu_of_half(picked).astype(BF16)
        places = rows_hot(place_ref[owner : owner + 1, :], grid.pool_capacity)
        summed = dot_last(message, places).astype(BF16)
        rows = rows_ref[owner]
        update = dot(update_weights, jnp.concatenate([summed, rows], axis=0))
        coarse = (rows.astype(F32) + silu_of_half(update)).astype(BF16)
        prolonged.append(silu_of_half(dot(prolong_weight, coarse)))
    prolonged = jnp.concatenate(prolonged, axis=1)
    high = prolonged.astype(BF16)
    low = (prolonged - high.astype(F32)).astype(BF16)
    parts = jnp.concatenate([high, low], axis=1)
    prolonged_ref[...] = parts
    weight = turned(weights_ref[1, 0])
    index_row = ahead_ref[features : features + 16, :].astype(F32).astype(I32)[:1]
    lifted = lift(ahead_ref[:features, :], parts, index_row)
    terms = dot(weight, lifted).astype(BF16)
    capacity = sent_refs[0].shape[1]
    for index, out_ref in enumerate(sent_refs):
        out_ref[...] = terms[:, index * capacity : (index + 1) * capacity]


def lift_near_kernel(
    grid,
    first_ref,
    prolonged_ref,
    prolong_ref,
    source_ref,
    place_ref,
    weights_ref,
    lifted_ref,
    aimed_ref,
    sums_ref,
    terms_ref,
):
    indices = prolong_ref[...]
    shift = (4 * grid.pool_capacity).bit_length() - 1
    indices = lax.shift_right_logical(indices, shift) * grid.pool_capacity + (indices & (grid.pool_capacity - 1))
    row = jnp.concatenate([indices[block : block + 1, :] for block in range(indices.shape[0])], axis=1)
    lifted = lift(first_ref[...], prolonged_ref[...], row)
    lifted_ref[...] = lifted
    near_edges(lifted, source_ref, place_ref, weights_ref, 1, aimed_ref, sums_ref, terms_ref)


def call(kernel, outs, scratch=(), flops=0, name=None, limit=VMEM_BYTES, **specs):
    return pl.pallas_call(
        kernel,
        out_shape=tuple(jax.ShapeDtypeStruct(shape, dtype) for shape, dtype in outs),
        scratch_shapes=list(scratch),
        compiler_params=pltpu.CompilerParams(vmem_limit_bytes=limit),
        cost_estimate=pl.CostEstimate(flops=flops, bytes_accessed=4 << 20, transcendentals=0),
        name=name,
        **specs,
    )


def swap_dom(grid, arrays):
    return [
        lax.ppermute(array, "dom", [(dom, grid.partner(dom, step)) for dom in range(grid.dom_count)])
        for array, step in zip(arrays, grid.steps)
    ]


def trade_packets(grid, packets):
    if grid.swapped:
        pairs = [(0, 1), (1, 0)]
        near, far = packets
        over = lax.ppermute(far, "sub", pairs)
        across = lax.ppermute(near, "chip", pairs)
        both = lax.ppermute(far, ("sub", "chip"), [(0, 3), (1, 2), (2, 1), (3, 0)])
        return [near, across, over, both]
    gathered = lax.all_gather(packets[0], ("sub", "chip"), axis=0, tiled=False)
    return [gathered[place] for place in range(grid.places)]


def body(
    mesh,
    fine_nodes,
    fine_src,
    fine_dst,
    halo_send,
    pool_send,
    coarse_src,
    coarse_dst,
    coarse_send,
    prolong_idx,
    fine_weights,
    coarse_weights,
    prolong_weight,
):
    node_count, features = fine_nodes.shape
    halo_capacity = halo_send.shape[2]
    coarse_blocks, coarse_slots = coarse_src.shape
    grid = Grid(mesh, halo_capacity, pool_send.shape[2], coarse_send.shape[2], coarse_blocks, coarse_slots)
    steps = len(grid.steps)
    block_count, slot_count = fine_src.shape
    far_count = slot_count - slot_count * 3 // 4
    table = ((features, node_count), BF16)
    sums_table = ((features, node_count), F32)
    aimed_table = ((features, block_count * far_count), BF16)
    far_lists = ((block_count // BATCH, BATCH * far_count), I32)
    halo_outs = [((features, halo_capacity), BF16)] * steps
    two_tables = pltpu.VMEM((2 * features, node_count), BF16)
    prolong_rows = prolong_idx.reshape(node_count // BLOCK, BLOCK)
    big = 1 << 30
    in_hbm = pl.BlockSpec(memory_space=pltpu.HBM)

    (nodes,) = call(
        turn_kernel,
        [table],
        [pltpu.VMEM((node_count, features), BF16), pltpu.SemaphoreType.DMA((PARTS,))],
        name="turn",
        limit=5300 * 10486,
        in_specs=[in_hbm],
    )(fine_nodes)
    sent = call(functools.partial(send_kernel, grid), halo_outs, flops=big, name="send")(
        nodes, halo_send, fine_weights
    )
    halo = swap_dom(grid, sent)
    far_sources, far_places, aimed, sums, pool_lists, *packed = call(
        functools.partial(near_kernel, grid),
        [
            far_lists,
            far_lists,
            aimed_table,
            sums_table,
            ((grid.owners, grid.pool_capacity), I32),
            *[((grid.packed_rows, features), BF16)] * grid.packets,
        ],
        [two_tables],
        flops=4 * big,
        name="near",
    )(nodes, fine_src, fine_dst, fine_weights, coarse_src, coarse_dst, coarse_send, pool_send)
    first, *packets = call(
        functools.partial(far_pool_kernel, grid),
        [table, *[((grid.packet, features), BF16)] * grid.packets],
        [two_tables],
        flops=2 * big,
        name="far_pool",
    )(nodes, aimed, far_sources, far_places, sums, fine_weights, pool_lists, *packed, *handed(halo, FIRST_ORDER))
    packets = trade_packets(grid, packets)
    (ahead,) = call(
        functools.partial(ahead_kernel, grid), [((features + 16, steps * halo_capacity), BF16)], flops=big, name="ahead"
    )(first, prolong_rows, halo_send)
    lists_scratch = pltpu.VMEM((grid.packed_rows, BLOCK), I32)
    sent = call(
        functools.partial(coarse_send_kernel, grid),
        [((grid.owners * features, grid.coarse_capacity), BF16)] * steps,
        [lists_scratch],
        flops=big // 2,
        name="coarse_send",
    )(coarse_weights, *packets)
    coarse_halo = swap_dom(grid, sent)
    picked, sources, places, rows = call(
        functools.partial(coarse_own_kernel, grid),
        [
            ((grid.owners, features, coarse_slots), F32),
            ((grid.owners, coarse_slots), I32),
            ((grid.owners, coarse_slots), I32),
            ((grid.owners, features, grid.pool_capacity), BF16),
        ],
        [lists_scratch],
        flops=4 * big,
        name="coarse_own",
    )(coarse_weights, *packets)
    prolonged, *sent = call(
        functools.partial(lift_halo_kernel, grid),
        [((features, 2 * grid.pooled_rows), BF16), *halo_outs],
        flops=big,
        name="lift_halo",
    )(picked, sources, places, rows, ahead, coarse_weights, prolong_weight, fine_weights, *coarse_halo)
    halo = swap_dom(grid, sent)
    lifted, aimed, sums = call(
        functools.partial(lift_near_kernel, grid),
        [table, aimed_table, sums_table],
        [two_tables],
        flops=4 * big,
        name="lift_near",
    )(first, prolonged, prolong_rows, fine_src, fine_dst, fine_weights)
    (fine_out,) = call(
        far_kernel,
        [((node_count, features), BF16)],
        [
            two_tables,
            pltpu.VMEM((node_count, features), BF16),
            pltpu.SemaphoreType.DMA((block_count // BATCH,)),
        ],
        flops=2 * big,
        name="far",
        out_specs=(pl.BlockSpec(memory_space=pltpu.HBM),),
    )(lifted, aimed, far_sources, far_places, sums, fine_weights, *handed(halo, SECOND_ORDER))
    return fine_out


def solution(mesh):
    split = ("groups", "dom", "sub", "chip")
    return jax.shard_map(
        functools.partial(body, mesh),
        mesh=mesh,
        in_specs=(
            P(split, None),
            P(split, None),
            P(split, None),
            P(split, None, None),
            P(split, None, None),
            P(split, None),
            P(split, None),
            P(split, None, None),
            P(split),
            P(),
            P(),
            P(),
        ),
        out_specs=P(split, None),
        check_vma=False,
    )
```

```python
import functools

import jax
import jax.numpy as jnp
from jax import lax
from jax.experimental import pallas as pl
from jax.experimental.pallas import tpu as pltpu
from jax.sharding import PartitionSpec as P

BF16 = jnp.bfloat16
F32 = jnp.float32
I32 = jnp.int32
BLOCK = 128
VMEM_BYTES = 32 << 20
BATCH = 8
FIRST_ORDER, SECOND_ORDER = (1, 0, 2), (1, 2, 0)
PARTS = 2
PAIR = 1


def dot(left, right):
    return jnp.dot(left, right, preferred_element_type=F32)


def dot_last(left, right):
    return lax.dot_general(left, right, (((1,), (1,)), ((), ())), preferred_element_type=F32)


def rows_hot(index_row, height):
    shape = (height, index_row.shape[1])
    index = jnp.broadcast_to(index_row, shape).astype(jnp.int16)
    return jnp.where(
        index == lax.broadcasted_iota(jnp.int16, shape, 0), jnp.ones((), BF16), jnp.zeros((), BF16)
    )


def silu_of_half(half):
    return half + half * jnp.tanh(half)


def halved(weight):
    return weight * jnp.asarray(0.5, BF16)


class Grid:
    def __init__(self, mesh, halo_capacity, pool_capacity, coarse_capacity, coarse_blocks, slot_count):
        self.dom_count = mesh.shape["dom"]
        self.sub_count = mesh.shape["sub"]
        self.chip_count = mesh.shape["chip"]
        self.places = self.sub_count * self.chip_count
        self.mirrored = self.dom_count == 4
        self.steps = (2, 3, 1) if self.mirrored else (1, self.dom_count - 1, 2)
        self.owners = len(range(0, self.places, 4))
        self.swapped = self.sub_count == 2 and self.chip_count == 2
        self.halo_capacity = halo_capacity
        self.pool_capacity = pool_capacity
        self.coarse_capacity = coarse_capacity
        self.blocks = coarse_blocks
        self.pieces = slot_count // BLOCK
        self.slots = self.places * pool_capacity
        self.pooled_rows = self.owners * pool_capacity
        self.sent_blocks = 1 if self.swapped else coarse_blocks
        self.list_rows = 2 * self.sent_blocks * self.pieces + self.dom_count
        self.packed_rows = -(-self.list_rows // 16) * 16
        self.packet = self.pooled_rows + self.packed_rows
        self.packets = 2 if self.swapped else 1
        self.octaves = -(-(self.slots + self.dom_count * coarse_capacity) // BLOCK)

    def partner(self, dom, step):
        return dom ^ step if self.mirrored else (dom + step) % self.dom_count

    def partner_here(self, step):
        own = lax.axis_index("dom")
        return own ^ step if self.mirrored else lax.rem(own + step, self.dom_count)

    def halo_place(self, source_dom):
        own = lax.axis_index("dom")
        if self.mirrored:
            step = source_dom ^ own
        else:
            step = own - source_dom
            step = jnp.where(step < 0, step + self.dom_count, step)
        place = jnp.zeros_like(step)
        for index, value in enumerate(self.steps):
            place = jnp.where(step == value, index, place)
        return place

    def block_of(self, place):
        return lax.div(place * self.pool_capacity, BLOCK)

    def own_place(self):
        return lax.axis_index("sub") * self.chip_count + lax.axis_index("chip")

    def slot_order(self, slots, place):
        return slots ^ (place * self.pool_capacity) if self.swapped else slots


def handed(halos, order):
    return [halos[turn] for turn in order]


def taken(refs, order):
    return [refs[order.index(turn)] for turn in range(len(refs))]


def turned(weight):
    return halved(weight).T


def turn_kernel(latent_hbm, table_ref, latent_ref, arrived):
    part = latent_ref.shape[0] // PARTS
    copies = []
    for index in range(PARTS):
        rows = pl.ds(index * part, part)
        copies.append(pltpu.make_async_copy(latent_hbm.at[rows], latent_ref.at[rows], arrived.at[index]))
        copies[-1].start()
    for index, copy in enumerate(copies):
        copy.wait()
        rows = slice(index * part, (index + 1) * part)
        table_ref[:, rows] = latent_ref[rows, :].T


def send_kernel(grid, table_ref, lists_ref, weights_ref, *sent_refs):
    index_row = jnp.concatenate([lists_ref[0, pl.ds(grid.partner_here(step), 1), :] for step in grid.steps], axis=1)
    picked = dot(table_ref[...], rows_hot(index_row, table_ref.shape[1])).astype(BF16)
    terms = dot(turned(weights_ref[0, 0]), picked).astype(BF16)
    capacity = lists_ref.shape[2]
    for index, out_ref in enumerate(sent_refs):
        out_ref[...] = terms[:, index * capacity : (index + 1) * capacity]


def far_rows(source_ref, place_ref, batch):
    local_count = source_ref.shape[1] * 3 // 4
    sources, places = [], []
    for index in range(BATCH):
        row = slice(batch * BATCH + index, batch * BATCH + index + 1)
        sources.append(source_ref[row, local_count:])
        place = place_ref[row, local_count:]
        places.append(jnp.where(place >= 0, place + index * BLOCK, -1))
    return jnp.concatenate(sources, axis=1), jnp.concatenate(places, axis=1)


def near_edges(table, source_ref, place_ref, weights_ref, layer, aimed_ref, sums_ref, terms_ref):
    features, node_count = table.shape
    block_count, slot_count = source_ref.shape
    local_count = slot_count * 3 // 4
    window = min(3 * BLOCK, node_count)
    both = jnp.concatenate([turned(weights_ref[layer, 0]), turned(weights_ref[layer, 1])], axis=0)
    terms_ref[...] = dot(both, table).astype(BF16)

    def messages(block):
        start = min(max(block * BLOCK - BLOCK, 0), node_count - window)
        terms = jnp.concatenate(
            [
                terms_ref[:features, start : start + window],
                terms_ref[features:, block * BLOCK : (block + 1) * BLOCK],
            ],
            axis=1,
        )
        places = rows_hot(place_ref[block : block + 1, :], BLOCK)
        sources = rows_hot(source_ref[block : block + 1, :] - start, window)
        picked = dot(terms, jnp.concatenate([sources, places], axis=0))
        far_count = slot_count - local_count
        aimed_ref[:, block * far_count : (block + 1) * far_count] = picked[:, local_count:].astype(BF16)
        return silu_of_half(picked[:, :local_count]).astype(BF16)

    def add_up(block, message):
        places = rows_hot(place_ref[block : block + 1, :local_count], BLOCK)
        sums_ref[:, block * BLOCK : (block + 1) * BLOCK] = dot_last(message, places)

    waiting = []
    for block in range(block_count):
        waiting.append((block, messages(block)))
        if len(waiting) > 16:
            add_up(*waiting.pop(0))
    for held in waiting:
        add_up(*held)


def near_kernel(
    grid,
    table_ref,
    source_ref,
    place_ref,
    weights_ref,
    coarse_source_ref,
    coarse_place_ref,
    coarse_send_ref,
    pool_ref,
    sources_ref,
    places_ref,
    aimed_ref,
    sums_ref,
    pooled_ref,
    *rest,
):
    packed_refs, terms_ref = rest[:-1], rest[-1]
    table = table_ref[...]
    halo_capacity = grid.halo_capacity
    for batch in range(source_ref.shape[0] // BATCH):
        sources, places = far_rows(source_ref, place_ref, batch)
        slots = sources - table.shape[1]
        source_dom = lax.shift_right_logical(slots, halo_capacity.bit_length() - 1)
        sources_ref[batch : batch + 1, :] = grid.halo_place(source_dom) * halo_capacity + (
            slots & (halo_capacity - 1)
        )
        places_ref[batch : batch + 1, :] = places
    near_edges(table, source_ref, place_ref, weights_ref, 0, aimed_ref, sums_ref, terms_ref)

    place = grid.own_place()
    for index, packed_ref in enumerate(packed_refs):
        if grid.swapped:
            block = grid.block_of(place ^ (2 * index))
            sources, places = coarse_source_ref[pl.ds(block, 1), :], coarse_place_ref[pl.ds(block, 1), :]
        else:
            sources, places = coarse_source_ref[...], coarse_place_ref[...]
        lists = jnp.minimum(coarse_send_ref[0], grid.slots - 1)
        pieces = lane_rows(sources) + [lists] + lane_rows(places + 1)
        spare = grid.packed_rows - grid.list_rows
        if spare:
            pieces.append(jnp.zeros((spare, BLOCK), I32))
        whole = jnp.concatenate(pieces, axis=0)
        coded = lax.shift_left((whole & (BLOCK - 1)) + BLOCK, lax.shift_right_logical(whole, BLOCK.bit_length() - 1))
        packed_ref[...] = coded.astype(F32).astype(BF16)
    for owner in range(grid.owners):
        pooled_ref[owner : owner + 1, :] = pool_ref[0, 4 * owner : 4 * owner + 1, :]


def far_edges(layer, table_ref, aimed_ref, sources_ref, places_ref, sums_ref, weights_ref, halo_refs, both_ref, write):
    features, node_count = table_ref.shape
    batch_count, slot_count = sources_ref.shape
    halo = jnp.concatenate([ref[...] for ref in halo_refs], axis=1)
    update_weights = jnp.concatenate([turned(weights_ref[layer, 2]), turned(weights_ref[layer, 3])], axis=1)
    pair_slots = slot_count * PAIR // BATCH
    pair_rows = PAIR * BLOCK
    batch_rows = BATCH * BLOCK
    both_ref[features:, :] = table_ref[...]

    def messages(batch):
        aimed = aimed_ref[:, batch * slot_count : (batch + 1) * slot_count].astype(F32)
        hot = rows_hot(sources_ref[batch : batch + 1, :], halo.shape[1])
        return silu_of_half(dot(halo, hot) + aimed).astype(BF16)

    def add_up(batch, message):
        for pair in range(BATCH // PAIR):
            slots = slice(pair * pair_slots, (pair + 1) * pair_slots)
            first = batch * batch_rows + pair * pair_rows
            columns = slice(first, first + pair_rows)
            hot = rows_hot(places_ref[batch : batch + 1, slots] - pair * pair_rows, pair_rows)
            both_ref[:features, columns] = (sums_ref[:, columns] + dot_last(message[:, slots], hot)).astype(BF16)

    def update(batch):
        columns = slice(batch * batch_rows, (batch + 1) * batch_rows)
        change = silu_of_half(dot(update_weights, both_ref[:, columns]))
        write(columns, (both_ref[features:, columns].astype(F32) + change).astype(BF16))

    held = [messages(batch) for batch in range(batch_count)]
    for batch in range(batch_count):
        add_up(batch, held[batch])
    for batch in range(batch_count):
        update(batch)


def lane_rows(values):
    pieces = []
    for block in range(values.shape[0]):
        for start in range(0, values.shape[1], BLOCK):
            pieces.append(values[block : block + 1, start : start + BLOCK])
    return pieces


def far_pool_kernel(
    grid, table_ref, aimed_ref, sources_ref, places_ref, sums_ref, weights_ref, pool_ref, *rest
):
    count = grid.packets
    packed_refs, halo_refs = rest[:count], taken(rest[count : count + len(grid.steps)], FIRST_ORDER)
    first_ref, packet_refs, both_ref = rest[-2 - count], rest[-1 - count : -1], rest[-1]

    def write(columns, value):
        first_ref[:, columns] = value

    for packet_ref, packed_ref in zip(packet_refs, packed_refs):
        packet_ref[grid.pooled_rows :, :] = packed_ref[...]
    far_edges(0, table_ref, aimed_ref, sources_ref, places_ref, sums_ref, weights_ref, halo_refs, both_ref, write)
    for owner in range(grid.owners):
        hot = rows_hot(pool_ref[owner : owner + 1, :], first_ref.shape[1])
        pooled = dot(first_ref[...], hot).astype(BF16).T
        for packet_ref in packet_refs:
            packet_ref[owner * grid.pool_capacity : (owner + 1) * grid.pool_capacity, :] = pooled


def far_kernel(table_ref, aimed_ref, sources_ref, places_ref, sums_ref, weights_ref, *rest):
    halo_refs, (out_hbm, both_ref, rows_ref, written) = taken(rest[:-4], SECOND_ORDER), rest[-4:]
    copies = []

    def write(columns, value):
        rows_ref[columns, :] = value.T
        rows = pl.ds(columns.start, columns.stop - columns.start)
        copies.append(pltpu.make_async_copy(rows_ref.at[rows], out_hbm.at[rows], written.at[len(copies)]))
        copies[-1].start()

    far_edges(1, table_ref, aimed_ref, sources_ref, places_ref, sums_ref, weights_ref, halo_refs, both_ref, write)
    for copy in copies:
        copy.wait()


def ahead_kernel(grid, first_ref, prolong_ref, lists_ref, out_ref):
    indices = prolong_ref[...]
    shift = (4 * grid.pool_capacity).bit_length() - 1
    indices = lax.shift_right_logical(indices, shift) * grid.pool_capacity + (indices & (grid.pool_capacity - 1))
    indices = indices.astype(F32)
    row = jnp.concatenate([indices[block : block + 1, :] for block in range(indices.shape[0])], axis=1)
    extra = jnp.concatenate([row, jnp.zeros((15, row.shape[1]), F32)], axis=0).astype(BF16)
    table = jnp.concatenate([first_ref[...], extra], axis=0)
    capacity = lists_ref.shape[2]
    for index, step in enumerate(grid.steps):
        index_row = lists_ref[0, pl.ds(grid.partner_here(step), 1), :]
        picked = dot(table, rows_hot(index_row, table.shape[1]))
        out_ref[:, index * capacity : (index + 1) * capacity] = picked.astype(BF16)


def owner_lists(grid, packets, owner, place):
    if grid.swapped:
        rows = packets[0][grid.pooled_rows :, :].astype(F32)
        for other in range(1, grid.places):
            rows = jnp.where(place == other, packets[other][grid.pooled_rows :, :].astype(F32), rows)
    else:
        rows = packets[4 * owner][grid.pooled_rows :, :].astype(F32)
    coded = rows.astype(I32)
    octave = jnp.zeros_like(coded)
    for power in range(1, grid.octaves):
        octave = octave + jnp.where(coded >= BLOCK << power, 1, 0)
    return octave * BLOCK + lax.shift_right_logical(coded, octave) - BLOCK


def owner_table(grid, packets, owner):
    start = owner * grid.pool_capacity
    return jnp.concatenate([packet[start : start + grid.pool_capacity, :] for packet in packets], axis=0)


def coarse_send_kernel(grid, weights_ref, *refs):
    packets = refs[: grid.places]
    outs = refs[grid.places : grid.places + len(grid.steps)]
    lists_ref = refs[-1]
    place = grid.own_place()
    first_list = grid.sent_blocks * grid.pieces
    capacity = grid.coarse_capacity
    for owner in range(grid.owners):
        lists_ref[...] = owner_lists(grid, packets, owner, place)
        table = owner_table(grid, packets, owner)
        terms = dot(table, halved(weights_ref[0])).astype(BF16).T
        index_row = jnp.concatenate(
            [lists_ref[pl.ds(first_list + grid.partner_here(step), 1), :] for step in grid.steps], axis=1
        )
        picked = dot(terms, rows_hot(grid.slot_order(index_row, place), grid.slots)).astype(BF16)
        for index, out_ref in enumerate(outs):
            out_ref[owner * BLOCK : (owner + 1) * BLOCK, :] = picked[:, index * capacity : (index + 1) * capacity]


def coarse_own_kernel(grid, weights_ref, *refs):
    packets = refs[: grid.places]
    picked_ref, source_out, place_out, rows_out, lists_ref = refs[grid.places :]
    place = grid.own_place()
    first_slot = place * grid.pool_capacity
    block = 0 if grid.swapped else grid.block_of(place)
    within = first_slot & (BLOCK - 1)
    shift = grid.coarse_capacity.bit_length() - 1
    for owner in range(grid.owners):
        lists_ref[...] = owner_lists(grid, packets, owner, place)
        sources = jnp.concatenate(
            [lists_ref[pl.ds(block * grid.pieces + piece, 1), :] for piece in range(grid.pieces)], axis=1
        )
        offset = grid.sent_blocks * grid.pieces + grid.dom_count
        places = jnp.concatenate(
            [lists_ref[pl.ds(offset + block * grid.pieces + piece, 1), :] for piece in range(grid.pieces)], axis=1
        )
        places = places - 1 - within
        places = jnp.where((places >= 0) & (places < grid.pool_capacity), places, -1)
        halo_slots = sources - grid.slots
        source_dom = lax.shift_right_arithmetic(halo_slots, shift)
        halo_sources = grid.halo_place(source_dom) * grid.coarse_capacity + (halo_slots & (grid.coarse_capacity - 1))
        is_halo = halo_slots >= 0
        source_out[owner] = rows_hot(jnp.where(is_halo, halo_sources, -1), source_out.shape[1])
        place_out[owner] = rows_hot(places, grid.pool_capacity)
        own_sources = jnp.where(is_halo, -1, grid.slot_order(sources, place))

        table = owner_table(grid, packets, owner)
        rows = table[: grid.pool_capacity]
        if not grid.swapped:
            for other in range(1, grid.places):
                other_rows = table[other * grid.pool_capacity : (other + 1) * grid.pool_capacity]
                rows = jnp.where(place == other, other_rows, rows)
        rows_out[owner] = rows.T
        sender = dot(table, halved(weights_ref[0])).astype(BF16).T
        target = dot(rows, halved(weights_ref[1])).astype(BF16).T
        hot = jnp.concatenate([rows_hot(own_sources, grid.slots), rows_hot(places, grid.pool_capacity)], axis=0)
        picked_ref[owner] = dot(jnp.concatenate([sender, target], axis=1), hot)


def lift(table, prolonged, index_row):
    pooled_rows = prolonged.shape[1] // 2
    hot = rows_hot(index_row, pooled_rows)
    hot = jnp.concatenate([hot, hot], axis=0)
    return (table.astype(F32) + dot(prolonged, hot)).astype(BF16)


def lift_halo_kernel(
    grid,
    picked_ref,
    source_ref,
    place_ref,
    rows_ref,
    ahead_ref,
    coarse_weights_ref,
    prolong_weight_ref,
    weights_ref,
    *rest,
):
    count = len(grid.steps)
    halo_refs, prolonged_ref, sent_refs = rest[:count], rest[count], rest[count + 1 :]
    features = rows_ref.shape[1]
    update_weights = jnp.concatenate([turned(coarse_weights_ref[2]), turned(coarse_weights_ref[3])], axis=1)
    prolong_weight = turned(prolong_weight_ref[...])
    prolonged = []
    for owner in range(grid.owners):
        halo = jnp.concatenate([ref[owner * BLOCK : (owner + 1) * BLOCK, :] for ref in halo_refs], axis=1)
        picked = picked_ref[owner] + dot(halo, source_ref[owner])
        message = silu_of_half(picked).astype(BF16)
        places = place_ref[owner]
        summed = dot_last(message, places).astype(BF16)
        rows = rows_ref[owner]
        update = dot(update_weights, jnp.concatenate([summed, rows], axis=0))
        coarse = (rows.astype(F32) + silu_of_half(update)).astype(BF16)
        prolonged.append(silu_of_half(dot(prolong_weight, coarse)))
    prolonged = jnp.concatenate(prolonged, axis=1)
    high = prolonged.astype(BF16)
    low = (prolonged - high.astype(F32)).astype(BF16)
    parts = jnp.concatenate([high, low], axis=1)
    prolonged_ref[...] = parts
    weight = turned(weights_ref[1, 0])
    index_row = ahead_ref[features : features + 16, :].astype(F32).astype(I32)[:1]
    lifted = lift(ahead_ref[:features, :], parts, index_row)
    terms = dot(weight, lifted).astype(BF16)
    capacity = sent_refs[0].shape[1]
    for index, out_ref in enumerate(sent_refs):
        out_ref[...] = terms[:, index * capacity : (index + 1) * capacity]


def lift_near_kernel(
    grid,
    first_ref,
    prolonged_ref,
    prolong_ref,
    source_ref,
    place_ref,
    weights_ref,
    lifted_ref,
    aimed_ref,
    sums_ref,
    terms_ref,
):
    indices = prolong_ref[...]
    shift = (4 * grid.pool_capacity).bit_length() - 1
    indices = lax.shift_right_logical(indices, shift) * grid.pool_capacity + (indices & (grid.pool_capacity - 1))
    row = jnp.concatenate([indices[block : block + 1, :] for block in range(indices.shape[0])], axis=1)
    lifted = lift(first_ref[...], prolonged_ref[...], row)
    lifted_ref[...] = lifted
    near_edges(lifted, source_ref, place_ref, weights_ref, 1, aimed_ref, sums_ref, terms_ref)


def call(kernel, outs, scratch=(), flops=0, name=None, limit=VMEM_BYTES, **specs):
    return pl.pallas_call(
        kernel,
        out_shape=tuple(jax.ShapeDtypeStruct(shape, dtype) for shape, dtype in outs),
        scratch_shapes=list(scratch),
        compiler_params=pltpu.CompilerParams(vmem_limit_bytes=limit),
        cost_estimate=pl.CostEstimate(flops=flops, bytes_accessed=4 << 20, transcendentals=0),
        name=name,
        **specs,
    )


def swap_dom(grid, arrays):
    return [
        lax.ppermute(array, "dom", [(dom, grid.partner(dom, step)) for dom in range(grid.dom_count)])
        for array, step in zip(arrays, grid.steps)
    ]


def trade_packets(grid, packets):
    if grid.swapped:
        pairs = [(0, 1), (1, 0)]
        near, far = packets
        over = lax.ppermute(far, "sub", pairs)
        across = lax.ppermute(near, "chip", pairs)
        both = lax.ppermute(far, ("sub", "chip"), [(0, 3), (1, 2), (2, 1), (3, 0)])
        return [near, across, over, both]
    gathered = lax.all_gather(packets[0], ("sub", "chip"), axis=0, tiled=False)
    return [gathered[place] for place in range(grid.places)]


def body(
    mesh,
    fine_nodes,
    fine_src,
    fine_dst,
    halo_send,
    pool_send,
    coarse_src,
    coarse_dst,
    coarse_send,
    prolong_idx,
    fine_weights,
    coarse_weights,
    prolong_weight,
):
    node_count, features = fine_nodes.shape
    halo_capacity = halo_send.shape[2]
    coarse_blocks, coarse_slots = coarse_src.shape
    grid = Grid(mesh, halo_capacity, pool_send.shape[2], coarse_send.shape[2], coarse_blocks, coarse_slots)
    steps = len(grid.steps)
    block_count, slot_count = fine_src.shape
    far_count = slot_count - slot_count * 3 // 4
    table = ((features, node_count), BF16)
    sums_table = ((features, node_count), F32)
    aimed_table = ((features, block_count * far_count), BF16)
    far_lists = ((block_count // BATCH, BATCH * far_count), I32)
    halo_outs = [((features, halo_capacity), BF16)] * steps
    two_tables = pltpu.VMEM((2 * features, node_count), BF16)
    prolong_rows = prolong_idx.reshape(node_count // BLOCK, BLOCK)
    big = 1 << 30
    in_hbm = pl.BlockSpec(memory_space=pltpu.HBM)

    (nodes,) = call(
        turn_kernel,
        [table],
        [pltpu.VMEM((node_count, features), BF16), pltpu.SemaphoreType.DMA((PARTS,))],
        name="turn",
        limit=5300 * 10486,
        in_specs=[in_hbm],
    )(fine_nodes)
    sent = call(functools.partial(send_kernel, grid), halo_outs, flops=big, name="send")(
        nodes, halo_send, fine_weights
    )
    halo = swap_dom(grid, sent)
    far_sources, far_places, aimed, sums, pool_lists, *packed = call(
        functools.partial(near_kernel, grid),
        [
            far_lists,
            far_lists,
            aimed_table,
            sums_table,
            ((grid.owners, grid.pool_capacity), I32),
            *[((grid.packed_rows, features), BF16)] * grid.packets,
        ],
        [two_tables],
        flops=4 * big,
        name="near",
    )(nodes, fine_src, fine_dst, fine_weights, coarse_src, coarse_dst, coarse_send, pool_send)
    first, *packets = call(
        functools.partial(far_pool_kernel, grid),
        [table, *[((grid.packet, features), BF16)] * grid.packets],
        [two_tables],
        flops=2 * big,
        name="far_pool",
    )(nodes, aimed, far_sources, far_places, sums, fine_weights, pool_lists, *packed, *handed(halo, FIRST_ORDER))
    packets = trade_packets(grid, packets)
    (ahead,) = call(
        functools.partial(ahead_kernel, grid), [((features + 16, steps * halo_capacity), BF16)], flops=big, name="ahead"
    )(first, prolong_rows, halo_send)
    lists_scratch = pltpu.VMEM((grid.packed_rows, BLOCK), I32)
    sent = call(
        functools.partial(coarse_send_kernel, grid),
        [((grid.owners * features, grid.coarse_capacity), BF16)] * steps,
        [lists_scratch],
        flops=big // 2,
        name="coarse_send",
    )(coarse_weights, *packets)
    coarse_halo = swap_dom(grid, sent)
    picked, sources, places, rows = call(
        functools.partial(coarse_own_kernel, grid),
        [
            ((grid.owners, features, coarse_slots), F32),
            ((grid.owners, steps * grid.coarse_capacity, coarse_slots), BF16),
            ((grid.owners, grid.pool_capacity, coarse_slots), BF16),
            ((grid.owners, features, grid.pool_capacity), BF16),
        ],
        [lists_scratch],
        flops=4 * big,
        name="coarse_own",
    )(coarse_weights, *packets)
    prolonged, *sent = call(
        functools.partial(lift_halo_kernel, grid),
        [((features, 2 * grid.pooled_rows), BF16), *halo_outs],
        flops=big,
        name="lift_halo",
    )(picked, sources, places, rows, ahead, coarse_weights, prolong_weight, fine_weights, *coarse_halo)
    halo = swap_dom(grid, sent)
    lifted, aimed, sums = call(
        functools.partial(lift_near_kernel, grid),
        [table, aimed_table, sums_table],
        [two_tables],
        flops=4 * big,
        name="lift_near",
    )(first, prolonged, prolong_rows, fine_src, fine_dst, fine_weights)
    (fine_out,) = call(
        far_kernel,
        [((node_count, features), BF16)],
        [
            two_tables,
            pltpu.VMEM((node_count, features), BF16),
            pltpu.SemaphoreType.DMA((block_count // BATCH,)),
        ],
        flops=2 * big,
        name="far",
        out_specs=(pl.BlockSpec(memory_space=pltpu.HBM),),
    )(lifted, aimed, far_sources, far_places, sums, fine_weights, *handed(halo, SECOND_ORDER))
    return fine_out


def solution(mesh):
    split = ("groups", "dom", "sub", "chip")
    return jax.shard_map(
        functools.partial(body, mesh),
        mesh=mesh,
        in_specs=(
            P(split, None),
            P(split, None),
            P(split, None),
            P(split, None, None),
            P(split, None, None),
            P(split, None),
            P(split, None),
            P(split, None, None),
            P(split),
            P(),
            P(),
            P(),
        ),
        out_specs=P(split, None),
        check_vma=False,
    )
```

```python
import functools

import jax
import jax.numpy as jnp
from jax import lax
from jax.experimental import pallas as pl
from jax.experimental.pallas import tpu as pltpu
from jax.sharding import PartitionSpec as P

BF16 = jnp.bfloat16
F32 = jnp.float32
I32 = jnp.int32
BLOCK = 128
VMEM_BYTES = 32 << 20
BATCH = 8
FIRST_ORDER, SECOND_ORDER = (1, 0, 2), (1, 2, 0)
PARTS = 2
PAIR = 1


def dot(left, right):
    return jnp.dot(left, right, preferred_element_type=F32)


def dot_last(left, right):
    return lax.dot_general(left, right, (((1,), (1,)), ((), ())), preferred_element_type=F32)


def rows_hot(index_row, height):
    shape = (height, index_row.shape[1])
    index = jnp.broadcast_to(index_row, shape).astype(jnp.int16)
    return jnp.where(
        index == lax.broadcasted_iota(jnp.int16, shape, 0), jnp.ones((), BF16), jnp.zeros((), BF16)
    )


def silu_of_half(half):
    return half + half * jnp.tanh(half)


def halved(weight):
    return weight * jnp.asarray(0.5, BF16)


class Grid:
    def __init__(self, mesh, halo_capacity, pool_capacity, coarse_capacity, coarse_blocks, slot_count):
        self.dom_count = mesh.shape["dom"]
        self.sub_count = mesh.shape["sub"]
        self.chip_count = mesh.shape["chip"]
        self.places = self.sub_count * self.chip_count
        self.mirrored = self.dom_count == 4
        self.steps = (2, 3, 1) if self.mirrored else (1, self.dom_count - 1, 2)
        self.owners = len(range(0, self.places, 4))
        self.swapped = self.sub_count == 2 and self.chip_count == 2
        self.halo_capacity = halo_capacity
        self.pool_capacity = pool_capacity
        self.coarse_capacity = coarse_capacity
        self.blocks = coarse_blocks
        self.pieces = slot_count // BLOCK
        self.slots = self.places * pool_capacity
        self.pooled_rows = self.owners * pool_capacity
        self.sent_blocks = 1 if self.swapped else coarse_blocks
        self.list_rows = 2 * self.sent_blocks * self.pieces + self.dom_count
        self.packed_rows = -(-self.list_rows // 16) * 16
        self.packet = self.pooled_rows + self.packed_rows
        self.packets = 2 if self.swapped else 1
        self.octaves = -(-(self.slots + self.dom_count * coarse_capacity) // BLOCK)

    def partner(self, dom, step):
        return dom ^ step if self.mirrored else (dom + step) % self.dom_count

    def partner_here(self, step):
        own = lax.axis_index("dom")
        return own ^ step if self.mirrored else lax.rem(own + step, self.dom_count)

    def halo_place(self, source_dom):
        own = lax.axis_index("dom")
        if self.mirrored:
            step = source_dom ^ own
        else:
            step = own - source_dom
            step = jnp.where(step < 0, step + self.dom_count, step)
        place = jnp.zeros_like(step)
        for index, value in enumerate(self.steps):
            place = jnp.where(step == value, index, place)
        return place

    def block_of(self, place):
        return lax.div(place * self.pool_capacity, BLOCK)

    def own_place(self):
        return lax.axis_index("sub") * self.chip_count + lax.axis_index("chip")

    def slot_order(self, slots, place):
        return slots ^ (place * self.pool_capacity) if self.swapped else slots


def handed(halos, order):
    return [halos[turn] for turn in order]


def taken(refs, order):
    return [refs[order.index(turn)] for turn in range(len(refs))]


def turned(weight):
    return halved(weight).T


def turn_kernel(latent_hbm, table_ref, latent_ref, arrived):
    part = latent_ref.shape[0] // PARTS
    copies = []
    for index in range(PARTS):
        rows = pl.ds(index * part, part)
        copies.append(pltpu.make_async_copy(latent_hbm.at[rows], latent_ref.at[rows], arrived.at[index]))
        copies[-1].start()
    for index, copy in enumerate(copies):
        copy.wait()
        rows = slice(index * part, (index + 1) * part)
        table_ref[:, rows] = latent_ref[rows, :].T


def send_kernel(grid, table_ref, lists_ref, weights_ref, *sent_refs):
    index_row = jnp.concatenate([lists_ref[0, pl.ds(grid.partner_here(step), 1), :] for step in grid.steps], axis=1)
    picked = dot(table_ref[...], rows_hot(index_row, table_ref.shape[1])).astype(BF16)
    terms = dot(turned(weights_ref[0, 0]), picked).astype(BF16)
    capacity = lists_ref.shape[2]
    for index, out_ref in enumerate(sent_refs):
        out_ref[...] = terms[:, index * capacity : (index + 1) * capacity]


def far_rows(source_ref, place_ref, batch):
    local_count = source_ref.shape[1] * 3 // 4
    sources, places = [], []
    for index in range(BATCH):
        row = slice(batch * BATCH + index, batch * BATCH + index + 1)
        sources.append(source_ref[row, local_count:])
        place = place_ref[row, local_count:]
        places.append(jnp.where(place >= 0, place + index * BLOCK, -1))
    return jnp.concatenate(sources, axis=1), jnp.concatenate(places, axis=1)


def near_edges(table, source_ref, place_ref, weights_ref, layer, aimed_ref, sums_ref, terms_ref):
    features, node_count = table.shape
    block_count, slot_count = source_ref.shape
    local_count = slot_count * 3 // 4
    window = min(3 * BLOCK, node_count)
    both = jnp.concatenate([turned(weights_ref[layer, 0]), turned(weights_ref[layer, 1])], axis=0)
    terms_ref[...] = dot(both, table).astype(BF16)

    def messages(block):
        start = min(max(block * BLOCK - BLOCK, 0), node_count - window)
        terms = jnp.concatenate(
            [
                terms_ref[:features, start : start + window],
                terms_ref[features:, block * BLOCK : (block + 1) * BLOCK],
            ],
            axis=1,
        )
        places = rows_hot(place_ref[block : block + 1, :], BLOCK)
        sources = rows_hot(source_ref[block : block + 1, :] - start, window)
        picked = dot(terms, jnp.concatenate([sources, places], axis=0))
        far_count = slot_count - local_count
        aimed_ref[:, block * far_count : (block + 1) * far_count] = picked[:, local_count:].astype(BF16)
        return silu_of_half(picked[:, :local_count]).astype(BF16)

    def add_up(block, message):
        places = rows_hot(place_ref[block : block + 1, :local_count], BLOCK)
        sums_ref[:, block * BLOCK : (block + 1) * BLOCK] = dot_last(message, places)

    waiting = None
    for block in range(block_count):
        message = messages(block)
        if waiting is not None:
            add_up(*waiting)
        waiting = (block, message)
    add_up(*waiting)


def near_kernel(
    grid,
    table_ref,
    source_ref,
    place_ref,
    weights_ref,
    coarse_source_ref,
    coarse_place_ref,
    coarse_send_ref,
    pool_ref,
    sources_ref,
    places_ref,
    aimed_ref,
    sums_ref,
    pooled_ref,
    *rest,
):
    packed_refs, terms_ref = rest[:-1], rest[-1]
    table = table_ref[...]
    halo_capacity = grid.halo_capacity
    for batch in range(source_ref.shape[0] // BATCH):
        sources, places = far_rows(source_ref, place_ref, batch)
        slots = sources - table.shape[1]
        source_dom = lax.shift_right_logical(slots, halo_capacity.bit_length() - 1)
        sources_ref[batch : batch + 1, :] = grid.halo_place(source_dom) * halo_capacity + (
            slots & (halo_capacity - 1)
        )
        places_ref[batch : batch + 1, :] = places
    near_edges(table, source_ref, place_ref, weights_ref, 0, aimed_ref, sums_ref, terms_ref)

    place = grid.own_place()
    for index, packed_ref in enumerate(packed_refs):
        if grid.swapped:
            block = grid.block_of(place ^ (2 * index))
            sources, places = coarse_source_ref[pl.ds(block, 1), :], coarse_place_ref[pl.ds(block, 1), :]
        else:
            sources, places = coarse_source_ref[...], coarse_place_ref[...]
        lists = jnp.minimum(coarse_send_ref[0], grid.slots - 1)
        pieces = lane_rows(sources) + [lists] + lane_rows(places + 1)
        spare = grid.packed_rows - grid.list_rows
        if spare:
            pieces.append(jnp.zeros((spare, BLOCK), I32))
        whole = jnp.concatenate(pieces, axis=0)
        coded = lax.shift_left((whole & (BLOCK - 1)) + BLOCK, lax.shift_right_logical(whole, BLOCK.bit_length() - 1))
        packed_ref[...] = coded.astype(F32).astype(BF16)
    for owner in range(grid.owners):
        pooled_ref[owner : owner + 1, :] = pool_ref[0, 4 * owner : 4 * owner + 1, :]


def far_edges(layer, table_ref, aimed_ref, sources_ref, places_ref, sums_ref, weights_ref, halo_refs, both_ref, write):
    features, node_count = table_ref.shape
    batch_count, slot_count = sources_ref.shape
    halo = jnp.concatenate([ref[...] for ref in halo_refs], axis=1)
    update_weights = jnp.concatenate([turned(weights_ref[layer, 2]), turned(weights_ref[layer, 3])], axis=1)
    pair_slots = slot_count * PAIR // BATCH
    pair_rows = PAIR * BLOCK
    batch_rows = BATCH * BLOCK
    both_ref[features:, :] = table_ref[...]

    def messages(batch):
        aimed = aimed_ref[:, batch * slot_count : (batch + 1) * slot_count].astype(F32)
        hot = rows_hot(sources_ref[batch : batch + 1, :], halo.shape[1])
        return silu_of_half(dot(halo, hot) + aimed).astype(BF16)

    def add_up(batch, message):
        for pair in range(BATCH // PAIR):
            slots = slice(pair * pair_slots, (pair + 1) * pair_slots)
            first = batch * batch_rows + pair * pair_rows
            columns = slice(first, first + pair_rows)
            hot = rows_hot(places_ref[batch : batch + 1, slots] - pair * pair_rows, pair_rows)
            both_ref[:features, columns] = (sums_ref[:, columns] + dot_last(message[:, slots], hot)).astype(BF16)

    def update(batch):
        part = batch_rows // 2
        for first in range(batch * batch_rows, (batch + 1) * batch_rows, part):
            columns = slice(first, first + part)
            change = silu_of_half(dot(update_weights, both_ref[:, columns]))
            write(columns, (both_ref[features:, columns].astype(F32) + change).astype(BF16))

    held = [messages(batch) for batch in range(batch_count)]
    for batch in range(batch_count):
        add_up(batch, held[batch])
    for batch in range(batch_count):
        update(batch)


def lane_rows(values):
    pieces = []
    for block in range(values.shape[0]):
        for start in range(0, values.shape[1], BLOCK):
            pieces.append(values[block : block + 1, start : start + BLOCK])
    return pieces


def far_pool_kernel(
    grid, table_ref, aimed_ref, sources_ref, places_ref, sums_ref, weights_ref, pool_ref, *rest
):
    count = grid.packets
    packed_refs, halo_refs = rest[:count], taken(rest[count : count + len(grid.steps)], FIRST_ORDER)
    first_ref, packet_refs, both_ref = rest[-2 - count], rest[-1 - count : -1], rest[-1]

    def write(columns, value):
        first_ref[:, columns] = value

    for packet_ref, packed_ref in zip(packet_refs, packed_refs):
        packet_ref[grid.pooled_rows :, :] = packed_ref[...]
    far_edges(0, table_ref, aimed_ref, sources_ref, places_ref, sums_ref, weights_ref, halo_refs, both_ref, write)
    for owner in range(grid.owners):
        hot = rows_hot(pool_ref[owner : owner + 1, :], first_ref.shape[1])
        pooled = dot(first_ref[...], hot).astype(BF16).T
        for packet_ref in packet_refs:
            packet_ref[owner * grid.pool_capacity : (owner + 1) * grid.pool_capacity, :] = pooled


def far_kernel(table_ref, aimed_ref, sources_ref, places_ref, sums_ref, weights_ref, *rest):
    halo_refs, (out_hbm, both_ref, rows_ref, written) = taken(rest[:-4], SECOND_ORDER), rest[-4:]
    copies = []

    def write(columns, value):
        rows_ref[columns, :] = value.T
        rows = pl.ds(columns.start, columns.stop - columns.start)
        copies.append(pltpu.make_async_copy(rows_ref.at[rows], out_hbm.at[rows], written.at[len(copies)]))
        copies[-1].start()

    far_edges(1, table_ref, aimed_ref, sources_ref, places_ref, sums_ref, weights_ref, halo_refs, both_ref, write)
    for copy in copies:
        copy.wait()


def ahead_kernel(grid, first_ref, prolong_ref, lists_ref, out_ref):
    indices = prolong_ref[...]
    shift = (4 * grid.pool_capacity).bit_length() - 1
    indices = lax.shift_right_logical(indices, shift) * grid.pool_capacity + (indices & (grid.pool_capacity - 1))
    indices = indices.astype(F32)
    row = jnp.concatenate([indices[block : block + 1, :] for block in range(indices.shape[0])], axis=1)
    extra = jnp.concatenate([row, jnp.zeros((15, row.shape[1]), F32)], axis=0).astype(BF16)
    table = jnp.concatenate([first_ref[...], extra], axis=0)
    capacity = lists_ref.shape[2]
    for index, step in enumerate(grid.steps):
        index_row = lists_ref[0, pl.ds(grid.partner_here(step), 1), :]
        picked = dot(table, rows_hot(index_row, table.shape[1]))
        out_ref[:, index * capacity : (index + 1) * capacity] = picked.astype(BF16)


def owner_lists(grid, packets, owner, place):
    if grid.swapped:
        rows = packets[0][grid.pooled_rows :, :].astype(F32)
        for other in range(1, grid.places):
            rows = jnp.where(place == other, packets[other][grid.pooled_rows :, :].astype(F32), rows)
    else:
        rows = packets[4 * owner][grid.pooled_rows :, :].astype(F32)
    coded = rows.astype(I32)
    octave = jnp.zeros_like(coded)
    for power in range(1, grid.octaves):
        octave = octave + jnp.where(coded >= BLOCK << power, 1, 0)
    return octave * BLOCK + lax.shift_right_logical(coded, octave) - BLOCK


def owner_table(grid, packets, owner):
    start = owner * grid.pool_capacity
    return jnp.concatenate([packet[start : start + grid.pool_capacity, :] for packet in packets], axis=0)


def coarse_send_kernel(grid, weights_ref, *refs):
    packets = refs[: grid.places]
    outs = refs[grid.places : grid.places + len(grid.steps)]
    lists_ref = refs[-1]
    place = grid.own_place()
    first_list = grid.sent_blocks * grid.pieces
    capacity = grid.coarse_capacity
    for owner in range(grid.owners):
        lists_ref[...] = owner_lists(grid, packets, owner, place)
        table = owner_table(grid, packets, owner)
        terms = dot(table, halved(weights_ref[0])).astype(BF16).T
        index_row = jnp.concatenate(
            [lists_ref[pl.ds(first_list + grid.partner_here(step), 1), :] for step in grid.steps], axis=1
        )
        picked = dot(terms, rows_hot(grid.slot_order(index_row, place), grid.slots)).astype(BF16)
        for index, out_ref in enumerate(outs):
            out_ref[owner * BLOCK : (owner + 1) * BLOCK, :] = picked[:, index * capacity : (index + 1) * capacity]


def coarse_own_kernel(grid, weights_ref, *refs):
    packets = refs[: grid.places]
    picked_ref, source_out, place_out, rows_out, lists_ref = refs[grid.places :]
    place = grid.own_place()
    first_slot = place * grid.pool_capacity
    block = 0 if grid.swapped else grid.block_of(place)
    within = first_slot & (BLOCK - 1)
    shift = grid.coarse_capacity.bit_length() - 1
    for owner in range(grid.owners):
        lists_ref[...] = owner_lists(grid, packets, owner, place)
        sources = jnp.concatenate(
            [lists_ref[pl.ds(block * grid.pieces + piece, 1), :] for piece in range(grid.pieces)], axis=1
        )
        offset = grid.sent_blocks * grid.pieces + grid.dom_count
        places = jnp.concatenate(
            [lists_ref[pl.ds(offset + block * grid.pieces + piece, 1), :] for piece in range(grid.pieces)], axis=1
        )
        places = places - 1 - within
        places = jnp.where((places >= 0) & (places < grid.pool_capacity), places, -1)
        halo_slots = sources - grid.slots
        source_dom = lax.shift_right_arithmetic(halo_slots, shift)
        halo_sources = grid.halo_place(source_dom) * grid.coarse_capacity + (halo_slots & (grid.coarse_capacity - 1))
        is_halo = halo_slots >= 0
        source_out[owner : owner + 1, :] = jnp.where(is_halo, halo_sources, -1)
        place_out[owner : owner + 1, :] = places
        own_sources = jnp.where(is_halo, -1, grid.slot_order(sources, place))

        table = owner_table(grid, packets, owner)
        rows = table[: grid.pool_capacity]
        if not grid.swapped:
            for other in range(1, grid.places):
                other_rows = table[other * grid.pool_capacity : (other + 1) * grid.pool_capacity]
                rows = jnp.where(place == other, other_rows, rows)
        rows_out[owner] = rows.T
        sender = dot(table, halved(weights_ref[0])).astype(BF16).T
        target = dot(rows, halved(weights_ref[1])).astype(BF16).T
        hot = jnp.concatenate([rows_hot(own_sources, grid.slots), rows_hot(places, grid.pool_capacity)], axis=0)
        picked_ref[owner] = dot(jnp.concatenate([sender, target], axis=1), hot)


def lift(table, prolonged, index_row):
    pooled_rows = prolonged.shape[1] // 2
    hot = rows_hot(index_row, pooled_rows)
    hot = jnp.concatenate([hot, hot], axis=0)
    return (table.astype(F32) + dot(prolonged, hot)).astype(BF16)


def lift_halo_kernel(
    grid,
    picked_ref,
    source_ref,
    place_ref,
    rows_ref,
    ahead_ref,
    coarse_weights_ref,
    prolong_weight_ref,
    weights_ref,
    *rest,
):
    count = len(grid.steps)
    halo_refs, prolonged_ref, sent_refs = rest[:count], rest[count], rest[count + 1 :]
    features = rows_ref.shape[1]
    update_weights = jnp.concatenate([turned(coarse_weights_ref[2]), turned(coarse_weights_ref[3])], axis=1)
    prolong_weight = turned(prolong_weight_ref[...])
    prolonged = []
    for owner in range(grid.owners):
        halo = jnp.concatenate([ref[owner * BLOCK : (owner + 1) * BLOCK, :] for ref in halo_refs], axis=1)
        picked = picked_ref[owner] + dot(halo, rows_hot(source_ref[owner : owner + 1, :], halo.shape[1]))
        message = silu_of_half(picked).astype(BF16)
        places = rows_hot(place_ref[owner : owner + 1, :], grid.pool_capacity)
        summed = dot_last(message, places).astype(BF16)
        rows = rows_ref[owner]
        update = dot(update_weights, jnp.concatenate([summed, rows], axis=0))
        coarse = (rows.astype(F32) + silu_of_half(update)).astype(BF16)
        prolonged.append(silu_of_half(dot(prolong_weight, coarse)))
    prolonged = jnp.concatenate(prolonged, axis=1)
    high = prolonged.astype(BF16)
    low = (prolonged - high.astype(F32)).astype(BF16)
    parts = jnp.concatenate([high, low], axis=1)
    prolonged_ref[...] = parts
    weight = turned(weights_ref[1, 0])
    index_row = ahead_ref[features : features + 16, :].astype(F32).astype(I32)[:1]
    lifted = lift(ahead_ref[:features, :], parts, index_row)
    terms = dot(weight, lifted).astype(BF16)
    capacity = sent_refs[0].shape[1]
    for index, out_ref in enumerate(sent_refs):
        out_ref[...] = terms[:, index * capacity : (index + 1) * capacity]


def lift_near_kernel(
    grid,
    first_ref,
    prolonged_ref,
    prolong_ref,
    source_ref,
    place_ref,
    weights_ref,
    lifted_ref,
    aimed_ref,
    sums_ref,
    terms_ref,
):
    indices = prolong_ref[...]
    shift = (4 * grid.pool_capacity).bit_length() - 1
    indices = lax.shift_right_logical(indices, shift) * grid.pool_capacity + (indices & (grid.pool_capacity - 1))
    row = jnp.concatenate([indices[block : block + 1, :] for block in range(indices.shape[0])], axis=1)
    lifted = lift(first_ref[...], prolonged_ref[...], row)
    lifted_ref[...] = lifted
    near_edges(lifted, source_ref, place_ref, weights_ref, 1, aimed_ref, sums_ref, terms_ref)


def call(kernel, outs, scratch=(), flops=0, name=None, limit=VMEM_BYTES, **specs):
    return pl.pallas_call(
        kernel,
        out_shape=tuple(jax.ShapeDtypeStruct(shape, dtype) for shape, dtype in outs),
        scratch_shapes=list(scratch),
        compiler_params=pltpu.CompilerParams(vmem_limit_bytes=limit),
        cost_estimate=pl.CostEstimate(flops=flops, bytes_accessed=4 << 20, transcendentals=0),
        name=name,
        **specs,
    )


def swap_dom(grid, arrays):
    return [
        lax.ppermute(array, "dom", [(dom, grid.partner(dom, step)) for dom in range(grid.dom_count)])
        for array, step in zip(arrays, grid.steps)
    ]


def trade_packets(grid, packets):
    if grid.swapped:
        pairs = [(0, 1), (1, 0)]
        near, far = packets
        over = lax.ppermute(far, "sub", pairs)
        across = lax.ppermute(near, "chip", pairs)
        both = lax.ppermute(far, ("sub", "chip"), [(0, 3), (1, 2), (2, 1), (3, 0)])
        return [near, across, over, both]
    gathered = lax.all_gather(packets[0], ("sub", "chip"), axis=0, tiled=False)
    return [gathered[place] for place in range(grid.places)]


def body(
    mesh,
    fine_nodes,
    fine_src,
    fine_dst,
    halo_send,
    pool_send,
    coarse_src,
    coarse_dst,
    coarse_send,
    prolong_idx,
    fine_weights,
    coarse_weights,
    prolong_weight,
):
    node_count, features = fine_nodes.shape
    halo_capacity = halo_send.shape[2]
    coarse_blocks, coarse_slots = coarse_src.shape
    grid = Grid(mesh, halo_capacity, pool_send.shape[2], coarse_send.shape[2], coarse_blocks, coarse_slots)
    steps = len(grid.steps)
    block_count, slot_count = fine_src.shape
    far_count = slot_count - slot_count * 3 // 4
    table = ((features, node_count), BF16)
    sums_table = ((features, node_count), F32)
    aimed_table = ((features, block_count * far_count), BF16)
    far_lists = ((block_count // BATCH, BATCH * far_count), I32)
    halo_outs = [((features, halo_capacity), BF16)] * steps
    two_tables = pltpu.VMEM((2 * features, node_count), BF16)
    prolong_rows = prolong_idx.reshape(node_count // BLOCK, BLOCK)
    big = 1 << 30
    in_hbm = pl.BlockSpec(memory_space=pltpu.HBM)

    (nodes,) = call(
        turn_kernel,
        [table],
        [pltpu.VMEM((node_count, features), BF16), pltpu.SemaphoreType.DMA((PARTS,))],
        name="turn",
        limit=5300 * 10486,
        in_specs=[in_hbm],
    )(fine_nodes)
    sent = call(functools.partial(send_kernel, grid), halo_outs, flops=big, name="send")(
        nodes, halo_send, fine_weights
    )
    halo = swap_dom(grid, sent)
    far_sources, far_places, aimed, sums, pool_lists, *packed = call(
        functools.partial(near_kernel, grid),
        [
            far_lists,
            far_lists,
            aimed_table,
            sums_table,
            ((grid.owners, grid.pool_capacity), I32),
            *[((grid.packed_rows, features), BF16)] * grid.packets,
        ],
        [two_tables],
        flops=4 * big,
        name="near",
    )(nodes, fine_src, fine_dst, fine_weights, coarse_src, coarse_dst, coarse_send, pool_send)
    first, *packets = call(
        functools.partial(far_pool_kernel, grid),
        [table, *[((grid.packet, features), BF16)] * grid.packets],
        [two_tables],
        flops=2 * big,
        name="far_pool",
    )(nodes, aimed, far_sources, far_places, sums, fine_weights, pool_lists, *packed, *handed(halo, FIRST_ORDER))
    packets = trade_packets(grid, packets)
    (ahead,) = call(
        functools.partial(ahead_kernel, grid), [((features + 16, steps * halo_capacity), BF16)], flops=big, name="ahead"
    )(first, prolong_rows, halo_send)
    lists_scratch = pltpu.VMEM((grid.packed_rows, BLOCK), I32)
    sent = call(
        functools.partial(coarse_send_kernel, grid),
        [((grid.owners * features, grid.coarse_capacity), BF16)] * steps,
        [lists_scratch],
        flops=big // 2,
        name="coarse_send",
    )(coarse_weights, *packets)
    coarse_halo = swap_dom(grid, sent)
    picked, sources, places, rows = call(
        functools.partial(coarse_own_kernel, grid),
        [
            ((grid.owners, features, coarse_slots), F32),
            ((grid.owners, coarse_slots), I32),
            ((grid.owners, coarse_slots), I32),
            ((grid.owners, features, grid.pool_capacity), BF16),
        ],
        [lists_scratch],
        flops=4 * big,
        name="coarse_own",
    )(coarse_weights, *packets)
    prolonged, *sent = call(
        functools.partial(lift_halo_kernel, grid),
        [((features, 2 * grid.pooled_rows), BF16), *halo_outs],
        flops=big,
        name="lift_halo",
    )(picked, sources, places, rows, ahead, coarse_weights, prolong_weight, fine_weights, *coarse_halo)
    halo = swap_dom(grid, sent)
    lifted, aimed, sums = call(
        functools.partial(lift_near_kernel, grid),
        [table, aimed_table, sums_table],
        [two_tables],
        flops=4 * big,
        name="lift_near",
    )(first, prolonged, prolong_rows, fine_src, fine_dst, fine_weights)
    (fine_out,) = call(
        far_kernel,
        [((node_count, features), BF16)],
        [
            two_tables,
            pltpu.VMEM((node_count, features), BF16),
            pltpu.SemaphoreType.DMA((2 * block_count // BATCH,)),
        ],
        flops=2 * big,
        name="far",
        out_specs=(pl.BlockSpec(memory_space=pltpu.HBM),),
    )(lifted, aimed, far_sources, far_places, sums, fine_weights, *handed(halo, SECOND_ORDER))
    return fine_out


def solution(mesh):
    split = ("groups", "dom", "sub", "chip")
    return jax.shard_map(
        functools.partial(body, mesh),
        mesh=mesh,
        in_specs=(
            P(split, None),
            P(split, None),
            P(split, None),
            P(split, None, None),
            P(split, None, None),
            P(split, None),
            P(split, None),
            P(split, None, None),
            P(split),
            P(),
            P(),
            P(),
        ),
        out_specs=P(split, None),
        check_vma=False,
    )
```

```python
import functools

import jax
import jax.numpy as jnp
from jax import lax
from jax.experimental import pallas as pl
from jax.experimental.pallas import tpu as pltpu
from jax.sharding import PartitionSpec as P

BF16 = jnp.bfloat16
F32 = jnp.float32
I32 = jnp.int32
BLOCK = 128
VMEM_BYTES = 32 << 20
BATCH = 8
FIRST_ORDER, SECOND_ORDER = (1, 0, 2), (1, 2, 0)
PARTS = 1
PAIR = 1


def dot(left, right):
    return jnp.dot(left, right, preferred_element_type=F32)


def dot_last(left, right):
    return lax.dot_general(left, right, (((1,), (1,)), ((), ())), preferred_element_type=F32)


def rows_hot(index_row, height):
    shape = (height, index_row.shape[1])
    index = jnp.broadcast_to(index_row, shape).astype(jnp.int16)
    return jnp.where(
        index == lax.broadcasted_iota(jnp.int16, shape, 0), jnp.ones((), BF16), jnp.zeros((), BF16)
    )


def silu_of_half(half):
    return half + half * jnp.tanh(half)


def halved(weight):
    return weight * jnp.asarray(0.5, BF16)


class Grid:
    def __init__(self, mesh, halo_capacity, pool_capacity, coarse_capacity, coarse_blocks, slot_count):
        self.dom_count = mesh.shape["dom"]
        self.sub_count = mesh.shape["sub"]
        self.chip_count = mesh.shape["chip"]
        self.places = self.sub_count * self.chip_count
        self.mirrored = self.dom_count == 4
        self.steps = (2, 3, 1) if self.mirrored else (1, self.dom_count - 1, 2)
        self.owners = len(range(0, self.places, 4))
        self.swapped = self.sub_count == 2 and self.chip_count == 2
        self.halo_capacity = halo_capacity
        self.pool_capacity = pool_capacity
        self.coarse_capacity = coarse_capacity
        self.blocks = coarse_blocks
        self.pieces = slot_count // BLOCK
        self.slots = self.places * pool_capacity
        self.pooled_rows = self.owners * pool_capacity
        self.sent_blocks = 1 if self.swapped else coarse_blocks
        self.list_rows = 2 * self.sent_blocks * self.pieces + self.dom_count
        self.packed_rows = -(-self.list_rows // 16) * 16
        self.packet = self.pooled_rows + self.packed_rows
        self.packets = 2 if self.swapped else 1
        self.octaves = -(-(self.slots + self.dom_count * coarse_capacity) // BLOCK)

    def partner(self, dom, step):
        return dom ^ step if self.mirrored else (dom + step) % self.dom_count

    def partner_here(self, step):
        own = lax.axis_index("dom")
        return own ^ step if self.mirrored else lax.rem(own + step, self.dom_count)

    def halo_place(self, source_dom):
        own = lax.axis_index("dom")
        if self.mirrored:
            step = source_dom ^ own
        else:
            step = own - source_dom
            step = jnp.where(step < 0, step + self.dom_count, step)
        place = jnp.zeros_like(step)
        for index, value in enumerate(self.steps):
            place = jnp.where(step == value, index, place)
        return place

    def block_of(self, place):
        return lax.div(place * self.pool_capacity, BLOCK)

    def own_place(self):
        return lax.axis_index("sub") * self.chip_count + lax.axis_index("chip")

    def slot_order(self, slots, place):
        return slots ^ (place * self.pool_capacity) if self.swapped else slots


def handed(halos, order):
    return [halos[turn] for turn in order]


def taken(refs, order):
    return [refs[order.index(turn)] for turn in range(len(refs))]


def turned(weight):
    return halved(weight).T


def turn_kernel(latent_hbm, table_ref, latent_ref, arrived):
    part = latent_ref.shape[0] // PARTS
    copies = []
    for index in range(PARTS):
        rows = pl.ds(index * part, part)
        copies.append(pltpu.make_async_copy(latent_hbm.at[rows], latent_ref.at[rows], arrived.at[index]))
        copies[-1].start()
    for index, copy in enumerate(copies):
        copy.wait()
        rows = slice(index * part, (index + 1) * part)
        table_ref[:, rows] = latent_ref[rows, :].T


def send_kernel(grid, table_ref, lists_ref, weights_ref, *sent_refs):
    index_row = jnp.concatenate([lists_ref[0, pl.ds(grid.partner_here(step), 1), :] for step in grid.steps], axis=1)
    picked = dot(table_ref[...], rows_hot(index_row, table_ref.shape[1])).astype(BF16)
    terms = dot(turned(weights_ref[0, 0]), picked).astype(BF16)
    capacity = lists_ref.shape[2]
    for index, out_ref in enumerate(sent_refs):
        out_ref[...] = terms[:, index * capacity : (index + 1) * capacity]


def far_rows(source_ref, place_ref, batch):
    local_count = source_ref.shape[1] * 3 // 4
    sources, places = [], []
    for index in range(BATCH):
        row = slice(batch * BATCH + index, batch * BATCH + index + 1)
        sources.append(source_ref[row, local_count:])
        place = place_ref[row, local_count:]
        places.append(jnp.where(place >= 0, place + index * BLOCK, -1))
    return jnp.concatenate(sources, axis=1), jnp.concatenate(places, axis=1)


def near_edges(table, source_ref, place_ref, weights_ref, layer, aimed_ref, sums_ref, terms_ref):
    features, node_count = table.shape
    block_count, slot_count = source_ref.shape
    local_count = slot_count * 3 // 4
    window = min(3 * BLOCK, node_count)
    both = jnp.concatenate([turned(weights_ref[layer, 0]), turned(weights_ref[layer, 1])], axis=0)
    terms_ref[...] = dot(both, table).astype(BF16)

    def messages(block):
        start = min(max(block * BLOCK - BLOCK, 0), node_count - window)
        terms = jnp.concatenate(
            [
                terms_ref[:features, start : start + window],
                terms_ref[features:, block * BLOCK : (block + 1) * BLOCK],
            ],
            axis=1,
        )
        places = rows_hot(place_ref[block : block + 1, :], BLOCK)
        sources = rows_hot(source_ref[block : block + 1, :] - start, window)
        picked = dot(terms, jnp.concatenate([sources, places], axis=0))
        far_count = slot_count - local_count
        aimed_ref[:, block * far_count : (block + 1) * far_count] = picked[:, local_count:].astype(BF16)
        return silu_of_half(picked[:, :local_count]).astype(BF16)

    def add_up(block, message):
        places = rows_hot(place_ref[block : block + 1, :local_count], BLOCK)
        sums_ref[:, block * BLOCK : (block + 1) * BLOCK] = dot_last(message, places)

    waiting = None
    for block in range(block_count):
        message = messages(block)
        if waiting is not None:
            add_up(*waiting)
        waiting = (block, message)
    add_up(*waiting)


def near_kernel(
    grid,
    table_ref,
    source_ref,
    place_ref,
    weights_ref,
    coarse_source_ref,
    coarse_place_ref,
    coarse_send_ref,
    pool_ref,
    sources_ref,
    places_ref,
    aimed_ref,
    sums_ref,
    pooled_ref,
    *rest,
):
    packed_refs, terms_ref = rest[:-1], rest[-1]
    table = table_ref[...]
    halo_capacity = grid.halo_capacity
    for batch in range(source_ref.shape[0] // BATCH):
        sources, places = far_rows(source_ref, place_ref, batch)
        slots = sources - table.shape[1]
        source_dom = lax.shift_right_logical(slots, halo_capacity.bit_length() - 1)
        sources_ref[batch : batch + 1, :] = grid.halo_place(source_dom) * halo_capacity + (
            slots & (halo_capacity - 1)
        )
        places_ref[batch : batch + 1, :] = places
    near_edges(table, source_ref, place_ref, weights_ref, 0, aimed_ref, sums_ref, terms_ref)

    place = grid.own_place()
    for index, packed_ref in enumerate(packed_refs):
        if grid.swapped:
            block = grid.block_of(place ^ (2 * index))
            sources, places = coarse_source_ref[pl.ds(block, 1), :], coarse_place_ref[pl.ds(block, 1), :]
        else:
            sources, places = coarse_source_ref[...], coarse_place_ref[...]
        lists = jnp.minimum(coarse_send_ref[0], grid.slots - 1)
        pieces = lane_rows(sources) + [lists] + lane_rows(places + 1)
        spare = grid.packed_rows - grid.list_rows
        if spare:
            pieces.append(jnp.zeros((spare, BLOCK), I32))
        whole = jnp.concatenate(pieces, axis=0)
        coded = lax.shift_left((whole & (BLOCK - 1)) + BLOCK, lax.shift_right_logical(whole, BLOCK.bit_length() - 1))
        packed_ref[...] = coded.astype(F32).astype(BF16)
    for owner in range(grid.owners):
        pooled_ref[owner : owner + 1, :] = pool_ref[0, 4 * owner : 4 * owner + 1, :]


def far_edges(layer, table_ref, aimed_ref, sources_ref, places_ref, sums_ref, weights_ref, halo_refs, both_ref, write):
    features, node_count = table_ref.shape
    batch_count, slot_count = sources_ref.shape
    halo = jnp.concatenate([ref[...] for ref in halo_refs], axis=1)
    update_weights = jnp.concatenate([turned(weights_ref[layer, 2]), turned(weights_ref[layer, 3])], axis=1)
    pair_slots = slot_count * PAIR // BATCH
    pair_rows = PAIR * BLOCK
    batch_rows = BATCH * BLOCK
    both_ref[features:, :] = table_ref[...]

    def messages(batch):
        aimed = aimed_ref[:, batch * slot_count : (batch + 1) * slot_count].astype(F32)
        hot = rows_hot(sources_ref[batch : batch + 1, :], halo.shape[1])
        return silu_of_half(dot(halo, hot) + aimed).astype(BF16)

    def add_up(batch, message):
        for pair in range(BATCH // PAIR):
            slots = slice(pair * pair_slots, (pair + 1) * pair_slots)
            first = batch * batch_rows + pair * pair_rows
            columns = slice(first, first + pair_rows)
            hot = rows_hot(places_ref[batch : batch + 1, slots] - pair * pair_rows, pair_rows)
            both_ref[:features, columns] = (sums_ref[:, columns] + dot_last(message[:, slots], hot)).astype(BF16)

    def update(batch):
        columns = slice(batch * batch_rows, (batch + 1) * batch_rows)
        change = silu_of_half(dot(update_weights, both_ref[:, columns]))
        write(columns, (both_ref[features:, columns].astype(F32) + change).astype(BF16))

    held = [messages(batch) for batch in range(batch_count)]
    for batch in range(batch_count):
        add_up(batch, held[batch])
    for batch in range(batch_count):
        update(batch)


def lane_rows(values):
    pieces = []
    for block in range(values.shape[0]):
        for start in range(0, values.shape[1], BLOCK):
            pieces.append(values[block : block + 1, start : start + BLOCK])
    return pieces


def far_pool_kernel(
    grid, table_ref, aimed_ref, sources_ref, places_ref, sums_ref, weights_ref, pool_ref, *rest
):
    count = grid.packets
    packed_refs, halo_refs = rest[:count], taken(rest[count : count + len(grid.steps)], FIRST_ORDER)
    first_ref, packet_refs, both_ref = rest[-2 - count], rest[-1 - count : -1], rest[-1]

    def write(columns, value):
        first_ref[:, columns] = value

    for packet_ref, packed_ref in zip(packet_refs, packed_refs):
        packet_ref[grid.pooled_rows :, :] = packed_ref[...]
    far_edges(0, table_ref, aimed_ref, sources_ref, places_ref, sums_ref, weights_ref, halo_refs, both_ref, write)
    for owner in range(grid.owners):
        hot = rows_hot(pool_ref[owner : owner + 1, :], first_ref.shape[1])
        pooled = dot(first_ref[...], hot).astype(BF16).T
        for packet_ref in packet_refs:
            packet_ref[owner * grid.pool_capacity : (owner + 1) * grid.pool_capacity, :] = pooled


def far_kernel(table_ref, aimed_ref, sources_ref, places_ref, sums_ref, weights_ref, *rest):
    halo_refs, (out_hbm, both_ref, rows_ref, written) = taken(rest[:-4], SECOND_ORDER), rest[-4:]
    copies = []

    def write(columns, value):
        rows_ref[columns, :] = value.T
        rows = pl.ds(columns.start, columns.stop - columns.start)
        copies.append(pltpu.make_async_copy(rows_ref.at[rows], out_hbm.at[rows], written.at[len(copies)]))
        copies[-1].start()

    far_edges(1, table_ref, aimed_ref, sources_ref, places_ref, sums_ref, weights_ref, halo_refs, both_ref, write)
    for copy in copies:
        copy.wait()


def ahead_kernel(grid, first_ref, prolong_ref, lists_ref, out_ref):
    indices = prolong_ref[...]
    shift = (4 * grid.pool_capacity).bit_length() - 1
    indices = lax.shift_right_logical(indices, shift) * grid.pool_capacity + (indices & (grid.pool_capacity - 1))
    indices = indices.astype(F32)
    row = jnp.concatenate([indices[block : block + 1, :] for block in range(indices.shape[0])], axis=1)
    extra = jnp.concatenate([row, jnp.zeros((15, row.shape[1]), F32)], axis=0).astype(BF16)
    table = jnp.concatenate([first_ref[...], extra], axis=0)
    capacity = lists_ref.shape[2]
    for index, step in enumerate(grid.steps):
        index_row = lists_ref[0, pl.ds(grid.partner_here(step), 1), :]
        picked = dot(table, rows_hot(index_row, table.shape[1]))
        out_ref[:, index * capacity : (index + 1) * capacity] = picked.astype(BF16)


def owner_lists(grid, packets, owner, place):
    if grid.swapped:
        rows = packets[0][grid.pooled_rows :, :].astype(F32)
        for other in range(1, grid.places):
            rows = jnp.where(place == other, packets[other][grid.pooled_rows :, :].astype(F32), rows)
    else:
        rows = packets[4 * owner][grid.pooled_rows :, :].astype(F32)
    coded = rows.astype(I32)
    octave = jnp.zeros_like(coded)
    for power in range(1, grid.octaves):
        octave = octave + jnp.where(coded >= BLOCK << power, 1, 0)
    return octave * BLOCK + lax.shift_right_logical(coded, octave) - BLOCK


def owner_table(grid, packets, owner):
    start = owner * grid.pool_capacity
    return jnp.concatenate([packet[start : start + grid.pool_capacity, :] for packet in packets], axis=0)


def coarse_send_kernel(grid, weights_ref, *refs):
    packets = refs[: grid.places]
    outs = refs[grid.places : grid.places + len(grid.steps)]
    lists_ref = refs[-1]
    place = grid.own_place()
    first_list = grid.sent_blocks * grid.pieces
    capacity = grid.coarse_capacity
    for owner in range(grid.owners):
        lists_ref[...] = owner_lists(grid, packets, owner, place)
        table = owner_table(grid, packets, owner)
        terms = dot(table, halved(weights_ref[0])).astype(BF16).T
        index_row = jnp.concatenate(
            [lists_ref[pl.ds(first_list + grid.partner_here(step), 1), :] for step in grid.steps], axis=1
        )
        picked = dot(terms, rows_hot(grid.slot_order(index_row, place), grid.slots)).astype(BF16)
        for index, out_ref in enumerate(outs):
            out_ref[owner * BLOCK : (owner + 1) * BLOCK, :] = picked[:, index * capacity : (index + 1) * capacity]


def coarse_own_kernel(grid, weights_ref, *refs):
    packets = refs[: grid.places]
    picked_ref, source_out, place_out, rows_out, lists_ref = refs[grid.places :]
    place = grid.own_place()
    first_slot = place * grid.pool_capacity
    block = 0 if grid.swapped else grid.block_of(place)
    within = first_slot & (BLOCK - 1)
    shift = grid.coarse_capacity.bit_length() - 1
    for owner in range(grid.owners):
        lists_ref[...] = owner_lists(grid, packets, owner, place)
        sources = jnp.concatenate(
            [lists_ref[pl.ds(block * grid.pieces + piece, 1), :] for piece in range(grid.pieces)], axis=1
        )
        offset = grid.sent_blocks * grid.pieces + grid.dom_count
        places = jnp.concatenate(
            [lists_ref[pl.ds(offset + block * grid.pieces + piece, 1), :] for piece in range(grid.pieces)], axis=1
        )
        places = places - 1 - within
        places = jnp.where((places >= 0) & (places < grid.pool_capacity), places, -1)
        halo_slots = sources - grid.slots
        source_dom = lax.shift_right_arithmetic(halo_slots, shift)
        halo_sources = grid.halo_place(source_dom) * grid.coarse_capacity + (halo_slots & (grid.coarse_capacity - 1))
        is_halo = halo_slots >= 0
        source_out[owner : owner + 1, :] = jnp.where(is_halo, halo_sources, -1)
        place_out[owner : owner + 1, :] = places
        own_sources = jnp.where(is_halo, -1, grid.slot_order(sources, place))

        table = owner_table(grid, packets, owner)
        rows = table[: grid.pool_capacity]
        if not grid.swapped:
            for other in range(1, grid.places):
                other_rows = table[other * grid.pool_capacity : (other + 1) * grid.pool_capacity]
                rows = jnp.where(place == other, other_rows, rows)
        rows_out[owner] = rows.T
        sender = dot(table, halved(weights_ref[0])).astype(BF16).T
        target = dot(rows, halved(weights_ref[1])).astype(BF16).T
        hot = jnp.concatenate([rows_hot(own_sources, grid.slots), rows_hot(places, grid.pool_capacity)], axis=0)
        picked_ref[owner] = dot(jnp.concatenate([sender, target], axis=1), hot)


def lift(table, prolonged, index_row):
    pooled_rows = prolonged.shape[1] // 2
    hot = rows_hot(index_row, pooled_rows)
    hot = jnp.concatenate([hot, hot], axis=0)
    return (table.astype(F32) + dot(prolonged, hot)).astype(BF16)


def lift_halo_kernel(
    grid,
    picked_ref,
    source_ref,
    place_ref,
    rows_ref,
    ahead_ref,
    coarse_weights_ref,
    prolong_weight_ref,
    weights_ref,
    *rest,
):
    count = len(grid.steps)
    halo_refs, prolonged_ref, sent_refs = rest[:count], rest[count], rest[count + 1 :]
    features = rows_ref.shape[1]
    update_weights = jnp.concatenate([turned(coarse_weights_ref[2]), turned(coarse_weights_ref[3])], axis=1)
    prolong_weight = turned(prolong_weight_ref[...])
    prolonged = []
    for owner in range(grid.owners):
        halo = jnp.concatenate([ref[owner * BLOCK : (owner + 1) * BLOCK, :] for ref in halo_refs], axis=1)
        picked = picked_ref[owner] + dot(halo, rows_hot(source_ref[owner : owner + 1, :], halo.shape[1]))
        message = silu_of_half(picked).astype(BF16)
        places = rows_hot(place_ref[owner : owner + 1, :], grid.pool_capacity)
        summed = dot_last(message, places).astype(BF16)
        rows = rows_ref[owner]
        update = dot(update_weights, jnp.concatenate([summed, rows], axis=0))
        coarse = (rows.astype(F32) + silu_of_half(update)).astype(BF16)
        prolonged.append(silu_of_half(dot(prolong_weight, coarse)))
    prolonged = jnp.concatenate(prolonged, axis=1)
    high = prolonged.astype(BF16)
    low = (prolonged - high.astype(F32)).astype(BF16)
    parts = jnp.concatenate([high, low], axis=1)
    prolonged_ref[...] = parts
    weight = turned(weights_ref[1, 0])
    index_row = ahead_ref[features : features + 16, :].astype(F32).astype(I32)[:1]
    lifted = lift(ahead_ref[:features, :], parts, index_row)
    terms = dot(weight, lifted).astype(BF16)
    capacity = sent_refs[0].shape[1]
    for index, out_ref in enumerate(sent_refs):
        out_ref[...] = terms[:, index * capacity : (index + 1) * capacity]


def lift_near_kernel(
    grid,
    first_ref,
    prolonged_ref,
    prolong_ref,
    source_ref,
    place_ref,
    weights_ref,
    lifted_ref,
    aimed_ref,
    sums_ref,
    terms_ref,
):
    indices = prolong_ref[...]
    shift = (4 * grid.pool_capacity).bit_length() - 1
    indices = lax.shift_right_logical(indices, shift) * grid.pool_capacity + (indices & (grid.pool_capacity - 1))
    row = jnp.concatenate([indices[block : block + 1, :] for block in range(indices.shape[0])], axis=1)
    lifted = lift(first_ref[...], prolonged_ref[...], row)
    lifted_ref[...] = lifted
    near_edges(lifted, source_ref, place_ref, weights_ref, 1, aimed_ref, sums_ref, terms_ref)


def call(kernel, outs, scratch=(), flops=0, name=None, limit=VMEM_BYTES, **specs):
    return pl.pallas_call(
        kernel,
        out_shape=tuple(jax.ShapeDtypeStruct(shape, dtype) for shape, dtype in outs),
        scratch_shapes=list(scratch),
        compiler_params=pltpu.CompilerParams(vmem_limit_bytes=limit),
        cost_estimate=pl.CostEstimate(flops=flops, bytes_accessed=4 << 20, transcendentals=0),
        name=name,
        **specs,
    )


def swap_dom(grid, arrays):
    return [
        lax.ppermute(array, "dom", [(dom, grid.partner(dom, step)) for dom in range(grid.dom_count)])
        for array, step in zip(arrays, grid.steps)
    ]


def trade_packets(grid, packets):
    if grid.swapped:
        pairs = [(0, 1), (1, 0)]
        near, far = packets
        over = lax.ppermute(far, "sub", pairs)
        across = lax.ppermute(near, "chip", pairs)
        both = lax.ppermute(far, ("sub", "chip"), [(0, 3), (1, 2), (2, 1), (3, 0)])
        return [near, across, over, both]
    gathered = lax.all_gather(packets[0], ("sub", "chip"), axis=0, tiled=False)
    return [gathered[place] for place in range(grid.places)]


def body(
    mesh,
    fine_nodes,
    fine_src,
    fine_dst,
    halo_send,
    pool_send,
    coarse_src,
    coarse_dst,
    coarse_send,
    prolong_idx,
    fine_weights,
    coarse_weights,
    prolong_weight,
):
    node_count, features = fine_nodes.shape
    halo_capacity = halo_send.shape[2]
    coarse_blocks, coarse_slots = coarse_src.shape
    grid = Grid(mesh, halo_capacity, pool_send.shape[2], coarse_send.shape[2], coarse_blocks, coarse_slots)
    steps = len(grid.steps)
    block_count, slot_count = fine_src.shape
    far_count = slot_count - slot_count * 3 // 4
    table = ((features, node_count), BF16)
    sums_table = ((features, node_count), F32)
    aimed_table = ((features, block_count * far_count), BF16)
    far_lists = ((block_count // BATCH, BATCH * far_count), I32)
    halo_outs = [((features, halo_capacity), BF16)] * steps
    two_tables = pltpu.VMEM((2 * features, node_count), BF16)
    prolong_rows = prolong_idx.reshape(node_count // BLOCK, BLOCK)
    big = 1 << 30
    in_hbm = pl.BlockSpec(memory_space=pltpu.HBM)

    (nodes,) = call(
        turn_kernel,
        [table],
        [pltpu.VMEM((node_count, features), BF16), pltpu.SemaphoreType.DMA((PARTS,))],
        name="turn",
        limit=5300 * 10486,
        in_specs=[in_hbm],
    )(fine_nodes)
    sent = call(functools.partial(send_kernel, grid), halo_outs, flops=big, name="send")(
        nodes, halo_send, fine_weights
    )
    halo = swap_dom(grid, sent)
    far_sources, far_places, aimed, sums, pool_lists, *packed = call(
        functools.partial(near_kernel, grid),
        [
            far_lists,
            far_lists,
            aimed_table,
            sums_table,
            ((grid.owners, grid.pool_capacity), I32),
            *[((grid.packed_rows, features), BF16)] * grid.packets,
        ],
        [two_tables],
        flops=4 * big,
        name="near",
    )(nodes, fine_src, fine_dst, fine_weights, coarse_src, coarse_dst, coarse_send, pool_send)
    first, *packets = call(
        functools.partial(far_pool_kernel, grid),
        [table, *[((grid.packet, features), BF16)] * grid.packets],
        [two_tables],
        flops=2 * big,
        name="far_pool",
    )(nodes, aimed, far_sources, far_places, sums, fine_weights, pool_lists, *packed, *handed(halo, FIRST_ORDER))
    packets = trade_packets(grid, packets)
    (ahead,) = call(
        functools.partial(ahead_kernel, grid), [((features + 16, steps * halo_capacity), BF16)], flops=big, name="ahead"
    )(first, prolong_rows, halo_send)
    lists_scratch = pltpu.VMEM((grid.packed_rows, BLOCK), I32)
    sent = call(
        functools.partial(coarse_send_kernel, grid),
        [((grid.owners * features, grid.coarse_capacity), BF16)] * steps,
        [lists_scratch],
        flops=big // 2,
        name="coarse_send",
    )(coarse_weights, *packets)
    coarse_halo = swap_dom(grid, sent)
    picked, sources, places, rows = call(
        functools.partial(coarse_own_kernel, grid),
        [
            ((grid.owners, features, coarse_slots), F32),
            ((grid.owners, coarse_slots), I32),
            ((grid.owners, coarse_slots), I32),
            ((grid.owners, features, grid.pool_capacity), BF16),
        ],
        [lists_scratch],
        flops=4 * big,
        name="coarse_own",
    )(coarse_weights, *packets)
    prolonged, *sent = call(
        functools.partial(lift_halo_kernel, grid),
        [((features, 2 * grid.pooled_rows), BF16), *halo_outs],
        flops=big,
        name="lift_halo",
    )(picked, sources, places, rows, ahead, coarse_weights, prolong_weight, fine_weights, *coarse_halo)
    halo = swap_dom(grid, sent)
    lifted, aimed, sums = call(
        functools.partial(lift_near_kernel, grid),
        [table, aimed_table, sums_table],
        [two_tables],
        flops=4 * big,
        name="lift_near",
    )(first, prolonged, prolong_rows, fine_src, fine_dst, fine_weights)
    (fine_out,) = call(
        far_kernel,
        [((node_count, features), BF16)],
        [
            two_tables,
            pltpu.VMEM((node_count, features), BF16),
            pltpu.SemaphoreType.DMA((block_count // BATCH,)),
        ],
        flops=2 * big,
        name="far",
        out_specs=(pl.BlockSpec(memory_space=pltpu.HBM),),
    )(lifted, aimed, far_sources, far_places, sums, fine_weights, *handed(halo, SECOND_ORDER))
    return fine_out


def solution(mesh):
    split = ("groups", "dom", "sub", "chip")
    return jax.shard_map(
        functools.partial(body, mesh),
        mesh=mesh,
        in_specs=(
            P(split, None),
            P(split, None),
            P(split, None),
            P(split, None, None),
            P(split, None, None),
            P(split, None),
            P(split, None),
            P(split, None, None),
            P(split),
            P(),
            P(),
            P(),
        ),
        out_specs=P(split, None),
        check_vma=False,
    )
```
